32 devices in a mesh: gx: 8 (over y, x, core), gy: 4 (over z).
Axes of the slice: x: 2, y: 2, z: 4, core: 2. Of those that a mesh axis runs over, the one named last changes fastest.
Arguments:
- initial: float32 [128, 256, 128], P('gx', 'gy'), may hold values from -6 to 6, as said below
- material: int32 [128, 256, 128], P('gx', 'gy'), may hold values from 0 to 7
- goal_faces: int32 [128, 256, 128], P('gx', 'gy'), may hold values 0 or 1
- conductivity: float32 [8], replicated, may hold values from 0.2 to 2
Outputs:
- indicators: float32 [128, 256, 128], P('gx', 'gy')
- sensitivity: float32 [128, 256, 128], P('gx', 'gy')
The draws below stay inside these ranges and needn't reach their ends.
Inputs may be any that keep to these rules, and one draw needn't show every extreme that they name: `initial`: temperatures.
All inputs are finite; a program needn't handle non-finite values. No bound on the sum of `goal_faces` on one device may be relied on, other than what follows from the above.
Results may differ from the reference program's by a relative error of at most 0.00002.
Values sent between devices are 32-bit elements; how exact they have to be, the bound alone decides.
No kernel may reach another device: no remote copies, remote signals or barrier semaphores. Data moves between devices by JAX's collectives and lax.ppermute only.
A program may use at most 64 MiB of HBM per device.

```python
import math
import jax
import jax.numpy as jnp

NZ = 128
STEPS = 3
MATS = 8
NX = 128
NY = 256


def draw_initial(key, part):
    return jnp.clip(jax.random.normal(key, (NX, NY, NZ), jnp.float32), -6.0, 6.0)


def touch_ends(array, own_key, low, high):
    extent = array.shape
    index_at = [jax.random.randint(jax.random.fold_in(own_key, axis), (), 0, extent[axis]) for axis in range(len(extent))]
    array = array.at[tuple(index_at)].set(low)
    longest = extent.index(max(extent))
    index_at[longest] = (index_at[longest] + 1) % extent[longest]
    return array.at[tuple(index_at)].set(high)


def setup_inputs(seed: int = 0) -> dict:
    streams_of = jax.random.split(jax.random.key(seed), 5)
    initial = draw_initial(jax.random.fold_in(streams_of[4], 71), 0)
    material = touch_ends(jax.random.randint(streams_of[1], (NX, NY, NZ), 0, MATS), jax.random.fold_in(streams_of[1], 1), 0, MATS - 1).astype(jnp.int32)
    goal_faces = touch_ends((jax.random.randint(streams_of[2], (NX, NY, NZ), 0, 4) < 1).astype(jnp.int32), jax.random.fold_in(streams_of[2], 1), 0, 1)
    conductivity = jnp.clip(jnp.exp(jax.random.uniform(streams_of[3], (MATS,), jnp.float32, math.log(0.2), math.log(2.0))), 0.2, 2.0)
    return {"initial": initial, "material": material, "goal_faces": goal_faces, "conductivity": conductivity}


step_size = 0.075


def lookup(material, conductivity):
    result = jnp.zeros(material.shape, jnp.float32)
    for which in range(MATS):
        result = jnp.where(material == which, conductivity[which], result)
    return result


def neighbours(padded):
    return [padded[2:, 1:-1, 1:-1], padded[:-2, 1:-1, 1:-1], padded[1:-1, 2:, 1:-1],
            padded[1:-1, :-2, 1:-1], padded[1:-1, 1:-1, 2:], padded[1:-1, 1:-1, :-2]]


def face_values(padded):
    centre = padded[1:-1, 1:-1, 1:-1]
    return [0.5 * (centre + other) for other in neighbours(padded)]


def divergence(field, padded, weights):
    total = jnp.zeros_like(field)
    for weight, other in zip(weights, neighbours(padded)):
        total = total + weight * (other - field)
    return total


def patch_mean(padded):
    rows = padded[:-2] + padded[1:-1] + padded[2:]
    rows = rows[:, :-2] + rows[:, 1:-1] + rows[:, 2:]
    rows = rows[:, :, :-2] + rows[:, :, 1:-1] + rows[:, :, 2:]
    return rows / 27.0


def reference(initial, material, goal_faces, conductivity):
    conduct = lookup(material, conductivity)
    weights = face_values(jnp.pad(conduct, 1))
    states = [initial]
    slopes = []
    for section in range(STEPS):
        slopes.append(divergence(states[-1], jnp.pad(states[-1], 1), weights))
        states.append(states[-1] + step_size * slopes[-1])
    slopes.append(divergence(states[-1], jnp.pad(states[-1], 1), weights))
    residuals = [(states[section + 1] - states[section]) / step_size - slopes[section + 1] for section in range(STEPS)]
    flux = goal_faces.astype(jnp.float32) * weights[0]
    adjoint = flux - jnp.pad(flux, ((1, 0), (0, 0), (0, 0)))[:-1]
    indicators = jnp.zeros_like(initial)
    for section in range(STEPS - 1, -1, -1):
        padded = jnp.pad(adjoint, 1)
        indicators = indicators + residuals[section] * (patch_mean(padded) - adjoint)
        adjoint = adjoint + step_size * divergence(adjoint, padded, weights)
    return indicators, adjoint
```

```python
import functools

import jax
import jax.numpy as jnp
from jax import lax
from jax.experimental import pallas as pl
from jax.experimental.pallas import tpu as pltpu
from jax.sharding import PartitionSpec as P

step_size = 0.075
HALO = 4
LIMIT = 48 * 1024 * 1024


def lanes_of(shape):
    return lax.broadcasted_iota(jnp.int32, shape, len(shape) - 1)


def gather_rows(table, index):
    return jnp.take_along_axis(jnp.broadcast_to(table, index.shape), index, axis=1, mode="promise_in_bounds")


def pack_kernel(initial, material, goal, cond, kh, up, down):
    cells_x, cells_y, cells_z = initial.shape
    lane = lanes_of((8, cells_z))
    table = jnp.zeros((8, cells_z), jnp.float32)
    for which in range(cond.shape[0]):
        table = jnp.where(lane == which, cond[which] * (0.5 * step_size), table)
    low_half = lax.broadcasted_iota(jnp.int32, (8, cells_z), 0) < HALO

    def plane(i, _):
        for first in range(0, cells_y, 8):
            index = material[i, first : first + 8, :]
            kh[i, first : first + 8, :] = gather_rows(table, index)
        top = cells_y - 8
        up[i] = jnp.where(low_half, pltpu.roll(kh[i, top:, :], HALO, 0), initial[i, top:, :])
        down[i] = jnp.where(low_half, initial[i, :8, :], pltpu.roll(kh[i, :8, :], HALO, 0))
        return 0

    lax.fori_loop(0, cells_x, plane, 0)
    for pair in range(cells_x // 2):
        one, two = 2 * pair, 2 * pair + 1
        top = cells_y - 8
        g_one = goal[one, top:, :].astype(jnp.float32)
        g_two = goal[two, top:, :].astype(jnp.float32)
        up[cells_x + pair] = jnp.where(low_half, pltpu.roll(g_two, HALO, 0), g_one)
        g_one = goal[one, :8, :].astype(jnp.float32)
        g_two = goal[two, :8, :].astype(jnp.float32)
        down[cells_x + pair] = jnp.where(low_half, g_one, pltpu.roll(g_two, HALO, 0))


def halo_tiles(plane, cells_x, from_low, from_high, low_half):
    below, above = from_low[plane], from_high[plane]
    u = jnp.where(low_half, above, below)
    k = pltpu.roll(jnp.where(low_half, below, above), HALO, 0)
    return u, k


def goal_tiles(pair, cells_x, from_low, from_high, low_half):
    below, above = from_low[cells_x + pair], from_high[cells_x + pair]
    one = jnp.where(low_half, above, below)
    two = pltpu.roll(jnp.where(low_half, below, above), HALO, 0)
    return one, two


def face_kernel(cells_x, u_lo, u_hi, k_lo, k_hi, g_lo, g_hi, from_low, from_high, lo, hi):
    cells_y, cells_z = u_lo.shape[1:]
    low_half = lax.broadcasted_iota(jnp.int32, (8, cells_z), 0) < HALO
    for u, k, g, out, start in ((u_lo, k_lo, g_lo, lo, 0), (u_hi, k_hi, g_hi, hi, cells_x - HALO)):
        for i in range(HALO):
            out[i, :cells_y, :] = u[i]
            out[HALO + i, :cells_y, :] = k[i]
            out[2 * HALO + i, :cells_y, :] = g[i].astype(jnp.float32)
            hu, hk = halo_tiles(start + i, cells_x, from_low, from_high, low_half)
            out[i, cells_y:, :] = hu
            out[HALO + i, cells_y:, :] = hk
        for i in range(0, HALO, 2):
            one, two = goal_tiles((start + i) // 2, cells_x, from_low, from_high, low_half)
            out[2 * HALO + i, cells_y:, :] = one
            out[2 * HALO + i + 1, cells_y:, :] = two


def main_kernel(initial, kh, goal, from_low, from_high, xlo, xhi, ind, sens,
                U, K, G, Wx, Wy, Wz, S, EA, EB, ZA, ZB, M0, Q3):
    cells_x, cells_y, cells_z = initial.shape
    H = HALO
    rows = cells_y + 8
    base = 8
    end = base + rows
    top = H + cells_x
    planes = cells_x + 2 * H
    low_half = lax.broadcasted_iota(jnp.int32, (8, cells_z), 0) < H

    U[0:H, base:end, :] = xlo[0:H]
    K[0:H, base:end, :] = xlo[H : 2 * H]
    G[0:H] = xlo[2 * H : 3 * H]
    U[top:planes, base:end, :] = xhi[0:H]
    K[top:planes, base:end, :] = xhi[H : 2 * H]
    G[top:planes] = xhi[2 * H : 3 * H]

    def own(p, _):
        for i in (2 * p, 2 * p + 1):
            U[H + i, base : base + cells_y, :] = initial[i]
            K[H + i, base : base + cells_y, :] = kh[i]
            G[H + i, 0:cells_y, :] = goal[i].astype(jnp.float32)
            hu, hk = halo_tiles(i, cells_x, from_low, from_high, low_half)
            U[H + i, base + cells_y : end, :] = hu
            K[H + i, base + cells_y : end, :] = hk
        one, two = goal_tiles(p, cells_x, from_low, from_high, low_half)
        G[H + 2 * p, cells_y:, :] = one
        G[H + 2 * p + 1, cells_y:, :] = two
        return 0

    lax.fori_loop(0, cells_x // 2, own, 0)
    for field in (U, K):
        field[:, 0:base, :] = field[:, end - 8 : end, :]
        field[:, end : end + 8, :] = field[:, base : base + 8, :]

    def put(ref, i, first, size, value):
        ref[i, pl.ds(first, size), :] = value
        if first == base:
            ref[i, end : end + 8, :] = value[0:8]
        if first + size == end:
            ref[i, 0:8, :] = value[size - 8 : size]

    def get(ref, i, first, size):
        return ref[i, pl.ds(first, size), :]

    own_chunks = []
    first = base
    while first < base + cells_y:
        size = min(24, base + cells_y - first)
        own_chunks.append((first, size))
        first += size
    all_chunks = own_chunks + [(base + cells_y, 8)]
    right = cells_z - 1

    def up_lane(value):
        return pltpu.roll(value, right, 1)

    def down_lane(value):
        return pltpu.roll(value, 1, 1)

    Wx[0] = K[0, base:end, :] + K[1, base:end, :]

    def prelude(i, _):
        for first, size in all_chunks:
            lane = lanes_of((size, cells_z))
            k = get(K, i, first, size)
            wx = k + get(K, i + 1, first, size)
            wxm = Wx[i - 1, pl.ds(first - base, size), :]
            wy = k + get(K, i, first + 1, size)
            wym = k + get(K, i, first - 1, size)
            wzt = k + jnp.where(lane == right, 0.0, up_lane(k))
            wzm = k + jnp.where(lane == 0, 0.0, down_lane(k))
            wz = jnp.where(lane == right, 0.0, wzt)
            s = ((wx + wxm) + (wy + wym)) + (wzt + wzm)
            u = get(U, i, first, size)
            e = (wx * get(U, i + 1, first, size) + wxm * get(U, i - 1, first, size)) + (
                wy * get(U, i, first + 1, size) + wym * get(U, i, first - 1, size)
            ) + (wz * up_lane(u) + down_lane(wz * u)) - s * u
            here = pl.ds(first - base, size)
            z = G[i, here, :] * wx - G[i - 1, here, :] * wxm
            Wx[i, here, :] = wx
            Wy[i, pl.ds(first, size), :] = wy
            if first + size == end:
                Wy[i, 0:8, :] = wy[size - 8 : size]
            Wz[i, here, :] = wz
            S[i, here, :] = s
            put(EA, i, first, size, e)
            put(ZA, i, first, size, z)
        return 0

    lax.fori_loop(1, planes - 1, prelude, 0)

    gx, gy = lax.axis_index("gx"), lax.axis_index("gy")
    empty = jnp.zeros((rows + 16, cells_z), jnp.float32)
    row = jnp.zeros((planes, 1, cells_z), jnp.float32)

    @pl.when(gx == 0)
    def _():
        EA[H - 1] = empty
        Wx[H - 1] = empty[0:rows]

    @pl.when(gx == lax.axis_size("gx") - 1)
    def _():
        EA[top] = empty
        ZA[top] = empty
        Wx[top - 1] = empty[0:rows]

    @pl.when(gy == 0)
    def _():
        EA[:, 7:8, :] = row
        EA[:, end - 1 : end, :] = row
        Wy[:, 7:8, :] = row
        Wy[:, end - 1 : end, :] = row

    @pl.when(gy == lax.axis_size("gy") - 1)
    def _():
        EA[:, base + cells_y : base + cells_y + 1, :] = row
        Wy[:, base + cells_y - 1 : base + cells_y, :] = row

    def sweep(E, Z, start, count, chunks, finish, box):
        for first, size in chunks:
            here = pl.ds(first - base, size)
            lane = lanes_of((size, cells_z))
            ec = [get(E, start + j, first, size) for j in range(-1, count + 1)]
            zc = [get(Z, start + j, first, size) for j in range(-1, count + 1)]
            wxs = [Wx[start + j, here, :] for j in range(-1, count)]
            want_box = box and first < base + cells_y
            sums = {}

            def y_pair(j):
                return get(Z, start + j, first + 1, size), get(Z, start + j, first - 1, size)

            if want_box:
                for j in (-1, count):
                    a, b = y_pair(j)
                    sums[j] = zc[j + 1] + (a + b)
            parts = []
            for j in range(count):
                i = start + j
                wx, wxm = wxs[j + 1], wxs[j]
                wy, wym = get(Wy, i, first, size), get(Wy, i, first - 1, size)
                wz, s = Wz[i, here, :], S[i, here, :]
                zyp, zym = y_pair(j)
                if want_box:
                    sums[j] = zc[j + 1] + (zyp + zym)

                def apply(c, xp, xm, yp, ym):
                    return (wx * xp + wxm * xm) + (wy * yp + wym * ym) + (
                        wz * up_lane(c) + down_lane(wz * c)) - s * c

                em = apply(ec[j + 1], ec[j + 2], ec[j], get(E, i, first + 1, size), get(E, i, first - 1, size))
                zm = apply(zc[j + 1], zc[j + 2], zc[j], zyp, zym)
                parts.append((em, zm))
            for j in range(count):
                em, zm = parts[j]
                q = None
                if want_box:
                    xs = sums[j - 1] + sums[j] + sums[j + 1]
                    xs = xs + (jnp.where(lane == right, 0.0, up_lane(xs)) + jnp.where(lane == 0, 0.0, down_lane(xs)))
                    q = xs * (1.0 / 27.0) - zc[j + 1]
                finish(start + j, first, size, ec[j + 1], em, zc[j + 1], zm, q)

    def store_a(i, first, size, e, em, z, zm, q):
        put(EB, i, first, size, e + em)
        put(ZB, i, first, size, z + zm)
        if q is not None:
            here = pl.ds(first - base, size)
            M0[i - H, here, :] = em
            Q3[i - H, here, :] = q

    def store_b(i, first, size, e, em, z, zm, q):
        put(EA, i, first, size, e + em)
        put(ZA, i, first, size, z + zm)
        if q is not None:
            ind[i - H, pl.ds(first - base, size), :] = em * q

    def store_c(i, first, size, e, em, z, zm, q):
        here = pl.ds(first - base, size)
        total = ind[i - H, here, :] + em * Q3[i - H, here, :] + M0[i - H, here, :] * q
        ind[i - H, here, :] = total * (-1.0 / (step_size * step_size))
        sens[i - H, here, :] = (z + zm) * (1.0 / step_size)

    def middle(E, Z, chunks, finish):
        def body(p, _):
            sweep(E, Z, H + 2 * p, 2, chunks, finish, True)
            return 0

        lax.fori_loop(0, cells_x // 2, body, 0)

    sweep(EA, ZA, H - 2, 2, all_chunks, store_a, False)
    middle(EA, ZA, all_chunks, store_a)
    sweep(EA, ZA, top, 2, all_chunks, store_a, False)
    sweep(EB, ZB, H - 1, 1, all_chunks, store_b, False)
    middle(EB, ZB, all_chunks, store_b)
    sweep(EB, ZB, top, 1, all_chunks, store_b, False)
    middle(EA, ZA, own_chunks, store_c)


def whole(memory=None):
    return pl.BlockSpec(memory_space=memory or pltpu.VMEM)


def exchange(up, down, axis):
    count = lax.axis_size(axis)
    forward = [(i, i + 1) for i in range(count - 1)]
    backward = [(b, a) for a, b in forward]
    return lax.ppermute(up, axis, forward), lax.ppermute(down, axis, backward)


def per_device(initial, material, goal_faces, conductivity):
    cells_x, cells_y, cells_z = initial.shape
    f32 = jnp.float32
    params = pltpu.CompilerParams(vmem_limit_bytes=LIMIT)
    shape = jax.ShapeDtypeStruct
    send = shape((cells_x + cells_x // 2, 8, cells_z), f32)
    kh, up, down = pl.pallas_call(
        pack_kernel,
        out_shape=(shape(initial.shape, f32), send, send),
        in_specs=[whole(), whole(), whole(), whole(pltpu.SMEM)],
        out_specs=(whole(), whole(), whole()),
        compiler_params=params,
        name="pack",
    )(initial, material, goal_faces, conductivity)
    from_low, from_high = exchange(up, down, "gy")
    last = cells_x // HALO - 1
    lo_block = pl.BlockSpec((HALO, cells_y, cells_z), lambda i: (0, 0, 0))
    hi_block = pl.BlockSpec((HALO, cells_y, cells_z), lambda i: (last, 0, 0))
    y_block = pl.BlockSpec(send.shape, lambda i: (0, 0, 0))
    rows = cells_y + 8
    face = shape((3 * HALO, rows, cells_z), f32)
    face_block = pl.BlockSpec(face.shape, lambda i: (0, 0, 0))
    lo, hi = pl.pallas_call(
        functools.partial(face_kernel, cells_x),
        grid=(1,),
        out_shape=(face, face),
        in_specs=[lo_block, hi_block] * 3 + [y_block, y_block],
        out_specs=(face_block, face_block),
        compiler_params=params,
        name="faces",
    )(initial, initial, kh, kh, goal_faces, goal_faces, from_low, from_high)
    xlo, xhi = exchange(hi, lo, "gx")
    planes = cells_x + 2 * HALO
    wide = pltpu.VMEM((planes, rows + 16, cells_z), f32)
    narrow = pltpu.VMEM((planes, rows, cells_z), f32)
    inner = pltpu.VMEM(initial.shape, f32)
    return pl.pallas_call(
        main_kernel,
        out_shape=(shape(initial.shape, f32), shape(initial.shape, f32)),
        in_specs=[whole()] * 7,
        out_specs=(whole(), whole()),
        scratch_shapes=[wide, wide, narrow, narrow, wide, narrow, narrow, wide, wide, wide, wide, inner, inner],
        compiler_params=params,
        name="chain",
    )(initial, kh, goal_faces, from_low, from_high, xlo, xhi)


def solution(mesh):
    placed = (P("gx", "gy", None), P("gx", "gy", None), P("gx", "gy", None), P())
    return jax.shard_map(
        per_device,
        mesh=mesh,
        in_specs=placed,
        out_specs=(P("gx", "gy", None), P("gx", "gy", None)),
        check_vma=False,
    )
```

```python
import functools

import jax
import jax.numpy as jnp
from jax import lax
from jax.experimental import pallas as pl
from jax.experimental.pallas import tpu as pltpu
from jax.sharding import PartitionSpec as P

step_size = 0.075
HALO = 4
LIMIT = 48 * 1024 * 1024


def lanes_of(shape):
    return lax.broadcasted_iota(jnp.int32, shape, len(shape) - 1)


def gather_rows(table, index):
    return jnp.take_along_axis(jnp.broadcast_to(table, index.shape), index, axis=1, mode="promise_in_bounds")


def pack_kernel(initial, material, goal, cond, u, kh, g, up, down, near, far, ids, flags, sems):
    cells_x, cells_y, cells_z = initial.shape
    moves = [
        pltpu.make_async_copy(source, target, sems.at[i])
        for i, (source, target) in enumerate(((material, ids), (initial, u), (goal, flags)))
    ]
    for move in moves:
        move.start()
    lane = lanes_of((8, cells_z))
    table = jnp.zeros((8, cells_z), jnp.float32)
    for which in range(cond.shape[0]):
        table = jnp.where(lane == which, cond[which] * (0.5 * step_size), table)
    low_half = lax.broadcasted_iota(jnp.int32, (8, cells_z), 0) < HALO
    for move in moves:
        move.wait()

    def plane(p, _):
        for i in (2 * p, 2 * p + 1):
            kh[i] = gather_rows(table[0:1], ids[i])
            g[i] = flags[i].astype(jnp.float32)
        return 0

    lax.fori_loop(0, cells_x // 2, plane, 0)
    top = cells_y - 8
    for i in range(cells_x):
        up[i] = jnp.where(low_half, pltpu.roll(kh[i, top:, :], HALO, 0), u[i, top:, :])
        down[i] = jnp.where(low_half, u[i, :8, :], pltpu.roll(kh[i, :8, :], HALO, 0))
    for pair in range(cells_x // 2):
        one, two = 2 * pair, 2 * pair + 1
        up[cells_x + pair] = jnp.where(low_half, pltpu.roll(g[two, top:, :], HALO, 0), g[one, top:, :])
        down[cells_x + pair] = jnp.where(low_half, g[one, :8, :], pltpu.roll(g[two, :8, :], HALO, 0))
    odd = lax.axis_index("gx") % 2
    last = cells_x - HALO
    for send, start in ((near, (1 - odd) * last), (far, odd * last)):
        for field, ref in enumerate((u, kh, g)):
            for i in range(HALO):
                send[field * HALO + i] = ref[start + i]


def halo_tiles(plane, cells_x, from_low, from_high, low_half):
    below, above = from_low[plane], from_high[plane]
    u = jnp.where(low_half, above, below)
    k = pltpu.roll(jnp.where(low_half, below, above), HALO, 0)
    return u, k


def goal_tiles(pair, cells_x, from_low, from_high, low_half):
    below, above = from_low[cells_x + pair], from_high[cells_x + pair]
    one = jnp.where(low_half, above, below)
    two = pltpu.roll(jnp.where(low_half, below, above), HALO, 0)
    return one, two


def corner_kernel(cells_x, from_low, from_high, near, far):
    cells_z = from_low.shape[-1]
    low_half = lax.broadcasted_iota(jnp.int32, (8, cells_z), 0) < HALO
    odd = lax.axis_index("gx") % 2
    last = cells_x - HALO
    for send, start in ((near, (1 - odd) * last), (far, odd * last)):
        for i in range(HALO):
            send[i], send[HALO + i] = halo_tiles(start + i, cells_x, from_low, from_high, low_half)
        for i in range(0, HALO, 2):
            one, two = goal_tiles(start // 2 + i // 2, cells_x, from_low, from_high, low_half)
            send[2 * HALO + i], send[2 * HALO + i + 1] = one, two


def main_kernel(initial, kh, goal, from_low, from_high, near, far, near_corner, far_corner, ind, sens,
                sems, U, K, G, Wx, Wy, Wz, S, EA, EB, ZA, ZB, M0, Q3):
    cells_x, cells_y, cells_z = initial.shape
    H = HALO
    rows = cells_y + 8
    base = 8
    end = base + rows
    top = H + cells_x
    planes = cells_x + 2 * H
    low_half = lax.broadcasted_iota(jnp.int32, (8, cells_z), 0) < H

    gx, gy = lax.axis_index("gx"), lax.axis_index("gy")
    odd = gx % 2
    near_at, far_at = (1 - odd) * top, odd * top
    own_rows = pl.ds(base, cells_y)
    moves = []
    for source, half, at in ((near, 1 - odd, near_at), (far, odd, far_at)):
        for field, ref in enumerate((U, K, G)):
            rows_at = own_rows if field < 2 else pl.ds(0, cells_y)
            moves.append(pltpu.make_async_copy(
                source.at[pl.ds((half * 3 + field) * H, H)],
                ref.at[pl.ds(at, H), rows_at, :],
                sems.at[len(moves)],
            ))
    for move in moves:
        move.start()
    for source, at in ((near_corner, near_at), (far_corner, far_at)):
        for i in range(H):
            U[at + i, base + cells_y : end, :] = source[i]
            K[at + i, base + cells_y : end, :] = source[H + i]
            G[at + i, cells_y:, :] = source[2 * H + i]

    def own(p, _):
        for i in (2 * p, 2 * p + 1):
            U[H + i, base : base + cells_y, :] = initial[i]
            K[H + i, base : base + cells_y, :] = kh[i]
            G[H + i, 0:cells_y, :] = goal[i]
            hu, hk = halo_tiles(i, cells_x, from_low, from_high, low_half)
            U[H + i, base + cells_y : end, :] = hu
            K[H + i, base + cells_y : end, :] = hk
        one, two = goal_tiles(p, cells_x, from_low, from_high, low_half)
        G[H + 2 * p, cells_y:, :] = one
        G[H + 2 * p + 1, cells_y:, :] = two
        return 0

    lax.fori_loop(0, cells_x // 2, own, 0)
    for move in moves:
        move.wait()

    @pl.when((gx == 0) | (gx == lax.axis_size("gx") - 1))
    def _():
        nothing = jnp.zeros((cells_y, cells_z), jnp.float32)
        for i in range(H):
            U[far_at + i, base : base + cells_y, :] = nothing
            K[far_at + i, base : base + cells_y, :] = nothing
            G[far_at + i, 0:cells_y, :] = nothing

    for field in (U, K):
        field[:, 0:base, :] = field[:, end - 8 : end, :]
        field[:, end : end + 8, :] = field[:, base : base + 8, :]

    def put(ref, i, first, size, value):
        ref[i, pl.ds(first, size), :] = value
        if first == base:
            ref[i, end : end + 8, :] = value[0:8]
        if first + size == end:
            ref[i, 0:8, :] = value[size - 8 : size]

    def get(ref, i, first, size):
        return ref[i, pl.ds(first, size), :]

    own_chunks = []
    first = base
    while first < base + cells_y:
        size = min(24, base + cells_y - first)
        own_chunks.append((first, size))
        first += size
    all_chunks = own_chunks + [(base + cells_y, 8)]
    right = cells_z - 1

    def up_lane(value):
        return pltpu.roll(value, right, 1)

    def down_lane(value):
        return pltpu.roll(value, 1, 1)

    Wx[0] = K[0, base:end, :] + K[1, base:end, :]

    def prelude(i, _):
        for first, size in all_chunks:
            lane = lanes_of((size, cells_z))
            k = get(K, i, first, size)
            wx = k + get(K, i + 1, first, size)
            wxm = Wx[i - 1, pl.ds(first - base, size), :]
            wy = k + get(K, i, first + 1, size)
            wym = k + get(K, i, first - 1, size)
            wzt = k + jnp.where(lane == right, 0.0, up_lane(k))
            wzm = k + jnp.where(lane == 0, 0.0, down_lane(k))
            wz = jnp.where(lane == right, 0.0, wzt)
            s = ((wx + wxm) + (wy + wym)) + (wzt + wzm)
            u = get(U, i, first, size)
            e = (wx * get(U, i + 1, first, size) + wxm * get(U, i - 1, first, size)) + (
                wy * get(U, i, first + 1, size) + wym * get(U, i, first - 1, size)
            ) + (wz * up_lane(u) + down_lane(wz * u)) - s * u
            here = pl.ds(first - base, size)
            z = G[i, here, :] * wx - G[i - 1, here, :] * wxm
            Wx[i, here, :] = wx
            Wy[i, pl.ds(first, size), :] = wy
            if first + size == end:
                Wy[i, 0:8, :] = wy[size - 8 : size]
            Wz[i, here, :] = wz
            S[i, here, :] = s
            put(EA, i, first, size, e)
            put(ZA, i, first, size, z)
        return 0

    lax.fori_loop(1, planes - 1, prelude, 0)

    empty = jnp.zeros((rows + 16, cells_z), jnp.float32)
    row = jnp.zeros((planes, 1, cells_z), jnp.float32)

    @pl.when(gx == 0)
    def _():
        EA[H - 1] = empty
        Wx[H - 1] = empty[0:rows]

    @pl.when(gx == lax.axis_size("gx") - 1)
    def _():
        EA[top] = empty
        ZA[top] = empty
        Wx[top - 1] = empty[0:rows]

    @pl.when(gy == 0)
    def _():
        EA[:, 7:8, :] = row
        EA[:, end - 1 : end, :] = row
        Wy[:, 7:8, :] = row
        Wy[:, end - 1 : end, :] = row

    @pl.when(gy == lax.axis_size("gy") - 1)
    def _():
        EA[:, base + cells_y : base + cells_y + 1, :] = row
        Wy[:, base + cells_y - 1 : base + cells_y, :] = row

    def sweep(E, Z, start, count, chunks, finish, box):
        for first, size in chunks:
            here = pl.ds(first - base, size)
            lane = lanes_of((size, cells_z))
            ec = [get(E, start + j, first, size) for j in range(-1, count + 1)]
            zc = [get(Z, start + j, first, size) for j in range(-1, count + 1)]
            wxs = [Wx[start + j, here, :] for j in range(-1, count)]
            want_box = box and first < base + cells_y
            sums = {}

            def y_pair(j):
                return get(Z, start + j, first + 1, size), get(Z, start + j, first - 1, size)

            if want_box:
                for j in (-1, count):
                    a, b = y_pair(j)
                    sums[j] = zc[j + 1] + (a + b)
            parts = []
            for j in range(count):
                i = start + j
                wx, wxm = wxs[j + 1], wxs[j]
                wy, wym = get(Wy, i, first, size), get(Wy, i, first - 1, size)
                wz, s = Wz[i, here, :], S[i, here, :]
                zyp, zym = y_pair(j)
                if want_box:
                    sums[j] = zc[j + 1] + (zyp + zym)

                def apply(c, xp, xm, yp, ym):
                    return (wx * xp + wxm * xm) + (wy * yp + wym * ym) + (
                        wz * up_lane(c) + down_lane(wz * c)) - s * c

                em = apply(ec[j + 1], ec[j + 2], ec[j], get(E, i, first + 1, size), get(E, i, first - 1, size))
                zm = apply(zc[j + 1], zc[j + 2], zc[j], zyp, zym)
                parts.append((em, zm))
            for j in range(count):
                em, zm = parts[j]
                q = None
                if want_box:
                    xs = sums[j - 1] + sums[j] + sums[j + 1]
                    xs = xs + (jnp.where(lane == right, 0.0, up_lane(xs)) + jnp.where(lane == 0, 0.0, down_lane(xs)))
                    q = xs * (1.0 / 27.0) - zc[j + 1]
                finish(start + j, first, size, ec[j + 1], em, zc[j + 1], zm, q)

    def store_a(i, first, size, e, em, z, zm, q):
        put(EB, i, first, size, e + em)
        put(ZB, i, first, size, z + zm)
        if q is not None:
            here = pl.ds(first - base, size)
            M0[i - H, here, :] = em
            Q3[i - H, here, :] = q

    def store_b(i, first, size, e, em, z, zm, q):
        put(EA, i, first, size, e + em)
        put(ZA, i, first, size, z + zm)
        if q is not None:
            ind[i - H, pl.ds(first - base, size), :] = em * q

    def store_c(i, first, size, e, em, z, zm, q):
        here = pl.ds(first - base, size)
        total = ind[i - H, here, :] + em * Q3[i - H, here, :] + M0[i - H, here, :] * q
        ind[i - H, here, :] = total * (-1.0 / (step_size * step_size))
        sens[i - H, here, :] = (z + zm) * (1.0 / step_size)

    def middle(E, Z, chunks, finish):
        def body(p, _):
            sweep(E, Z, H + 2 * p, 2, chunks, finish, True)
            return 0

        lax.fori_loop(0, cells_x // 2, body, 0)

    sweep(EA, ZA, H - 2, 2, all_chunks, store_a, False)
    middle(EA, ZA, all_chunks, store_a)
    sweep(EA, ZA, top, 2, all_chunks, store_a, False)
    sweep(EB, ZB, H - 1, 1, all_chunks, store_b, False)
    middle(EB, ZB, all_chunks, store_b)
    sweep(EB, ZB, top, 1, all_chunks, store_b, False)
    middle(EA, ZA, own_chunks, store_c)


def whole(memory=None):
    return pl.BlockSpec(memory_space=memory or pltpu.VMEM)


def exchange(up, down, axis):
    count = lax.axis_size(axis)
    forward = [(i, i + 1) for i in range(count - 1)]
    backward = [(b, a) for a, b in forward]
    return lax.ppermute(up, axis, forward), lax.ppermute(down, axis, backward)


def per_device(initial, material, goal_faces, conductivity):
    cells_x, cells_y, cells_z = initial.shape
    f32 = jnp.float32
    params = pltpu.CompilerParams(vmem_limit_bytes=LIMIT)
    shape = jax.ShapeDtypeStruct
    hbm = whole(pltpu.HBM)
    send = shape((cells_x + cells_x // 2, 8, cells_z), f32)
    block = shape(initial.shape, f32)
    side = shape((3 * HALO, cells_y, cells_z), f32)
    count = lax.axis_size("gx")
    u, kh, g, up, down, near, far = pl.pallas_call(
        pack_kernel,
        out_shape=(block, block, block, send, send, side, side),
        in_specs=[hbm, hbm, hbm, whole(pltpu.SMEM)],
        out_specs=(whole(),) * 7,
        scratch_shapes=[
            pltpu.VMEM(initial.shape, jnp.int32),
            pltpu.VMEM(initial.shape, jnp.int32),
            pltpu.SemaphoreType.DMA((3,)),
        ],
        compiler_params=params,
        name="pack",
    )(initial, material, goal_faces, conductivity)
    far_pairs = [[i % count, (i + 1) % count] for i in range(1, count, 2)]
    near_pairs = [[i, i + 1] for i in range(0, count, 2)]
    far_all = lax.all_gather(far, "gx", axis_index_groups=far_pairs, tiled=True)
    near_all = lax.all_gather(near, "gx", axis_index_groups=near_pairs, tiled=True)
    from_low, from_high = exchange(up, down, "gy")
    corner = shape((3 * HALO, 8, cells_z), f32)
    near_corner, far_corner = pl.pallas_call(
        functools.partial(corner_kernel, cells_x),
        out_shape=(corner, corner),
        in_specs=[whole()] * 2,
        out_specs=(whole(), whole()),
        compiler_params=params,
        name="corners",
    )(from_low, from_high)

    def swap(pairs):
        return [(a, b) for a, b in pairs] + [(b, a) for a, b in pairs]

    far_corner = lax.ppermute(far_corner, "gx", swap(far_pairs[:-1]))
    near_corner = lax.ppermute(near_corner, "gx", swap(near_pairs))
    planes = cells_x + 2 * HALO
    rows = cells_y + 8
    wide = pltpu.VMEM((planes, rows + 16, cells_z), f32)
    narrow = pltpu.VMEM((planes, rows, cells_z), f32)
    inner = pltpu.VMEM(initial.shape, f32)
    return pl.pallas_call(
        main_kernel,
        out_shape=(block, block),
        in_specs=[whole()] * 5 + [hbm, hbm] + [whole()] * 2,
        out_specs=(whole(), whole()),
        scratch_shapes=[pltpu.SemaphoreType.DMA((6,))]
        + [wide, wide, narrow, narrow, wide, narrow, narrow, wide, wide, wide, wide, inner, inner],
        compiler_params=params,
        name="chain",
    )(u, kh, g, from_low, from_high, near_all, far_all, near_corner, far_corner)


def solution(mesh):
    placed = (P("gx", "gy", None), P("gx", "gy", None), P("gx", "gy", None), P())
    return jax.shard_map(
        per_device,
        mesh=mesh,
        in_specs=placed,
        out_specs=(P("gx", "gy", None), P("gx", "gy", None)),
        check_vma=False,
    )
```

```python
import functools

import jax
import jax.numpy as jnp
from jax import lax
from jax.experimental import pallas as pl
from jax.experimental.pallas import tpu as pltpu
from jax.sharding import PartitionSpec as P

step_size = 0.075
HALO = 4
LIMIT = 40 * 1024 * 1024


def lanes_of(shape):
    return lax.broadcasted_iota(jnp.int32, shape, len(shape) - 1)


def half_weights(cond, lanes):
    lane = lanes_of((1, lanes))
    table = jnp.zeros((1, lanes), jnp.float32)
    for which in range(cond.shape[0]):
        table = jnp.where(lane == which, cond[which] * (0.5 * step_size), table)
    return table


def gather_rows(table, index):
    return jnp.take_along_axis(jnp.broadcast_to(table, index.shape), index, axis=1, mode="promise_in_bounds")


def far_kernel(initial, material, goal, cond, far, ids, flags, values, sems):
    cells_x, _, cells_z = initial.shape
    odd = lax.axis_index("gx") % 2
    planes = pl.ds(odd * (cells_x - HALO), HALO)
    moves = [
        pltpu.make_async_copy(source, target, sems.at[i])
        for i, (source, target) in enumerate((
            (cond, values),
            (material.at[planes], ids),
            (goal.at[planes], flags),
            (initial.at[planes], far.at[pl.ds(0, HALO)]),
        ))
    ]
    for move in moves:
        move.start()
    moves[0].wait()
    table = half_weights(values, cells_z)
    for move in moves[1:]:
        move.wait()
    for i in range(HALO):
        far[HALO + i] = gather_rows(table, ids[i])
        far[2 * HALO + i] = flags[i].astype(jnp.float32)


def pack_kernel(u, material, goal, cond, kh, up, down, near):
    cells_x, cells_y, cells_z = u.shape
    table = half_weights(cond, cells_z)
    low_half = lax.broadcasted_iota(jnp.int32, (8, cells_z), 0) < HALO
    top = cells_y - 8

    def pair(p, _):
        for i in (2 * p, 2 * p + 1):
            k = gather_rows(table, material[i])
            kh[i] = k
            up[i] = jnp.where(low_half, pltpu.roll(k[top:], HALO, 0), u[i, top:, :])
            down[i] = jnp.where(low_half, u[i, :8, :], pltpu.roll(k[:8], HALO, 0))
        for send, rows in ((up, pl.ds(top, 8)), (down, pl.ds(0, 8))):
            one = goal[2 * p, rows, :].astype(jnp.float32)
            two = pltpu.roll(goal[2 * p + 1, rows, :].astype(jnp.float32), HALO, 0)
            first, second = (two, one) if send is up else (one, two)
            send[cells_x + p] = jnp.where(low_half, first, second)
        return 0

    lax.fori_loop(0, cells_x // 2, pair, 0)
    odd = lax.axis_index("gx") % 2
    start = (1 - odd) * (cells_x - HALO)
    for i in range(HALO):
        near[i] = u[start + i]
        near[HALO + i] = kh[start + i]
        near[2 * HALO + i] = goal[start + i].astype(jnp.float32)


def halo_tiles(plane, cells_x, from_low, from_high, low_half):
    below, above = from_low[plane], from_high[plane]
    u = jnp.where(low_half, above, below)
    k = pltpu.roll(jnp.where(low_half, below, above), HALO, 0)
    return u, k


def goal_tiles(pair, cells_x, from_low, from_high, low_half):
    below, above = from_low[cells_x + pair], from_high[cells_x + pair]
    one = jnp.where(low_half, above, below)
    two = pltpu.roll(jnp.where(low_half, below, above), HALO, 0)
    return one, two


def corner_kernel(cells_x, from_low, from_high, near, far):
    cells_z = from_low.shape[-1]
    low_half = lax.broadcasted_iota(jnp.int32, (8, cells_z), 0) < HALO
    odd = lax.axis_index("gx") % 2
    last = cells_x - HALO
    for send, start in ((near, (1 - odd) * last), (far, odd * last)):
        for i in range(HALO):
            send[i], send[HALO + i] = halo_tiles(start + i, cells_x, from_low, from_high, low_half)
        for i in range(0, HALO, 2):
            one, two = goal_tiles(start // 2 + i // 2, cells_x, from_low, from_high, low_half)
            send[2 * HALO + i], send[2 * HALO + i + 1] = one, two


def main_kernel(initial, kh, goal, from_low, from_high, near, far, near_corner, far_corner, ind, sens,
                U, K, G, Wx, Wy, Wz, S, EA, EB, ZA, ZB, M0, Q3, AC, OI, OS, sems):
    cells_x, cells_y, cells_z = initial.shape
    H = HALO
    rows = cells_y + 8
    T = rows // 8
    top = H + cells_x
    planes = cells_x + 2 * H
    right = cells_z - 1
    low_half = lax.broadcasted_iota(jnp.int32, (8, cells_z), 0) < H
    lane = lanes_of((8, cells_z))
    gx, gy = lax.axis_index("gx"), lax.axis_index("gy")
    odd = gx % 2

    half = (1 - odd) * (3 * H)
    for source, offset, corner, at in (
        (near, half, near_corner, (1 - odd) * top),
        (far, 0, far_corner, odd * top),
    ):
        for field, ref in enumerate((U, K, G)):
            for i in range(H):
                ref[at + i, 0:cells_y, :] = source[offset + field * H + i]
                ref[at + i, cells_y:, :] = corner[field * H + i]

    def own(p, _):
        for i in (2 * p, 2 * p + 1):
            U[H + i, 0:cells_y, :] = initial[i]
            K[H + i, 0:cells_y, :] = kh[i]
            G[H + i, 0:cells_y, :] = goal[i].astype(jnp.float32)
            hu, hk = halo_tiles(i, cells_x, from_low, from_high, low_half)
            U[H + i, cells_y:, :] = hu
            K[H + i, cells_y:, :] = hk
        one, two = goal_tiles(p, cells_x, from_low, from_high, low_half)
        G[H + 2 * p, cells_y:, :] = one
        G[H + 2 * p + 1, cells_y:, :] = two
        return 0

    lax.fori_loop(0, cells_x // 2, own, 0)

    def rower(ref):
        return lambda i, j: ref[i, pl.ds(j, 8, stride=T), :]

    def tiler(ref):
        return lambda i, j: ref[i, j]

    def reader(load, start):
        seen = {}

        def read(d, j):
            if (d, j) not in seen:
                if j == -1:
                    seen[d, j] = pltpu.roll(load(start + d, T - 1), 1, 0)
                elif j == T:
                    seen[d, j] = pltpu.roll(load(start + d, 0), 7, 0)
                else:
                    seen[d, j] = load(start + d, j)
            return seen[d, j]

        return read

    def up_lane(value):
        return pltpu.roll(value, right, 1)

    def down_lane(value):
        return pltpu.roll(value, 1, 1)

    def inner_up(value):
        return jnp.where(lane == right, 0.0, up_lane(value))

    def inner_down(value):
        return jnp.where(lane == 0, 0.0, down_lane(value))

    def change(v, d, j, wx, wxm, wy, wym, wz, s):
        c = v(d, j)
        along = (wx * v(d + 1, j) + wxm * v(d - 1, j)) + (wy * v(d, j + 1) + wym * v(d, j - 1))
        return along + (wz * up_lane(c) + down_lane(wz * c)) - s * c

    def prelude(start, count):
        k, u, g = (reader(rower(ref), start) for ref in (K, U, G))
        for j in range(T):
            wx = {d: k(d, j) + k(d + 1, j) for d in range(-1, count)}
            flux = {d: g(d, j) * wx[d] for d in range(-1, count)}
            for d in range(count):
                i = start + d
                c = k(d, j)
                wy, wym = c + k(d, j + 1), c + k(d, j - 1)
                wzt, wzm = c + inner_up(c), c + inner_down(c)
                wz = jnp.where(lane == right, 0.0, wzt)
                s = ((wx[d] + wx[d - 1]) + (wy + wym)) + (wzt + wzm)
                Wx[i, j] = wx[d]
                Wy[i, j] = wy
                Wz[i, j] = wz
                S[i, j] = s
                EA[i, j] = change(u, d, j, wx[d], wx[d - 1], wy, wym, wz, s)
                ZA[i, j] = flux[d] - flux[d - 1]

    def prelude_body(p, _):
        prelude(1 + 2 * p, 2)
        return 0

    lax.fori_loop(0, (planes - 2) // 2, prelude_body, 0)
    for j in range(T):
        Wx[0, j] = K[0, pl.ds(j, 8, stride=T), :] + K[1, pl.ds(j, 8, stride=T), :]

    plane = jnp.zeros((T, 8, cells_z), jnp.float32)
    row = jnp.zeros((planes, 1, cells_z), jnp.float32)

    def clear_row(ref, r):
        ref[:, r % T, r // T : r // T + 1, :] = row

    @pl.when(gx == 0)
    def _():
        EA[H - 1] = plane
        Wx[H - 1] = plane

    @pl.when(gx == lax.axis_size("gx") - 1)
    def _():
        EA[top] = plane
        ZA[top] = plane
        Wx[top - 1] = plane

    @pl.when(gy == 0)
    def _():
        clear_row(EA, rows - 1)
        clear_row(Wy, rows - 1)

    @pl.when(gy == lax.axis_size("gy") - 1)
    def _():
        clear_row(EA, cells_y)
        clear_row(Wy, cells_y - 1)

    def sweep(E, Z, start, count, finish, box):
        e, z = reader(tiler(E), start), reader(tiler(Z), start)
        wxs, wys = reader(tiler(Wx), start), reader(tiler(Wy), start)
        for j in range(T):
            if box:
                sums = {d: z(d, j) + (z(d, j + 1) + z(d, j - 1)) for d in range(-1, count + 1)}
            for d in range(count):
                i = start + d
                weights = (wxs(d, j), wxs(d - 1, j), wys(d, j), wys(d, j - 1), Wz[i, j], S[i, j])
                em = change(e, d, j, *weights)
                zm = change(z, d, j, *weights)
                q = None
                if box:
                    xs = sums[d - 1] + sums[d] + sums[d + 1]
                    xs = xs + (inner_up(xs) + inner_down(xs))
                    q = xs * (1.0 / 27.0) - z(d, j)
                finish(i, j, e(d, j), em, z(d, j), zm, q)

    def store_a(i, j, e, em, z, zm, q):
        EB[i, j] = e + em
        ZB[i, j] = z + zm
        if q is not None:
            M0[i - H, j] = em
            Q3[i - H, j] = q

    def store_b(i, j, e, em, z, zm, q):
        EA[i, j] = e + em
        ZA[i, j] = z + zm
        if q is not None:
            AC[i - H, j] = em * q

    def store_c(i, j, e, em, z, zm, q):
        o = i - H
        total = AC[o, j] + em * Q3[o, j] + M0[o, j] * q
        OI[o, pl.ds(j, 8, stride=T), :] = total * (-1.0 / (step_size * step_size))
        OS[o, pl.ds(j, 8, stride=T), :] = (z + zm) * (1.0 / step_size)

    def middle(E, Z, finish):
        def body(p, _):
            sweep(E, Z, H + 2 * p, 2, finish, True)
            return 0

        lax.fori_loop(0, cells_x // 2, body, 0)

    sweep(EA, ZA, H - 2, 2, store_a, False)
    middle(EA, ZA, store_a)
    sweep(EA, ZA, top, 2, store_a, False)
    sweep(EB, ZB, H - 1, 1, store_b, False)
    middle(EB, ZB, store_b)
    sweep(EB, ZB, top, 1, store_b, False)

    def leave(p):
        pair = pl.ds(2 * p, 2)
        return [
            pltpu.make_async_copy(source.at[pair, pl.ds(0, cells_y), :], target.at[pair], sems.at[k, p])
            for k, (source, target) in enumerate(((OI, ind), (OS, sens)))
        ]

    def last(p, _):
        sweep(EA, ZA, H + 2 * p, 2, store_c, True)
        for move in leave(p):
            move.start()
        return 0

    lax.fori_loop(0, cells_x // 2, last, 0)

    def settle(p, _):
        for move in leave(p):
            move.wait()
        return 0

    lax.fori_loop(0, cells_x // 2, settle, 0)


def whole(memory=None):
    return pl.BlockSpec(memory_space=memory or pltpu.VMEM)


def exchange(up, down, axis):
    count = lax.axis_size(axis)
    forward = [(i, i + 1) for i in range(count - 1)]
    backward = [(b, a) for a, b in forward]
    return lax.ppermute(up, axis, forward), lax.ppermute(down, axis, backward)


def swap(pairs):
    return [(a, b) for a, b in pairs] + [(b, a) for a, b in pairs]


def per_device(initial, material, goal_faces, conductivity):
    cells_x, cells_y, cells_z = initial.shape
    f32 = jnp.float32
    params = pltpu.CompilerParams(vmem_limit_bytes=LIMIT)
    small = pltpu.CompilerParams(vmem_limit_bytes=LIMIT // 4)
    shape = jax.ShapeDtypeStruct
    hbm = whole(pltpu.HBM)
    send = shape((cells_x + cells_x // 2, 8, cells_z), f32)
    block = shape(initial.shape, f32)
    side = shape((3 * HALO, cells_y, cells_z), f32)
    count = lax.axis_size("gx")
    far_pairs = [(i, i + 1) for i in range(1, count - 1, 2)]
    near_pairs = [(i, i + 1) for i in range(0, count, 2)]

    here = [pltpu.with_memory_space_constraint(x, pltpu.HBM) for x in (initial, material, goal_faces, conductivity)]
    far = pl.pallas_call(
        far_kernel,
        out_shape=side,
        in_specs=[hbm] * 4,
        out_specs=whole(),
        scratch_shapes=[
            pltpu.VMEM((HALO, cells_y, cells_z), jnp.int32),
            pltpu.VMEM((HALO, cells_y, cells_z), jnp.int32),
            pltpu.SMEM(conductivity.shape, f32),
            pltpu.SemaphoreType.DMA((4,)),
        ],
        compiler_params=small,
        name="far",
    )(*here)
    far = lax.ppermute(far, "gx", swap(far_pairs))
    kh, up, down, near = pl.pallas_call(
        pack_kernel,
        out_shape=(block, send, send, side),
        in_specs=[whole(), whole(), whole(), whole(pltpu.SMEM)],
        out_specs=(whole(),) * 4,
        compiler_params=small,
        name="pack",
    )(initial, material, goal_faces, conductivity)
    from_low, from_high = exchange(up, down, "gy")
    near = lax.all_gather(near, "gx", axis_index_groups=[list(pair) for pair in near_pairs], tiled=True)
    corner = shape((3 * HALO, 8, cells_z), f32)
    near_corner, far_corner = pl.pallas_call(
        functools.partial(corner_kernel, cells_x),
        out_shape=(corner, corner),
        in_specs=[whole()] * 2,
        out_specs=(whole(), whole()),
        compiler_params=small,
        name="corners",
    )(from_low, from_high)
    far_corner = lax.ppermute(far_corner, "gx", swap(far_pairs))
    near_corner = lax.ppermute(near_corner, "gx", swap(near_pairs))
    planes = cells_x + 2 * HALO
    rows = cells_y + 8
    natural = pltpu.VMEM((planes, rows, cells_z), f32)
    wide = pltpu.VMEM((planes, rows // 8, 8, cells_z), f32)
    inner = pltpu.VMEM((cells_x, rows // 8, 8, cells_z), f32)
    out = pltpu.VMEM((cells_x, rows, cells_z), f32)
    return pl.pallas_call(
        main_kernel,
        out_shape=(block, block),
        in_specs=[whole()] * 9,
        out_specs=(hbm, hbm),
        scratch_shapes=[natural] * 3 + [wide] * 8 + [inner] * 3 + [out] * 2
        + [pltpu.SemaphoreType.DMA((2, cells_x // 2))],
        compiler_params=params,
        name="chain",
    )(initial, kh, goal_faces, from_low, from_high, near, far, near_corner, far_corner)


def solution(mesh):
    placed = (P("gx", "gy", None), P("gx", "gy", None), P("gx", "gy", None), P())
    return jax.shard_map(
        per_device,
        mesh=mesh,
        in_specs=placed,
        out_specs=(P("gx", "gy", None), P("gx", "gy", None)),
        check_vma=False,
    )
```

```python
import functools

import jax
import jax.numpy as jnp
from jax import lax
from jax.experimental import pallas as pl
from jax.experimental.pallas import tpu as pltpu
from jax.sharding import PartitionSpec as P

step_size = 0.075
HALO = 4
LIMIT = 40 * 1024 * 1024


def lanes_of(shape):
    return lax.broadcasted_iota(jnp.int32, shape, len(shape) - 1)


def half_weights(cond, lanes):
    lane = lanes_of((1, lanes))
    table = jnp.zeros((1, lanes), jnp.float32)
    for which in range(cond.shape[0]):
        table = jnp.where(lane == which, cond[which] * (0.5 * step_size), table)
    return table


def gather_rows(table, index):
    return jnp.take_along_axis(jnp.broadcast_to(table, index.shape), index, axis=1, mode="promise_in_bounds")


def edge_kernel(initial, material, goal, cond, up, down, u, ids, flags, values, sems):
    cells_x, cells_y, cells_z = initial.shape
    moves = [pltpu.make_async_copy(cond, values, sems.at[6])]
    for end, first in enumerate((0, cells_y - 8)):
        for k, (source, target) in enumerate(((material, ids), (initial, u), (goal, flags))):
            moves.append(pltpu.make_async_copy(
                source.at[:, pl.ds(first, 8), :], target.at[end], sems.at[3 * end + k]))
    for move in moves:
        move.start()
    low_half = lax.broadcasted_iota(jnp.int32, (8, cells_z), 0) < HALO
    moves[0].wait()
    table = half_weights(values, cells_z)
    for move in moves[1:]:
        move.wait()
    for i in range(cells_x):
        k_low = pltpu.roll(gather_rows(table, ids[0, i]), HALO, 0)
        k_high = pltpu.roll(gather_rows(table, ids[1, i]), HALO, 0)
        up[i] = jnp.where(low_half, k_high, u[1, i])
        down[i] = jnp.where(low_half, u[0, i], k_low)
    for p in range(cells_x // 2):
        one, two = flags[1, 2 * p], pltpu.roll(flags[1, 2 * p + 1], HALO, 0)
        up[cells_x + p] = jnp.where(low_half, two, one).astype(jnp.float32)
        one, two = flags[0, 2 * p], pltpu.roll(flags[0, 2 * p + 1], HALO, 0)
        down[cells_x + p] = jnp.where(low_half, one, two).astype(jnp.float32)


def face_planes(send, start, u, material, goal, table):
    cells_y = u.shape[1]
    for i in range(HALO):
        send[i, 0:cells_y, :] = u[start + i]
        send[HALO + i, 0:cells_y, :] = gather_rows(table, material[start + i])
        send[2 * HALO + i, 0:cells_y, :] = goal[start + i].astype(jnp.float32)


def far_kernel(u, material, goal, cond, up, far):
    cells_x, _, cells_z = u.shape
    odd = lax.axis_index("gx") % 2
    face_planes(far, odd * (cells_x - HALO), u, material, goal, half_weights(cond, cells_z))


def halo_tiles(plane, cells_x, from_low, from_high, low_half):
    below, above = from_low[plane], from_high[plane]
    u = jnp.where(low_half, above, below)
    k = pltpu.roll(jnp.where(low_half, below, above), HALO, 0)
    return u, k


def goal_tiles(pair, cells_x, from_low, from_high, low_half):
    below, above = from_low[cells_x + pair], from_high[cells_x + pair]
    one = jnp.where(low_half, above, below)
    two = pltpu.roll(jnp.where(low_half, below, above), HALO, 0)
    return one, two


def near_kernel(u, material, goal, cond, from_low, from_high, far, near, far_corner):
    cells_x, cells_y, cells_z = u.shape
    low_half = lax.broadcasted_iota(jnp.int32, (8, cells_z), 0) < HALO
    odd = lax.axis_index("gx") % 2
    last = cells_x - HALO
    face_planes(near, (1 - odd) * last, u, material, goal, half_weights(cond, cells_z))
    for send, rows, start in ((near, pl.ds(cells_y, 8), (1 - odd) * last), (far_corner, slice(None), odd * last)):
        for i in range(HALO):
            send[i, rows, :], send[HALO + i, rows, :] = halo_tiles(start + i, cells_x, from_low, from_high, low_half)
        for i in range(0, HALO, 2):
            one, two = goal_tiles(start // 2 + i // 2, cells_x, from_low, from_high, low_half)
            send[2 * HALO + i, rows, :], send[2 * HALO + i + 1, rows, :] = one, two


class Steps:
    def __init__(self, cells_x, cells_y, cells_z):
        self.rows = cells_y + 8
        self.cells = (cells_x, cells_y, cells_z)
        self.T = self.rows // 8
        self.right = cells_z - 1
        self.lane = lanes_of((8, cells_z))
        gx, gy = lax.axis_index("gx"), lax.axis_index("gy")
        self.odd = gx % 2
        self.sign = (1 - 2 * self.odd).astype(jnp.float32)
        self.no_far = (gx == 0) | (gx == lax.axis_size("gx") - 1)
        self.no_low, self.no_high = gy == 0, gy == lax.axis_size("gy") - 1

    def rower(self, ref):
        return lambda i, j: ref[i, pl.ds(j, 8, stride=self.T), :]

    def reader(self, load, start):
        seen = {}
        T = self.T

        def read(d, j):
            if (d, j) not in seen:
                if j == -1:
                    seen[d, j] = pltpu.roll(load(start + d, T - 1), 1, 0)
                elif j == T:
                    seen[d, j] = pltpu.roll(load(start + d, 0), 7, 0)
                else:
                    seen[d, j] = load(start + d, j)
            return seen[d, j]

        return read

    def up_lane(self, value):
        return pltpu.roll(value, self.right, 1)

    def down_lane(self, value):
        return pltpu.roll(value, 1, 1)

    def inner_up(self, value):
        return jnp.where(self.lane == self.right, 0.0, self.up_lane(value))

    def inner_down(self, value):
        return jnp.where(self.lane == 0, 0.0, self.down_lane(value))

    def change(self, v, d, j, wx, wxm, wy, wym, wz, s):
        c = v(d, j)
        along = (wx * v(d + 1, j) + wxm * v(d - 1, j)) + (wy * v(d, j + 1) + wym * v(d, j - 1))
        return along + (wz * self.up_lane(c) + self.down_lane(wz * c)) - s * c

    def prelude(self, loads, start, count, finish):
        k, u, g = (self.reader(load, start) for load in loads)
        for j in range(self.T):
            wx = {d: k(d, j) + k(d + 1, j) for d in range(-1, count)}
            flux = {d: (self.sign * g(d, j)) * wx[d] for d in range(-1, count)}
            for d in range(count):
                c = k(d, j)
                wy, wym = c + k(d, j + 1), c + k(d, j - 1)
                wzt, wzm = c + self.inner_up(c), c + self.inner_down(c)
                wz = jnp.where(self.lane == self.right, 0.0, wzt)
                s = ((wx[d] + wx[d - 1]) + (wy + wym)) + (wzt + wzm)
                e = self.change(u, d, j, wx[d], wx[d - 1], wy, wym, wz, s)
                finish(start + d, j, wx[d], wy, wz, s, e, flux[d] - flux[d - 1])

    def clear_rows(self, E, Wy, first, count):
        row = jnp.zeros((count, 1, self.cells[2]), jnp.float32)

        def clear(ref, r):
            at = r // self.T
            ref[first : first + count, r % self.T, at : at + 1, :] = row

        @pl.when(self.no_low)
        def _():
            clear(E, self.rows - 1)
            clear(Wy, self.rows - 1)

        @pl.when(self.no_high)
        def _():
            clear(E, self.cells[1])
            clear(Wy, self.cells[1] - 1)

    def sweep(self, loads, start, count, finish, boxes):
        le, lz, lwx, lwy, lwz, ls = loads
        e, z, wxs, wys = (self.reader(load, start) for load in (le, lz, lwx, lwy))
        for j in range(self.T):
            wanted = {d + o for d in range(count) if boxes[d] for o in (-1, 0, 1)}
            sums = {d: z(d, j) + (z(d, j + 1) + z(d, j - 1)) for d in sorted(wanted)}
            for d in range(count):
                i = start + d
                weights = (wxs(d, j), wxs(d - 1, j), wys(d, j), wys(d, j - 1), lwz(i, j), ls(i, j))
                em = self.change(e, d, j, *weights)
                zm = self.change(z, d, j, *weights)
                q = None
                if boxes[d]:
                    xs = sums[d - 1] + sums[d] + sums[d + 1]
                    xs = xs + (self.inner_up(xs) + self.inner_down(xs))
                    q = xs * (1.0 / 27.0) - z(d, j)
                finish(i, j, e(d, j), em, z(d, j), zm, q)

    def results(self, OI, OS, o, j, total, z):
        OI[o, pl.ds(j, 8, stride=self.T), :] = total * (-1.0 / (step_size * step_size))
        OS[o, pl.ds(j, 8, stride=self.T), :] = z * (1.0 / step_size)

    def leave(self, first, OI, OS, ind, sens, sems, p):
        pair = pl.ds(first, 2)
        return [
            pltpu.make_async_copy(source.at[pair, pl.ds(0, self.cells[1]), :], target.at[pair], sems.at[k, p])
            for k, (source, target) in enumerate(((OI, ind), (OS, sens)))
        ]


KEPT = (("EA", 5, 4), ("ZA", 5, 4), ("EB", 6, 2), ("ZB", 6, 2), ("Wx", 4, 4), ("Wy", 5, 3), ("Wz", 5, 3),
        ("S", 5, 3), ("M0", 6, 2), ("Q3", 6, 2), ("AC", 7, 1))
KEPT_PLANES = sum(count for _, _, count in KEPT)


def tiler(ref):
    return lambda i, j: ref[i, j]


def inner_kernel(initial, material, goal, cond, from_low, from_high, near, ind, sens, edge, kept,
                 U, K, G, Wx, Wy, Wz, S, EA, EB, ZA, ZB, M0, Q3, AC, OI, OS, sems):
    cells_x, cells_y, cells_z = initial.shape
    H = HALO
    steps = Steps(cells_x, cells_y, cells_z)
    odd = steps.odd
    planes = cells_x + 2 * H
    low_half = lax.broadcasted_iota(jnp.int32, (8, cells_z), 0) < H
    table = half_weights(cond, cells_z)
    side, step = odd * (planes - 1), 1 - 2 * odd

    def place(natural):
        return side + step * natural

    def own(p, _):
        ones = goal_tiles(p, cells_x, from_low, from_high, low_half)
        for d in range(2):
            i = 2 * p + d
            f = place(H + i)
            U[f, 0:cells_y, :] = initial[i]
            K[f, 0:cells_y, :] = gather_rows(table, material[i])
            G[f + 1 - odd, 0:cells_y, :] = goal[i].astype(jnp.float32)
            U[f, cells_y:, :], K[f, cells_y:, :] = halo_tiles(i, cells_x, from_low, from_high, low_half)
            G[f + 1 - odd, cells_y:, :] = ones[d]
        return 0

    lax.fori_loop(0, cells_x // 2, own, 0)
    for i in range(H):
        f = (1 - odd) * (H + cells_x + i) + odd * (planes - 1 - i)
        U[f] = near[i]
        K[f] = near[H + i]
        G[f + 1 - odd] = near[2 * H + i]
    for d in range(2):
        edge[d] = U[H + d]
        edge[2 + d] = K[H + d]
        edge[4 + d] = G[H + d + 1 - odd]

    def first_goal(i, j):
        return G[i + 1, pl.ds(j, 8, stride=steps.T), :]

    def begin(i, j, wx, wy, wz, s, e, z):
        Wx[i, j], Wy[i, j], Wz[i, j], S[i, j], EA[i, j], ZA[i, j] = wx, wy, wz, s, e, z

    def prelude(p, _):
        steps.prelude((steps.rower(K), steps.rower(U), first_goal), H + 1 + 2 * p, 2, begin)
        return 0

    lax.fori_loop(0, (planes - 2 - H) // 2, prelude, 0)
    for j in range(steps.T):
        k = steps.rower(K)
        Wx[H, j] = k(H, j) + k(H + 1, j)
    steps.clear_rows(EA, Wy, H + 1, planes - 2 - H)

    def store_a(i, j, e, em, z, zm, q):
        EB[i, j] = e + em
        ZB[i, j] = z + zm
        if q is not None:
            M0[i - H, j] = em
            Q3[i - H, j] = q

    def store_b(i, j, e, em, z, zm, q):
        EA[i, j] = e + em
        ZA[i, j] = z + zm
        if q is not None:
            AC[i - H, j] = em * q

    def store_c(i, j, e, em, z, zm, q):
        o = i - H
        total = AC[o, j] + em * Q3[o, j] + M0[o, j] * q
        steps.results(OI, OS, place(i) - H, j, total, z + zm)

    weights = tuple(tiler(ref) for ref in (Wx, Wy, Wz, S))

    def sweep(E, Z, start, finish, boxes):
        steps.sweep((tiler(E), tiler(Z)) + weights, start, len(boxes), finish, boxes)

    def many(E, Z, start, pairs, finish):
        def body(p, _):
            sweep(E, Z, start + 2 * p, finish, (True, True))
            return 0

        lax.fori_loop(0, pairs, body, 0)

    top = H + cells_x
    many(EA, ZA, H + 2, (cells_x - 2) // 2, store_a)
    sweep(EA, ZA, top, store_a, (False, False))
    many(EB, ZB, H + 3, (cells_x - 4) // 2, store_b)
    sweep(EB, ZB, top - 1, store_b, (True, False))

    def leave(p):
        f = H + 4 + 2 * p
        return steps.leave((1 - odd) * (f - H) + odd * (top - 2 - f), OI, OS, ind, sens, sems, p)

    def last(p, _):
        sweep(EA, ZA, H + 4 + 2 * p, store_c, (True, True))
        for move in leave(p):
            move.start()
        return 0

    lax.fori_loop(0, (cells_x - 4) // 2, last, 0)
    refs = dict(EA=EA, ZA=ZA, EB=EB, ZB=ZB, Wx=Wx, Wy=Wy, Wz=Wz, S=S, M0=M0, Q3=Q3, AC=AC)
    at = 0
    for name, first, count in KEPT:
        shift = H if name in ("M0", "Q3", "AC") else 0
        for d in range(count):
            kept[at + d] = refs[name][first - shift + d]
        at += count

    def settle(p, _):
        for move in leave(p):
            move.wait()
        return 0

    lax.fori_loop(0, (cells_x - 4) // 2, settle, 0)


def outer_kernel(far, far_corner, edge, kept, ind_in, sens_in, ind, sens,
                 U, K, G, Wx, Wy, Wz, S, EA, EB, EC, ZA, ZB, ZC, M0, Q3, AC, OI, OS, sems):
    cells_x, cells_y, cells_z = ind.shape
    H = HALO
    steps = Steps(cells_x, cells_y, cells_z)
    odd = steps.odd
    for i in range(H):
        f = (1 - odd) * i + odd * (H - 1 - i)
        for field, (ref, at) in enumerate(((U, f), (K, f), (G, f + 1 - odd))):
            ref[at, 0:cells_y, :] = far[field * H + i]
            ref[at, cells_y:, :] = far_corner[field * H + i]
    for d in range(2):
        U[H + d] = edge[d]
        K[H + d] = edge[2 + d]
        G[H + d + 1 - odd] = edge[4 + d]

    places, at = {}, 0
    for name, first, count in KEPT:
        places[name] = (first, at)
        at += count

    def mixed(ref, name, own_first, own_last):
        first, offset = places[name]

        def load(i, j):
            if own_first <= i <= own_last:
                return ref[i, j]
            return kept[offset + i - first, j]

        return load

    def first_goal(i, j):
        return G[i + 1, pl.ds(j, 8, stride=steps.T), :]

    def begin(i, j, wx, wy, wz, s, e, z):
        Wx[i, j], Wy[i, j], Wz[i, j], S[i, j], EA[i, j], ZA[i, j] = wx, wy, wz, s, e, z

    for start in (1, 3):
        steps.prelude((steps.rower(K), steps.rower(U), first_goal), start, 2, begin)
    for j in range(steps.T):
        k = steps.rower(K)
        Wx[0, j] = k(0, j) + k(1, j)
    steps.clear_rows(EA, Wy, 1, H)

    @pl.when(steps.no_far)
    def _():
        plane = jnp.zeros((steps.T, 8, cells_z), jnp.float32)
        EA[H - 1] = plane
        ZA[H - 1] = plane
        Wx[H - 1] = plane

    weights = (mixed(Wx, "Wx", 0, H), mixed(Wy, "Wy", 1, H), mixed(Wz, "Wz", 1, H), mixed(S, "S", 1, H))

    def store_a(i, j, e, em, z, zm, q):
        EB[i, j] = e + em
        ZB[i, j] = z + zm
        if q is not None:
            M0[i, j] = em
            Q3[i, j] = q

    def store_b(i, j, e, em, z, zm, q):
        EC[i, j] = e + em
        ZC[i, j] = z + zm
        if q is not None:
            AC[i, j] = em * q

    top = H + cells_x
    m0, q3, ac = mixed(M0, "M0", H, H + 1), mixed(Q3, "Q3", H, H + 1), mixed(AC, "AC", H, H + 2)

    def store_c(i, j, e, em, z, zm, q):
        total = ac(i, j) + em * q3(i, j) + m0(i, j) * q
        steps.results(OI, OS, (1 - odd) * (i - H) + odd * (top - 1 - i), j, total, z + zm)

    first = (mixed(EA, "EA", 1, H), mixed(ZA, "ZA", 1, H)) + weights
    second = (mixed(EB, "EB", 2, H + 1), mixed(ZB, "ZB", 2, H + 1)) + weights
    third = (mixed(EC, "EA", 3, H + 2), mixed(ZC, "ZA", 3, H + 2)) + weights
    steps.sweep(first, 2, 2, store_a, (False, False))
    steps.sweep(first, 4, 2, store_a, (True, True))
    steps.sweep(second, 3, 2, store_b, (False, True))
    steps.sweep(second, 5, 2, store_b, (True, True))
    moves = []
    for p in range(2):
        f = H + 2 * p
        steps.sweep(third, f, 2, store_c, (True, True))
        moves += steps.leave((1 - odd) * (f - H) + odd * (top - 2 - f), OI, OS, ind, sens, sems, p)
        for move in moves[-2:]:
            move.start()
    for move in moves:
        move.wait()


def whole(memory=None):
    return pl.BlockSpec(memory_space=memory or pltpu.VMEM)


def exchange(up, down, axis):
    count = lax.axis_size(axis)
    forward = [(i, i + 1) for i in range(count - 1)]
    backward = [(b, a) for a, b in forward]
    return lax.ppermute(up, axis, forward), lax.ppermute(down, axis, backward)


def swap(pairs):
    return [(a, b) for a, b in pairs] + [(b, a) for a, b in pairs]


def per_device(initial, material, goal_faces, conductivity):
    cells_x, cells_y, cells_z = initial.shape
    f32 = jnp.float32
    params = pltpu.CompilerParams(vmem_limit_bytes=LIMIT)
    small = pltpu.CompilerParams(vmem_limit_bytes=LIMIT // 4)
    shape = jax.ShapeDtypeStruct
    hbm, vmem, smem = whole(pltpu.HBM), whole(), whole(pltpu.SMEM)
    rows = cells_y + 8
    planes = cells_x + 2 * HALO
    send = shape((cells_x + cells_x // 2, 8, cells_z), f32)
    block = shape(initial.shape, f32)
    count = lax.axis_size("gx")
    far_pairs = [(i, i + 1) for i in range(1, count - 1, 2)]
    near_pairs = [(i, i + 1) for i in range(0, count, 2)]

    here = [pltpu.with_memory_space_constraint(x, pltpu.HBM) for x in (initial, material, goal_faces, conductivity)]
    ends = (2, cells_x, 8, cells_z)
    up, down = pl.pallas_call(
        edge_kernel,
        out_shape=(send, send),
        in_specs=[hbm] * 4,
        out_specs=(vmem, vmem),
        scratch_shapes=[
            pltpu.VMEM(ends, f32),
            pltpu.VMEM(ends, jnp.int32),
            pltpu.VMEM(ends, jnp.int32),
            pltpu.SMEM(conductivity.shape, f32),
            pltpu.SemaphoreType.DMA((7,)),
        ],
        compiler_params=small,
        name="edges",
    )(*here)
    from_low, from_high = exchange(up, down, "gy")
    far = pl.pallas_call(
        far_kernel,
        out_shape=shape((3 * HALO, cells_y, cells_z), f32),
        in_specs=[vmem, vmem, vmem, smem, whole(pl.ANY)],
        out_specs=vmem,
        compiler_params=small,
        name="far",
    )(initial, material, goal_faces, conductivity, up)
    far_sent = far
    far = lax.ppermute(far, "gx", swap(far_pairs))
    near, far_corner = pl.pallas_call(
        near_kernel,
        out_shape=(shape((3 * HALO, rows, cells_z), f32), shape((3 * HALO, 8, cells_z), f32)),
        in_specs=[vmem, vmem, vmem, smem, vmem, vmem, whole(pl.ANY)],
        out_specs=(vmem, vmem),
        compiler_params=small,
        cost_estimate=pl.CostEstimate(flops=1000, bytes_accessed=1000, transcendentals=0),
        name="near",
    )(initial, material, goal_faces, conductivity, from_low, from_high, far_sent)
    near = lax.ppermute(near, "gx", swap(near_pairs))
    far_corner = lax.ppermute(far_corner, "gx", swap(far_pairs))

    def tiles(count):
        return pltpu.VMEM((count, rows // 8, 8, cells_z), f32)

    def natural(count):
        return pltpu.VMEM((count, rows, cells_z), f32)

    ind, sens, edge, kept = pl.pallas_call(
        inner_kernel,
        out_shape=(block, block, shape((6, rows, cells_z), f32), shape((KEPT_PLANES, rows // 8, 8, cells_z), f32)),
        in_specs=[vmem, vmem, vmem, smem, vmem, vmem, vmem],
        out_specs=(hbm, hbm, vmem, vmem),
        scratch_shapes=[natural(planes), natural(planes), natural(planes + 1)]
        + [tiles(planes)] * 8 + [tiles(cells_x)] * 3 + [natural(cells_x)] * 2
        + [pltpu.SemaphoreType.DMA((2, (cells_x - 4) // 2))],
        compiler_params=params,
        cost_estimate=pl.CostEstimate(flops=1000, bytes_accessed=1000, transcendentals=0),
        name="inner",
    )(initial, material, goal_faces, conductivity, from_low, from_high, near)
    return pl.pallas_call(
        outer_kernel,
        out_shape=(block, block),
        in_specs=[vmem] * 4 + [hbm, hbm],
        out_specs=(hbm, hbm),
        scratch_shapes=[natural(HALO + 2), natural(HALO + 2), natural(HALO + 3)]
        + [tiles(2 * HALO)] * 13 + [natural(cells_x)] * 2 + [pltpu.SemaphoreType.DMA((2, 2))],
        input_output_aliases={4: 0, 5: 1},
        compiler_params=small,
        name="outer",
    )(far, far_corner, edge, kept, ind, sens)


def solution(mesh):
    placed = (P("gx", "gy", None), P("gx", "gy", None), P("gx", "gy", None), P())
    return jax.shard_map(
        per_device,
        mesh=mesh,
        in_specs=placed,
        out_specs=(P("gx", "gy", None), P("gx", "gy", None)),
        check_vma=False,
    )
```

```python
import functools

import jax
import jax.numpy as jnp
from jax import lax
from jax.experimental import pallas as pl
from jax.experimental.pallas import tpu as pltpu
from jax.sharding import PartitionSpec as P

step_size = 0.075
HALO = 4
LIMIT = 40 * 1024 * 1024


def lanes_of(shape):
    return lax.broadcasted_iota(jnp.int32, shape, len(shape) - 1)


def half_weights(cond, lanes):
    lane = lanes_of((1, lanes))
    table = jnp.zeros((1, lanes), jnp.float32)
    for which in range(cond.shape[0]):
        table = jnp.where(lane == which, cond[which] * (0.5 * step_size), table)
    return table


def gather_rows(table, index):
    return jnp.take_along_axis(jnp.broadcast_to(table, index.shape), index, axis=1, mode="promise_in_bounds")


def edge_kernel(initial, material, goal, cond, up, down, shared, u, ids, flags, values, sems):
    cells_x, cells_y, cells_z = initial.shape
    moves = [pltpu.make_async_copy(cond, values, sems.at[6])]
    for end, first in enumerate((0, cells_y - 8)):
        for k, (source, target) in enumerate(((material, ids), (initial, u), (goal, flags))):
            moves.append(pltpu.make_async_copy(
                source.at[:, pl.ds(first, 8), :], target.at[end], sems.at[3 * end + k]))
    for move in moves:
        move.start()
    low_half = lax.broadcasted_iota(jnp.int32, (8, cells_z), 0) < HALO
    moves[0].wait()
    table = half_weights(values, cells_z)
    shared[...] = jnp.broadcast_to(table, shared.shape)
    for move in moves[1:]:
        move.wait()
    for i in range(cells_x):
        k_low = pltpu.roll(gather_rows(table, ids[0, i]), HALO, 0)
        k_high = pltpu.roll(gather_rows(table, ids[1, i]), HALO, 0)
        up[i] = jnp.where(low_half, k_high, u[1, i])
        down[i] = jnp.where(low_half, u[0, i], k_low)
    for p in range(cells_x // 2):
        one, two = flags[1, 2 * p], pltpu.roll(flags[1, 2 * p + 1], HALO, 0)
        up[cells_x + p] = jnp.where(low_half, two, one).astype(jnp.float32)
        one, two = flags[0, 2 * p], pltpu.roll(flags[0, 2 * p + 1], HALO, 0)
        down[cells_x + p] = jnp.where(low_half, one, two).astype(jnp.float32)


def face_planes(send, start, u, material, goal, table):
    cells_y = u.shape[1]
    for i in range(HALO):
        send[i, 0:cells_y, :] = u[start + i]
        send[HALO + i, 0:cells_y, :] = gather_rows(table, material[start + i])
        send[2 * HALO + i, 0:cells_y, :] = goal[start + i].astype(jnp.float32)


def far_kernel(u, material, goal, table, up, far):
    cells_x = u.shape[0]
    odd = lax.axis_index("gx") % 2
    face_planes(far, odd * (cells_x - HALO), u, material, goal, table[0:1])


def halo_tiles(plane, cells_x, from_low, from_high, low_half):
    below, above = from_low[plane], from_high[plane]
    u = jnp.where(low_half, above, below)
    k = pltpu.roll(jnp.where(low_half, below, above), HALO, 0)
    return u, k


def goal_tiles(pair, cells_x, from_low, from_high, low_half):
    below, above = from_low[cells_x + pair], from_high[cells_x + pair]
    one = jnp.where(low_half, above, below)
    two = pltpu.roll(jnp.where(low_half, below, above), HALO, 0)
    return one, two


def near_kernel(u, material, goal, table, from_low, from_high, far, near_a, near_b, far_corner):
    cells_x, cells_y, cells_z = u.shape
    low_half = lax.broadcasted_iota(jnp.int32, (8, cells_z), 0) < HALO
    odd = lax.axis_index("gx") % 2
    last = cells_x - HALO
    near = Halves(near_a, near_b)
    face_planes(near, (1 - odd) * last, u, material, goal, table[0:1])
    for send, rows, start in ((near, pl.ds(cells_y, 8), (1 - odd) * last), (far_corner, slice(None), odd * last)):
        for i in range(HALO):
            send[i, rows, :], send[HALO + i, rows, :] = halo_tiles(start + i, cells_x, from_low, from_high, low_half)
        for i in range(0, HALO, 2):
            one, two = goal_tiles(start // 2 + i // 2, cells_x, from_low, from_high, low_half)
            send[2 * HALO + i, rows, :], send[2 * HALO + i + 1, rows, :] = one, two


class Halves:
    def __init__(self, *parts):
        self.parts, self.size = parts, parts[0].shape[0]

    def at_plane(self, index):
        plane, *rest = index if isinstance(index, tuple) else (index,)
        return self.parts[plane // self.size], (plane % self.size, *rest)

    def __getitem__(self, index):
        ref, inside = self.at_plane(index)
        return ref[inside]

    def __setitem__(self, index, value):
        ref, inside = self.at_plane(index)
        ref[inside] = value


class Steps:
    def __init__(self, cells_x, cells_y, cells_z):
        self.rows = cells_y + 8
        self.cells = (cells_x, cells_y, cells_z)
        self.T = self.rows // 8
        self.right = cells_z - 1
        self.lane = lanes_of((8, cells_z))
        gx, gy = lax.axis_index("gx"), lax.axis_index("gy")
        self.odd = gx % 2
        self.sign = (1 - 2 * self.odd).astype(jnp.float32)
        self.no_far = (gx == 0) | (gx == lax.axis_size("gx") - 1)
        self.no_low, self.no_high = gy == 0, gy == lax.axis_size("gy") - 1

    def rower(self, ref):
        return lambda i, j: ref[i, pl.ds(j, 8, stride=self.T), :]

    def reader(self, load, start):
        seen = {}
        T = self.T

        def read(d, j):
            if (d, j) not in seen:
                if j == -1:
                    seen[d, j] = pltpu.roll(load(start + d, T - 1), 1, 0)
                elif j == T:
                    seen[d, j] = pltpu.roll(load(start + d, 0), 7, 0)
                else:
                    seen[d, j] = load(start + d, j)
            return seen[d, j]

        return read

    def up_lane(self, value):
        return pltpu.roll(value, self.right, 1)

    def down_lane(self, value):
        return pltpu.roll(value, 1, 1)

    def inner_up(self, value):
        return jnp.where(self.lane == self.right, 0.0, self.up_lane(value))

    def inner_down(self, value):
        return jnp.where(self.lane == 0, 0.0, self.down_lane(value))

    def change(self, v, d, j, wx, wxm, wy, wym, wz, s):
        c = v(d, j)
        along = (wx * v(d + 1, j) + wxm * v(d - 1, j)) + (wy * v(d, j + 1) + wym * v(d, j - 1))
        return along + (wz * self.up_lane(c) + self.down_lane(wz * c)) - s * c

    def prelude(self, loads, start, count, finish):
        k, u, g = (self.reader(load, start) for load in loads)
        for j in range(self.T):
            wx = {d: k(d, j) + k(d + 1, j) for d in range(-1, count)}
            flux = {d: (self.sign * g(d, j)) * wx[d] for d in range(-1, count)}
            for d in range(count):
                c = k(d, j)
                wy, wym = c + k(d, j + 1), c + k(d, j - 1)
                wzt, wzm = c + self.inner_up(c), c + self.inner_down(c)
                wz = jnp.where(self.lane == self.right, 0.0, wzt)
                s = ((wx[d] + wx[d - 1]) + (wy + wym)) + (wzt + wzm)
                e = self.change(u, d, j, wx[d], wx[d - 1], wy, wym, wz, s)
                finish(start + d, j, wx[d], wy, wz, s, e, flux[d] - flux[d - 1])

    def clear_rows(self, E, Wy, first, count):
        row = jnp.zeros((count, 1, self.cells[2]), jnp.float32)

        def clear(ref, r):
            at = r // self.T
            ref[first : first + count, r % self.T, at : at + 1, :] = row

        @pl.when(self.no_low)
        def _():
            clear(E, self.rows - 1)
            clear(Wy, self.rows - 1)

        @pl.when(self.no_high)
        def _():
            clear(E, self.cells[1])
            clear(Wy, self.cells[1] - 1)

    def sweep(self, loads, start, count, finish, boxes):
        le, lz, lwx, lwy, lwz, ls = loads
        e, z, wxs, wys = (self.reader(load, start) for load in (le, lz, lwx, lwy))
        for j in range(self.T):
            wanted = {d + o for d in range(count) if boxes[d] for o in (-1, 0, 1)}
            sums = {d: z(d, j) + (z(d, j + 1) + z(d, j - 1)) for d in sorted(wanted)}
            for d in range(count):
                i = start + d
                weights = (wxs(d, j), wxs(d - 1, j), wys(d, j), wys(d, j - 1), lwz(i, j), ls(i, j))
                em = self.change(e, d, j, *weights)
                zm = self.change(z, d, j, *weights)
                q = None
                if boxes[d]:
                    xs = sums[d - 1] + sums[d] + sums[d + 1]
                    xs = xs + (self.inner_up(xs) + self.inner_down(xs))
                    q = xs * (1.0 / 27.0) - z(d, j)
                finish(i, j, e(d, j), em, z(d, j), zm, q)

    def results(self, OI, OS, o, j, total, z):
        OI[o, pl.ds(j, 8, stride=self.T), :] = total * (-1.0 / (step_size * step_size))
        OS[o, pl.ds(j, 8, stride=self.T), :] = z * (1.0 / step_size)

    def leave(self, first, OI, OS, ind, sens, sems, p):
        pair = pl.ds(first, 2)
        return [
            pltpu.make_async_copy(source.at[pair, pl.ds(0, self.cells[1]), :], target.at[pair], sems.at[k, p])
            for k, (source, target) in enumerate(((OI, ind), (OS, sens)))
        ]


KEPT = (("EA", 5, 4), ("ZA", 5, 4), ("EB", 6, 2), ("ZB", 6, 2), ("Wx", 4, 4), ("Wy", 5, 3), ("Wz", 5, 3),
        ("S", 5, 3), ("M0", 6, 2), ("Q3", 6, 2), ("AC", 7, 1))
KEPT_PLANES = sum(count for _, _, count in KEPT)


def tiler(ref):
    return lambda i, j: ref[i, j]


def inner_kernel(initial, material, goal, table, from_low, from_high, near_a, near_b, ind, sens, edge, kept,
                 U, K, G, Wx, Wy, Wz, S, EA, EB, ZA, ZB, M0, Q3, AC, OI, OS, sems):
    cells_x, cells_y, cells_z = initial.shape
    H = HALO
    steps = Steps(cells_x, cells_y, cells_z)
    odd = steps.odd
    planes = cells_x + 2 * H
    low_half = lax.broadcasted_iota(jnp.int32, (8, cells_z), 0) < H
    near = Halves(near_a, near_b)
    side, step = odd * (planes - 1), 1 - 2 * odd

    def place(natural):
        return side + step * natural

    def own(p, _):
        ones = goal_tiles(p, cells_x, from_low, from_high, low_half)
        for d in range(2):
            i = 2 * p + d
            f = place(H + i)
            U[f, 0:cells_y, :] = initial[i]
            K[f, 0:cells_y, :] = gather_rows(table[0:1], material[i])
            G[f + 1 - odd, 0:cells_y, :] = goal[i].astype(jnp.float32)
            U[f, cells_y:, :], K[f, cells_y:, :] = halo_tiles(i, cells_x, from_low, from_high, low_half)
            G[f + 1 - odd, cells_y:, :] = ones[d]
        return 0

    lax.fori_loop(0, cells_x // 2, own, 0)
    for i in range(H):
        f = (1 - odd) * (H + cells_x + i) + odd * (planes - 1 - i)
        U[f] = near[i]
        K[f] = near[H + i]
        G[f + 1 - odd] = near[2 * H + i]
    for d in range(2):
        edge[d] = U[H + d]
        edge[2 + d] = K[H + d]
        edge[4 + d] = G[H + d + 1 - odd]

    def first_goal(i, j):
        return G[i + 1, pl.ds(j, 8, stride=steps.T), :]

    def begin(i, j, wx, wy, wz, s, e, z):
        Wx[i, j], Wy[i, j], Wz[i, j], S[i, j], EA[i, j], ZA[i, j] = wx, wy, wz, s, e, z

    def prelude(p, _):
        steps.prelude((steps.rower(K), steps.rower(U), first_goal), H + 1 + 2 * p, 2, begin)
        return 0

    lax.fori_loop(0, (planes - 2 - H) // 2, prelude, 0)
    for j in range(steps.T):
        k = steps.rower(K)
        Wx[H, j] = k(H, j) + k(H + 1, j)
    steps.clear_rows(EA, Wy, H + 1, planes - 2 - H)

    def store_a(i, j, e, em, z, zm, q):
        EB[i, j] = e + em
        ZB[i, j] = z + zm
        if q is not None:
            M0[i - H, j] = em
            Q3[i - H, j] = q

    def store_b(i, j, e, em, z, zm, q):
        EA[i, j] = e + em
        ZA[i, j] = z + zm
        if q is not None:
            AC[i - H, j] = em * q

    def store_c(i, j, e, em, z, zm, q):
        o = i - H
        total = AC[o, j] + em * Q3[o, j] + M0[o, j] * q
        steps.results(OI, OS, place(i) - H, j, total, z + zm)

    weights = tuple(tiler(ref) for ref in (Wx, Wy, Wz, S))

    def sweep(E, Z, start, finish, boxes):
        steps.sweep((tiler(E), tiler(Z)) + weights, start, len(boxes), finish, boxes)

    def many(E, Z, start, pairs, finish):
        def body(p, _):
            sweep(E, Z, start + 2 * p, finish, (True, True))
            return 0

        lax.fori_loop(0, pairs, body, 0)

    top = H + cells_x
    many(EA, ZA, H + 2, (cells_x - 2) // 2, store_a)
    sweep(EA, ZA, top, store_a, (False, False))
    many(EB, ZB, H + 3, (cells_x - 4) // 2, store_b)
    sweep(EB, ZB, top - 1, store_b, (True, False))

    def leave(p):
        f = H + 4 + 2 * p
        return steps.leave((1 - odd) * (f - H) + odd * (top - 2 - f), OI, OS, ind, sens, sems, p)

    def last(p, _):
        sweep(EA, ZA, H + 4 + 2 * p, store_c, (True, True))
        for move in leave(p):
            move.start()
        return 0

    lax.fori_loop(0, (cells_x - 4) // 2, last, 0)
    refs = dict(EA=EA, ZA=ZA, EB=EB, ZB=ZB, Wx=Wx, Wy=Wy, Wz=Wz, S=S, M0=M0, Q3=Q3, AC=AC)
    at = 0
    for name, first, count in KEPT:
        shift = H if name in ("M0", "Q3", "AC") else 0
        for d in range(count):
            kept[at + d] = refs[name][first - shift + d]
        at += count

    def settle(p, _):
        for move in leave(p):
            move.wait()
        return 0

    lax.fori_loop(0, (cells_x - 4) // 2, settle, 0)


def outer_kernel(far, far_corner, edge, kept, ind_in, sens_in, ind, sens,
                 U, K, G, Wx, Wy, Wz, S, EA, EB, EC, ZA, ZB, ZC, M0, Q3, AC, OI, OS, sems):
    cells_x, cells_y, cells_z = ind.shape
    H = HALO
    steps = Steps(cells_x, cells_y, cells_z)
    odd = steps.odd
    for i in range(H):
        f = (1 - odd) * i + odd * (H - 1 - i)
        for field, (ref, at) in enumerate(((U, f), (K, f), (G, f + 1 - odd))):
            ref[at, 0:cells_y, :] = far[field * H + i]
            ref[at, cells_y:, :] = far_corner[field * H + i]
    for d in range(2):
        U[H + d] = edge[d]
        K[H + d] = edge[2 + d]
        G[H + d + 1 - odd] = edge[4 + d]

    places, at = {}, 0
    for name, first, count in KEPT:
        places[name] = (first, at)
        at += count

    def mixed(ref, name, own_first, own_last):
        first, offset = places[name]

        def load(i, j):
            if own_first <= i <= own_last:
                return ref[i, j]
            return kept[offset + i - first, j]

        return load

    def first_goal(i, j):
        return G[i + 1, pl.ds(j, 8, stride=steps.T), :]

    def begin(i, j, wx, wy, wz, s, e, z):
        Wx[i, j], Wy[i, j], Wz[i, j], S[i, j], EA[i, j], ZA[i, j] = wx, wy, wz, s, e, z

    for start in (1, 3):
        steps.prelude((steps.rower(K), steps.rower(U), first_goal), start, 2, begin)
    for j in range(steps.T):
        k = steps.rower(K)
        Wx[0, j] = k(0, j) + k(1, j)
    steps.clear_rows(EA, Wy, 1, H)

    @pl.when(steps.no_far)
    def _():
        plane = jnp.zeros((steps.T, 8, cells_z), jnp.float32)
        EA[H - 1] = plane
        ZA[H - 1] = plane
        Wx[H - 1] = plane

    weights = (mixed(Wx, "Wx", 0, H), mixed(Wy, "Wy", 1, H), mixed(Wz, "Wz", 1, H), mixed(S, "S", 1, H))

    def store_a(i, j, e, em, z, zm, q):
        EB[i, j] = e + em
        ZB[i, j] = z + zm
        if q is not None:
            M0[i, j] = em
            Q3[i, j] = q

    def store_b(i, j, e, em, z, zm, q):
        EC[i, j] = e + em
        ZC[i, j] = z + zm
        if q is not None:
            AC[i, j] = em * q

    top = H + cells_x
    m0, q3, ac = mixed(M0, "M0", H, H + 1), mixed(Q3, "Q3", H, H + 1), mixed(AC, "AC", H, H + 2)

    def store_c(i, j, e, em, z, zm, q):
        total = ac(i, j) + em * q3(i, j) + m0(i, j) * q
        steps.results(OI, OS, (1 - odd) * (i - H) + odd * (top - 1 - i), j, total, z + zm)

    first = (mixed(EA, "EA", 1, H), mixed(ZA, "ZA", 1, H)) + weights
    second = (mixed(EB, "EB", 2, H + 1), mixed(ZB, "ZB", 2, H + 1)) + weights
    third = (mixed(EC, "EA", 3, H + 2), mixed(ZC, "ZA", 3, H + 2)) + weights
    steps.sweep(first, 2, 2, store_a, (False, False))
    steps.sweep(first, 4, 2, store_a, (True, True))
    steps.sweep(second, 3, 2, store_b, (False, True))
    steps.sweep(second, 5, 2, store_b, (True, True))
    moves = []
    for p in range(2):
        f = H + 2 * p
        steps.sweep(third, f, 2, store_c, (True, True))
        moves += steps.leave((1 - odd) * (f - H) + odd * (top - 2 - f), OI, OS, ind, sens, sems, p)
        for move in moves[-2:]:
            move.start()
    for move in moves:
        move.wait()


def whole(memory=None):
    return pl.BlockSpec(memory_space=memory or pltpu.VMEM)


def exchange(up, down, axis):
    count = lax.axis_size(axis)
    forward = [(i, i + 1) for i in range(count - 1)]
    backward = [(b, a) for a, b in forward]
    return lax.ppermute(up, axis, forward), lax.ppermute(down, axis, backward)


def swap(pairs):
    return [(a, b) for a, b in pairs] + [(b, a) for a, b in pairs]


def per_device(initial, material, goal_faces, conductivity):
    cells_x, cells_y, cells_z = initial.shape
    f32 = jnp.float32
    params = pltpu.CompilerParams(vmem_limit_bytes=LIMIT)
    small = pltpu.CompilerParams(vmem_limit_bytes=LIMIT // 4)
    shape = jax.ShapeDtypeStruct
    hbm, vmem = whole(pltpu.HBM), whole()
    rows = cells_y + 8
    planes = cells_x + 2 * HALO
    send = shape((cells_x + cells_x // 2, 8, cells_z), f32)
    block = shape(initial.shape, f32)
    count = lax.axis_size("gx")
    far_pairs = [(i, i + 1) for i in range(1, count - 1, 2)]
    near_pairs = [(i, i + 1) for i in range(0, count, 2)]

    here = [pltpu.with_memory_space_constraint(x, pltpu.HBM) for x in (initial, material, goal_faces, conductivity)]
    ends = (2, cells_x, 8, cells_z)
    up, down, table = pl.pallas_call(
        edge_kernel,
        out_shape=(send, send, shape((8, cells_z), f32)),
        in_specs=[hbm] * 4,
        out_specs=(vmem, vmem, vmem),
        scratch_shapes=[
            pltpu.VMEM(ends, f32),
            pltpu.VMEM(ends, jnp.int32),
            pltpu.VMEM(ends, jnp.int32),
            pltpu.SMEM(conductivity.shape, f32),
            pltpu.SemaphoreType.DMA((7,)),
        ],
        compiler_params=small,
        name="edges",
    )(*here)
    from_low, from_high = exchange(up, down, "gy")
    far = pl.pallas_call(
        far_kernel,
        out_shape=shape((3 * HALO, cells_y, cells_z), f32),
        in_specs=[vmem] * 4 + [whole(pl.ANY)],
        out_specs=vmem,
        compiler_params=small,
        name="far",
    )(initial, material, goal_faces, table, up)
    far_sent = far
    far = lax.ppermute(far, "gx", swap(far_pairs))
    part = shape((3 * HALO // 2, rows, cells_z), f32)
    near_a, near_b, far_corner = pl.pallas_call(
        near_kernel,
        out_shape=(part, part, shape((3 * HALO, 8, cells_z), f32)),
        in_specs=[vmem] * 6 + [whole(pl.ANY)],
        out_specs=(vmem,) * 3,
        compiler_params=small,
        cost_estimate=pl.CostEstimate(flops=1000, bytes_accessed=1000, transcendentals=0),
        name="near",
    )(initial, material, goal_faces, table, from_low, from_high, far_sent)
    near_a = lax.ppermute(near_a, "gx", swap(near_pairs))
    near_b = lax.ppermute(near_b, "gx", swap(near_pairs))
    far_corner = lax.ppermute(far_corner, "gx", swap(far_pairs))

    def tiles(count):
        return pltpu.VMEM((count, rows // 8, 8, cells_z), f32)

    def natural(count):
        return pltpu.VMEM((count, rows, cells_z), f32)

    ind, sens, edge, kept = pl.pallas_call(
        inner_kernel,
        out_shape=(block, block, shape((6, rows, cells_z), f32), shape((KEPT_PLANES, rows // 8, 8, cells_z), f32)),
        in_specs=[vmem] * 8,
        out_specs=(hbm, hbm, vmem, vmem),
        scratch_shapes=[natural(planes), natural(planes), natural(planes + 1)]
        + [tiles(planes)] * 8 + [tiles(cells_x)] * 3 + [natural(cells_x)] * 2
        + [pltpu.SemaphoreType.DMA((2, (cells_x - 4) // 2))],
        compiler_params=params,
        cost_estimate=pl.CostEstimate(flops=1000, bytes_accessed=1000, transcendentals=0),
        name="inner",
    )(initial, material, goal_faces, table, from_low, from_high, near_a, near_b)
    return pl.pallas_call(
        outer_kernel,
        out_shape=(block, block),
        in_specs=[vmem] * 4 + [hbm, hbm],
        out_specs=(hbm, hbm),
        scratch_shapes=[natural(HALO + 2), natural(HALO + 2), natural(HALO + 3)]
        + [tiles(2 * HALO)] * 13 + [natural(cells_x)] * 2 + [pltpu.SemaphoreType.DMA((2, 2))],
        input_output_aliases={4: 0, 5: 1},
        compiler_params=small,
        name="outer",
    )(far, far_corner, edge, kept, ind, sens)


def solution(mesh):
    placed = (P("gx", "gy", None), P("gx", "gy", None), P("gx", "gy", None), P())
    return jax.shard_map(
        per_device,
        mesh=mesh,
        in_specs=placed,
        out_specs=(P("gx", "gy", None), P("gx", "gy", None)),
        check_vma=False,
    )
```

```python
import functools

import jax
import jax.numpy as jnp
from jax import lax
from jax.experimental import pallas as pl
from jax.experimental.pallas import tpu as pltpu
from jax.sharding import PartitionSpec as P

step_size = 0.075
HALO = 4
LIMIT = 40 * 1024 * 1024


def lanes_of(shape):
    return lax.broadcasted_iota(jnp.int32, shape, len(shape) - 1)


def half_weights(cond, lanes):
    lane = lanes_of((1, lanes))
    table = jnp.zeros((1, lanes), jnp.float32)
    for which in range(cond.shape[0]):
        table = jnp.where(lane == which, cond[which] * (0.5 * step_size), table)
    return table


def gather_rows(table, index):
    return jnp.take_along_axis(jnp.broadcast_to(table, index.shape), index, axis=1, mode="promise_in_bounds")


def edge_kernel(initial, material, goal, cond, up, down, shared, u, ids, flags, values, sems):
    cells_x, cells_y, cells_z = initial.shape
    moves = [pltpu.make_async_copy(cond, values, sems.at[6])]
    for end, first in enumerate((0, cells_y - 8)):
        for k, (source, target) in enumerate(((material, ids), (initial, u), (goal, flags))):
            moves.append(pltpu.make_async_copy(
                source.at[:, pl.ds(first, 8), :], target.at[end], sems.at[3 * end + k]))
    for move in moves:
        move.start()
    low_half = lax.broadcasted_iota(jnp.int32, (8, cells_z), 0) < HALO
    moves[0].wait()
    table = half_weights(values, cells_z)
    shared[...] = jnp.broadcast_to(table, shared.shape)
    for move in moves[1:]:
        move.wait()
    for i in range(cells_x):
        k_low = pltpu.roll(gather_rows(table, ids[0, i]), HALO, 0)
        k_high = pltpu.roll(gather_rows(table, ids[1, i]), HALO, 0)
        up[i] = jnp.where(low_half, k_high, u[1, i])
        down[i] = jnp.where(low_half, u[0, i], k_low)
    for p in range(cells_x // 2):
        one, two = flags[1, 2 * p], pltpu.roll(flags[1, 2 * p + 1], HALO, 0)
        up[cells_x + p] = jnp.where(low_half, two, one).astype(jnp.float32)
        one, two = flags[0, 2 * p], pltpu.roll(flags[0, 2 * p + 1], HALO, 0)
        down[cells_x + p] = jnp.where(low_half, one, two).astype(jnp.float32)


def face_planes(send, start, u, material, goal, table):
    cells_y = u.shape[1]
    for i in range(HALO):
        send[i, 0:cells_y, :] = u[start + i]
        send[HALO + i, 0:cells_y, :] = gather_rows(table, material[start + i])
        send[2 * HALO + i, 0:cells_y, :] = goal[start + i].astype(jnp.float32)


def far_kernel(u, material, goal, table, up, far):
    cells_x = u.shape[0]
    odd = lax.axis_index("gx") % 2
    face_planes(far, odd * (cells_x - HALO), u, material, goal, table[0:1])


def halo_tiles(plane, cells_x, from_low, from_high, low_half):
    below, above = from_low[plane], from_high[plane]
    u = jnp.where(low_half, above, below)
    k = pltpu.roll(jnp.where(low_half, below, above), HALO, 0)
    return u, k


def goal_tiles(pair, cells_x, from_low, from_high, low_half):
    below, above = from_low[cells_x + pair], from_high[cells_x + pair]
    one = jnp.where(low_half, above, below)
    two = pltpu.roll(jnp.where(low_half, below, above), HALO, 0)
    return one, two


def near_kernel(u, material, goal, table, from_low, from_high, far, near_a, near_b, far_corner):
    cells_x, cells_y, cells_z = u.shape
    low_half = lax.broadcasted_iota(jnp.int32, (8, cells_z), 0) < HALO
    odd = lax.axis_index("gx") % 2
    last = cells_x - HALO
    near = Halves(near_a, near_b)
    face_planes(near, (1 - odd) * last, u, material, goal, table[0:1])
    for send, rows, start in ((near, pl.ds(cells_y, 8), (1 - odd) * last), (far_corner, slice(None), odd * last)):
        for i in range(HALO):
            send[i, rows, :], send[HALO + i, rows, :] = halo_tiles(start + i, cells_x, from_low, from_high, low_half)
        for i in range(0, HALO, 2):
            one, two = goal_tiles(start // 2 + i // 2, cells_x, from_low, from_high, low_half)
            send[2 * HALO + i, rows, :], send[2 * HALO + i + 1, rows, :] = one, two


class Halves:
    def __init__(self, *parts):
        self.parts, self.size = parts, parts[0].shape[0]

    def at_plane(self, index):
        plane, *rest = index if isinstance(index, tuple) else (index,)
        return self.parts[plane // self.size], (plane % self.size, *rest)

    def __getitem__(self, index):
        ref, inside = self.at_plane(index)
        return ref[inside]

    def __setitem__(self, index, value):
        ref, inside = self.at_plane(index)
        ref[inside] = value


class Steps:
    def __init__(self, cells_x, cells_y, cells_z):
        self.rows = cells_y + 8
        self.cells = (cells_x, cells_y, cells_z)
        self.T = self.rows // 8
        self.right = cells_z - 1
        self.lane = lanes_of((8, cells_z))
        gx, gy = lax.axis_index("gx"), lax.axis_index("gy")
        self.odd = gx % 2
        self.sign = (1 - 2 * self.odd).astype(jnp.float32)
        self.no_far = (gx == 0) | (gx == lax.axis_size("gx") - 1)
        self.no_low, self.no_high = gy == 0, gy == lax.axis_size("gy") - 1

    def rower(self, ref):
        return lambda i, j: ref[i, pl.ds(j, 8, stride=self.T), :]

    def reader(self, load, start):
        seen = {}
        T = self.T

        def read(d, j):
            if (d, j) not in seen:
                if j == -1:
                    seen[d, j] = pltpu.roll(load(start + d, T - 1), 1, 0)
                elif j == T:
                    seen[d, j] = pltpu.roll(load(start + d, 0), 7, 0)
                else:
                    seen[d, j] = load(start + d, j)
            return seen[d, j]

        return read

    def up_lane(self, value):
        return pltpu.roll(value, self.right, 1)

    def down_lane(self, value):
        return pltpu.roll(value, 1, 1)

    def inner_up(self, value):
        return jnp.where(self.lane == self.right, 0.0, self.up_lane(value))

    def inner_down(self, value):
        return jnp.where(self.lane == 0, 0.0, self.down_lane(value))

    def change(self, v, d, j, wx, wxm, wy, wym, wz, s):
        c = v(d, j)
        along = (wx * v(d + 1, j) + wxm * v(d - 1, j)) + (wy * v(d, j + 1) + wym * v(d, j - 1))
        return along + (wz * self.up_lane(c) + self.down_lane(wz * c)) - s * c

    def prelude(self, loads, start, count, finish):
        k, u, g = (self.reader(load, start) for load in loads)
        for j in range(self.T):
            wx = {d: k(d, j) + k(d + 1, j) for d in range(-1, count)}
            flux = {d: (self.sign * g(d, j)) * wx[d] for d in range(-1, count)}
            for d in range(count):
                c = k(d, j)
                wy, wym = c + k(d, j + 1), c + k(d, j - 1)
                wzt, wzm = c + self.inner_up(c), c + self.inner_down(c)
                wz = jnp.where(self.lane == self.right, 0.0, wzt)
                s = ((wx[d] + wx[d - 1]) + (wy + wym)) + (wzt + wzm)
                e = self.change(u, d, j, wx[d], wx[d - 1], wy, wym, wz, s)
                finish(start + d, j, wx[d], wy, wz, s, e, flux[d] - flux[d - 1])

    def clear_rows(self, E, Wy, first, count):
        row = jnp.zeros((count, 1, self.cells[2]), jnp.float32)

        def clear(ref, r):
            at = r // self.T
            ref[first : first + count, r % self.T, at : at + 1, :] = row

        @pl.when(self.no_low)
        def _():
            clear(E, self.rows - 1)
            clear(Wy, self.rows - 1)

        @pl.when(self.no_high)
        def _():
            clear(E, self.cells[1])
            clear(Wy, self.cells[1] - 1)

    def sweep(self, loads, start, count, finish, boxes):
        le, lz, lwx, lwy, lwz, ls = loads
        e, z, wxs, wys = (self.reader(load, start) for load in (le, lz, lwx, lwy))
        for j in range(self.T):
            wanted = {d + o for d in range(count) if boxes[d] for o in (-1, 0, 1)}
            sums = {d: z(d, j) + (z(d, j + 1) + z(d, j - 1)) for d in sorted(wanted)}
            for d in range(count):
                i = start + d
                weights = (wxs(d, j), wxs(d - 1, j), wys(d, j), wys(d, j - 1), lwz(i, j), ls(i, j))
                em = self.change(e, d, j, *weights)
                zm = self.change(z, d, j, *weights)
                q = None
                if boxes[d]:
                    xs = sums[d - 1] + sums[d] + sums[d + 1]
                    xs = xs + (self.inner_up(xs) + self.inner_down(xs))
                    q = xs * (1.0 / 27.0) - z(d, j)
                finish(i, j, e(d, j), em, z(d, j), zm, q)

    def results(self, OI, OS, o, j, total, z):
        OI[o, pl.ds(j, 8, stride=self.T), :] = total * (-1.0 / (step_size * step_size))
        OS[o, pl.ds(j, 8, stride=self.T), :] = z * (1.0 / step_size)

    def leave(self, first, OI, OS, ind, sens, sems, p):
        pair = pl.ds(first, 2)
        return [
            pltpu.make_async_copy(source.at[pair, pl.ds(0, self.cells[1]), :], target.at[pair], sems.at[k, p])
            for k, (source, target) in enumerate(((OI, ind), (OS, sens)))
        ]


KEPT = (("EA", 5, 4), ("ZA", 5, 4), ("EB", 6, 2), ("ZB", 6, 2), ("Wx", 4, 4), ("Wy", 5, 3), ("Wz", 5, 3),
        ("S", 5, 3), ("M0", 6, 2), ("Q3", 6, 2), ("AC", 7, 1))
KEPT_PLANES = sum(count for _, _, count in KEPT)


def tiler(ref):
    return lambda i, j: ref[i, j]


def inner_kernel(initial, material, goal, table, from_low, from_high, near_a, near_b, ind, sens, edge, kept,
                 U, K, G, Wx, Wy, Wz, S, EA, EB, ZA, ZB, M0, Q3, AC, OI, OS, sems):
    cells_x, cells_y, cells_z = initial.shape
    H = HALO
    steps = Steps(cells_x, cells_y, cells_z)
    odd = steps.odd
    planes = cells_x + 2 * H
    low_half = lax.broadcasted_iota(jnp.int32, (8, cells_z), 0) < H
    near = Halves(near_a, near_b)
    side, step = odd * (planes - 1), 1 - 2 * odd

    def place(natural):
        return side + step * natural

    def own(p, _):
        ones = goal_tiles(p, cells_x, from_low, from_high, low_half)
        for d in range(2):
            i = 2 * p + d
            f = place(H + i)
            U[f, 0:cells_y, :] = initial[i]
            K[f, 0:cells_y, :] = gather_rows(table[0:1], material[i])
            G[f + 1 - odd, 0:cells_y, :] = goal[i].astype(jnp.float32)
            U[f, cells_y:, :], K[f, cells_y:, :] = halo_tiles(i, cells_x, from_low, from_high, low_half)
            G[f + 1 - odd, cells_y:, :] = ones[d]
        return 0

    lax.fori_loop(0, cells_x // 2, own, 0)
    for i in range(H):
        f = (1 - odd) * (H + cells_x + i) + odd * (planes - 1 - i)
        U[f] = near[i]
        K[f] = near[H + i]
        G[f + 1 - odd] = near[2 * H + i]
    for d in range(2):
        edge[d] = U[H + d]
        edge[2 + d] = K[H + d]
        edge[4 + d] = G[H + d + 1 - odd]

    def first_goal(i, j):
        return G[i + 1, pl.ds(j, 8, stride=steps.T), :]

    def begin(i, j, wx, wy, wz, s, e, z):
        Wx[i, j], Wy[i, j], Wz[i, j], S[i, j], EA[i, j], ZA[i, j] = wx, wy, wz, s, e, z

    def prelude(p, _):
        steps.prelude((steps.rower(K), steps.rower(U), first_goal), H + 1 + 2 * p, 2, begin)
        return 0

    lax.fori_loop(0, (planes - 2 - H) // 2, prelude, 0)
    for j in range(steps.T):
        k = steps.rower(K)
        Wx[H, j] = k(H, j) + k(H + 1, j)
    steps.clear_rows(EA, Wy, H + 1, planes - 2 - H)

    def store_a(i, j, e, em, z, zm, q):
        EB[i, j] = e + em
        ZB[i, j] = z + zm
        if q is not None:
            M0[i - H, j] = em
            Q3[i - H, j] = q

    def store_b(i, j, e, em, z, zm, q):
        EA[i, j] = e + em
        ZA[i, j] = z + zm
        if q is not None:
            AC[i - H, j] = em * q

    def store_c(i, j, e, em, z, zm, q):
        o = i - H
        total = AC[o, j] + em * Q3[o, j] + M0[o, j] * q
        steps.results(OI, OS, place(i) - H, j, total, z + zm)

    weights = tuple(tiler(ref) for ref in (Wx, Wy, Wz, S))

    def sweep(E, Z, start, finish, boxes):
        steps.sweep((tiler(E), tiler(Z)) + weights, start, len(boxes), finish, boxes)

    def many(E, Z, start, pairs, finish):
        def body(p, _):
            sweep(E, Z, start + 2 * p, finish, (True, True))
            return 0

        lax.fori_loop(0, pairs, body, 0)

    top = H + cells_x
    many(EA, ZA, H + 2, (cells_x - 2) // 2, store_a)
    sweep(EA, ZA, top, store_a, (False, False))
    many(EB, ZB, H + 3, (cells_x - 4) // 2, store_b)
    sweep(EB, ZB, top - 1, store_b, (True, False))

    def leave(p):
        f = H + 4 + 2 * p
        return steps.leave((1 - odd) * (f - H) + odd * (top - 2 - f), OI, OS, ind, sens, sems, p)

    def last(p, _):
        sweep(EA, ZA, H + 4 + 2 * p, store_c, (True, True))
        for move in leave(p):
            move.start()
        return 0

    lax.fori_loop(0, (cells_x - 4) // 2, last, 0)
    refs = dict(EA=EA, ZA=ZA, EB=EB, ZB=ZB, Wx=Wx, Wy=Wy, Wz=Wz, S=S, M0=M0, Q3=Q3, AC=AC)
    at = 0
    for name, first, count in KEPT:
        shift = H if name in ("M0", "Q3", "AC") else 0
        for d in range(count):
            kept[at + d] = refs[name][first - shift + d]
        at += count

    def settle(p, _):
        for move in leave(p):
            move.wait()
        return 0

    lax.fori_loop(0, (cells_x - 4) // 2, settle, 0)


def outer_kernel(far, far_corner, edge, kept, ind_in, sens_in, ind, sens,
                 U, K, G, Wx, Wy, Wz, S, EA, EB, EC, ZA, ZB, ZC, M0, Q3, AC, OI, OS, sems):
    cells_x, cells_y, cells_z = ind.shape
    H = HALO
    steps = Steps(cells_x, cells_y, cells_z)
    odd = steps.odd
    for i in range(H):
        f = (1 - odd) * i + odd * (H - 1 - i)
        for field, (ref, at) in enumerate(((U, f), (K, f), (G, f + 1 - odd))):
            ref[at, 0:cells_y, :] = far[field * H + i]
            ref[at, cells_y:, :] = far_corner[field * H + i]
    for d in range(2):
        U[H + d] = edge[d]
        K[H + d] = edge[2 + d]
        G[H + d + 1 - odd] = edge[4 + d]

    places, at = {}, 0
    for name, first, count in KEPT:
        places[name] = (first, at)
        at += count

    def mixed(ref, name, own_first, own_last):
        first, offset = places[name]

        def load(i, j):
            if own_first <= i <= own_last:
                return ref[i, j]
            return kept[offset + i - first, j]

        return load

    def first_goal(i, j):
        return G[i + 1, pl.ds(j, 8, stride=steps.T), :]

    def begin(i, j, wx, wy, wz, s, e, z):
        Wx[i, j], Wy[i, j], Wz[i, j], S[i, j], EA[i, j], ZA[i, j] = wx, wy, wz, s, e, z

    for start in (1, 3):
        steps.prelude((steps.rower(K), steps.rower(U), first_goal), start, 2, begin)
    for j in range(steps.T):
        k = steps.rower(K)
        Wx[0, j] = k(0, j) + k(1, j)
    steps.clear_rows(EA, Wy, 1, H)

    @pl.when(steps.no_far)
    def _():
        plane = jnp.zeros((steps.T, 8, cells_z), jnp.float32)
        EA[H - 1] = plane
        ZA[H - 1] = plane
        Wx[H - 1] = plane

    weights = (mixed(Wx, "Wx", 0, H), mixed(Wy, "Wy", 1, H), mixed(Wz, "Wz", 1, H), mixed(S, "S", 1, H))

    def store_a(i, j, e, em, z, zm, q):
        EB[i, j] = e + em
        ZB[i, j] = z + zm
        if q is not None:
            M0[i, j] = em
            Q3[i, j] = q

    def store_b(i, j, e, em, z, zm, q):
        EC[i, j] = e + em
        ZC[i, j] = z + zm
        if q is not None:
            AC[i, j] = em * q

    top = H + cells_x
    m0, q3, ac = mixed(M0, "M0", H, H + 1), mixed(Q3, "Q3", H, H + 1), mixed(AC, "AC", H, H + 2)

    def store_c(i, j, e, em, z, zm, q):
        total = ac(i, j) + em * q3(i, j) + m0(i, j) * q
        steps.results(OI, OS, (1 - odd) * (i - H) + odd * (top - 1 - i), j, total, z + zm)

    first = (mixed(EA, "EA", 1, H), mixed(ZA, "ZA", 1, H)) + weights
    second = (mixed(EB, "EB", 2, H + 1), mixed(ZB, "ZB", 2, H + 1)) + weights
    third = (mixed(EC, "EA", 3, H + 2), mixed(ZC, "ZA", 3, H + 2)) + weights
    steps.sweep(first, 2, 2, store_a, (False, False))
    steps.sweep(first, 4, 2, store_a, (True, True))
    steps.sweep(second, 3, 2, store_b, (False, True))
    steps.sweep(second, 5, 2, store_b, (True, True))
    moves = []
    for p in range(2):
        f = H + 2 * p
        steps.sweep(third, f, 2, store_c, (True, True))
        moves += steps.leave((1 - odd) * (f - H) + odd * (top - 2 - f), OI, OS, ind, sens, sems, p)
        for move in moves[-2:]:
            move.start()
    for move in moves:
        move.wait()


def whole(memory=None):
    return pl.BlockSpec(memory_space=memory or pltpu.VMEM)


def exchange(up, down, axis):
    count = lax.axis_size(axis)
    forward = [(i, i + 1) for i in range(count - 1)]
    backward = [(b, a) for a, b in forward]
    return lax.ppermute(up, axis, forward), lax.ppermute(down, axis, backward)


def swap(pairs):
    return [(a, b) for a, b in pairs] + [(b, a) for a, b in pairs]


def per_device(initial, material, goal_faces, conductivity):
    cells_x, cells_y, cells_z = initial.shape
    f32 = jnp.float32
    params = pltpu.CompilerParams(vmem_limit_bytes=LIMIT)
    small = pltpu.CompilerParams(vmem_limit_bytes=LIMIT // 4)
    shape = jax.ShapeDtypeStruct
    hbm, vmem = whole(pltpu.HBM), whole()
    rows = cells_y + 8
    planes = cells_x + 2 * HALO
    send = shape((cells_x + cells_x // 2, 8, cells_z), f32)
    block = shape(initial.shape, f32)
    count = lax.axis_size("gx")
    far_pairs = [(i, i + 1) for i in range(1, count - 1, 2)]
    near_pairs = [(i, i + 1) for i in range(0, count, 2)]

    here = [pltpu.with_memory_space_constraint(x, pltpu.HBM) for x in (initial, material, goal_faces, conductivity)]
    ends = (2, cells_x, 8, cells_z)
    up, down, table = pl.pallas_call(
        edge_kernel,
        out_shape=(send, send, shape((8, cells_z), f32)),
        in_specs=[hbm] * 4,
        out_specs=(vmem, vmem, vmem),
        scratch_shapes=[
            pltpu.VMEM(ends, f32),
            pltpu.VMEM(ends, jnp.int32),
            pltpu.VMEM(ends, jnp.int32),
            pltpu.SMEM(conductivity.shape, f32),
            pltpu.SemaphoreType.DMA((7,)),
        ],
        compiler_params=small,
        name="edges",
    )(*here)
    from_low, from_high = exchange(up, down, "gy")
    far = pl.pallas_call(
        far_kernel,
        out_shape=shape((3 * HALO, cells_y, cells_z), f32),
        in_specs=[vmem] * 4 + [whole(pl.ANY)],
        out_specs=vmem,
        compiler_params=small,
        name="far",
    )(initial, material, goal_faces, table, up)
    far_sent = far
    far = lax.ppermute(far, "gx", swap(far_pairs))
    part = shape((3 * HALO // 2, rows, cells_z), f32)
    near_a, near_b, far_corner = pl.pallas_call(
        near_kernel,
        out_shape=(part, part, shape((3 * HALO, 8, cells_z), f32)),
        in_specs=[vmem] * 6 + [whole(pl.ANY)],
        out_specs=(vmem,) * 3,
        compiler_params=small,
        cost_estimate=pl.CostEstimate(flops=10**9, bytes_accessed=1000, transcendentals=0),
        name="near",
    )(initial, material, goal_faces, table, from_low, from_high, far_sent)
    near_a = lax.ppermute(near_a, "gx", swap(near_pairs))
    near_b = lax.ppermute(near_b, "gx", swap(near_pairs))
    far_corner = lax.ppermute(far_corner, "gx", swap(far_pairs))

    def tiles(count):
        return pltpu.VMEM((count, rows // 8, 8, cells_z), f32)

    def natural(count):
        return pltpu.VMEM((count, rows, cells_z), f32)

    ind, sens, edge, kept = pl.pallas_call(
        inner_kernel,
        out_shape=(block, block, shape((6, rows, cells_z), f32), shape((KEPT_PLANES, rows // 8, 8, cells_z), f32)),
        in_specs=[vmem] * 8,
        out_specs=(hbm, hbm, vmem, vmem),
        scratch_shapes=[natural(planes), natural(planes), natural(planes + 1)]
        + [tiles(planes)] * 8 + [tiles(cells_x)] * 3 + [natural(cells_x)] * 2
        + [pltpu.SemaphoreType.DMA((2, (cells_x - 4) // 2))],
        compiler_params=params,
        cost_estimate=pl.CostEstimate(flops=1000, bytes_accessed=1000, transcendentals=0),
        name="inner",
    )(initial, material, goal_faces, table, from_low, from_high, near_a, near_b)
    return pl.pallas_call(
        outer_kernel,
        out_shape=(block, block),
        in_specs=[vmem] * 4 + [hbm, hbm],
        out_specs=(hbm, hbm),
        scratch_shapes=[natural(HALO + 2), natural(HALO + 2), natural(HALO + 3)]
        + [tiles(2 * HALO)] * 13 + [natural(cells_x)] * 2 + [pltpu.SemaphoreType.DMA((2, 2))],
        input_output_aliases={4: 0, 5: 1},
        compiler_params=small,
        name="outer",
    )(far, far_corner, edge, kept, ind, sens)


def solution(mesh):
    placed = (P("gx", "gy", None), P("gx", "gy", None), P("gx", "gy", None), P())
    return jax.shard_map(
        per_device,
        mesh=mesh,
        in_specs=placed,
        out_specs=(P("gx", "gy", None), P("gx", "gy", None)),
        check_vma=False,
    )
```

```python
import functools

import jax
import jax.numpy as jnp
from jax import lax
from jax.experimental import pallas as pl
from jax.experimental.pallas import tpu as pltpu
from jax.sharding import PartitionSpec as P

step_size = 0.075
HALO = 4
LIMIT = 40 * 1024 * 1024


def lanes_of(shape):
    return lax.broadcasted_iota(jnp.int32, shape, len(shape) - 1)


def half_weights(cond, lanes):
    lane = lanes_of((1, lanes))
    table = jnp.zeros((1, lanes), jnp.float32)
    for which in range(cond.shape[0]):
        table = jnp.where(lane == which, cond[which] * (0.5 * step_size), table)
    return table


def gather_rows(table, index):
    return jnp.take_along_axis(jnp.broadcast_to(table, index.shape), index, axis=1, mode="promise_in_bounds")


def edge_kernel(initial, material, goal, cond, up, down, shared, u, ids, flags, values, sems):
    cells_x, cells_y, cells_z = initial.shape
    moves = [pltpu.make_async_copy(cond, values, sems.at[6])]
    for end, first in enumerate((0, cells_y - 8)):
        for k, (source, target) in enumerate(((material, ids), (initial, u), (goal, flags))):
            moves.append(pltpu.make_async_copy(
                source.at[:, pl.ds(first, 8), :], target.at[end], sems.at[3 * end + k]))
    for move in moves:
        move.start()
    low_half = lax.broadcasted_iota(jnp.int32, (8, cells_z), 0) < HALO
    moves[0].wait()
    table = half_weights(values, cells_z)
    shared[...] = jnp.broadcast_to(table, shared.shape)
    for move in moves[1:]:
        move.wait()
    for i in range(cells_x):
        k_low = pltpu.roll(gather_rows(table, ids[0, i]), HALO, 0)
        k_high = pltpu.roll(gather_rows(table, ids[1, i]), HALO, 0)
        up[i] = jnp.where(low_half, k_high, u[1, i])
        down[i] = jnp.where(low_half, u[0, i], k_low)
    for p in range(cells_x // 2):
        one, two = flags[1, 2 * p], pltpu.roll(flags[1, 2 * p + 1], HALO, 0)
        up[cells_x + p] = jnp.where(low_half, two, one).astype(jnp.float32)
        one, two = flags[0, 2 * p], pltpu.roll(flags[0, 2 * p + 1], HALO, 0)
        down[cells_x + p] = jnp.where(low_half, one, two).astype(jnp.float32)


def face_planes(send, start, u, material, goal, table):
    cells_y = u.shape[1]
    for i in range(HALO):
        send[i, 0:cells_y, :] = u[start + i]
        send[HALO + i, 0:cells_y, :] = gather_rows(table, material[start + i])
        send[2 * HALO + i, 0:cells_y, :] = goal[start + i].astype(jnp.float32)


def far_kernel(u, material, goal, table, up, far):
    cells_x = u.shape[0]
    odd = lax.axis_index("gx") % 2
    face_planes(far, odd * (cells_x - HALO), u, material, goal, table[0:1])


def halo_tiles(plane, cells_x, from_low, from_high, low_half):
    below, above = from_low[plane], from_high[plane]
    u = jnp.where(low_half, above, below)
    k = pltpu.roll(jnp.where(low_half, below, above), HALO, 0)
    return u, k


def goal_tiles(pair, cells_x, from_low, from_high, low_half):
    below, above = from_low[cells_x + pair], from_high[cells_x + pair]
    one = jnp.where(low_half, above, below)
    two = pltpu.roll(jnp.where(low_half, below, above), HALO, 0)
    return one, two


def near_kernel(u, material, goal, table, from_low, from_high, far, near_a, near_b, far_corner):
    cells_x, cells_y, cells_z = u.shape
    low_half = lax.broadcasted_iota(jnp.int32, (8, cells_z), 0) < HALO
    odd = lax.axis_index("gx") % 2
    last = cells_x - HALO
    near = Halves(near_a, near_b)
    face_planes(near, (1 - odd) * last, u, material, goal, table[0:1])
    for send, rows, start in ((near, pl.ds(cells_y, 8), (1 - odd) * last), (far_corner, slice(None), odd * last)):
        for i in range(HALO):
            send[i, rows, :], send[HALO + i, rows, :] = halo_tiles(start + i, cells_x, from_low, from_high, low_half)
        for i in range(0, HALO, 2):
            one, two = goal_tiles(start // 2 + i // 2, cells_x, from_low, from_high, low_half)
            send[2 * HALO + i, rows, :], send[2 * HALO + i + 1, rows, :] = one, two


class Halves:
    def __init__(self, *parts):
        self.parts, self.size = parts, parts[0].shape[0]

    def at_plane(self, index):
        plane, *rest = index if isinstance(index, tuple) else (index,)
        return self.parts[plane // self.size], (plane % self.size, *rest)

    def __getitem__(self, index):
        ref, inside = self.at_plane(index)
        return ref[inside]

    def __setitem__(self, index, value):
        ref, inside = self.at_plane(index)
        ref[inside] = value


class Steps:
    def __init__(self, cells_x, cells_y, cells_z):
        self.rows = cells_y + 8
        self.cells = (cells_x, cells_y, cells_z)
        self.T = self.rows // 8
        self.right = cells_z - 1
        self.lane = lanes_of((8, cells_z))
        gx, gy = lax.axis_index("gx"), lax.axis_index("gy")
        self.odd = gx % 2
        self.sign = (1 - 2 * self.odd).astype(jnp.float32)
        self.no_far = (gx == 0) | (gx == lax.axis_size("gx") - 1)
        self.no_low, self.no_high = gy == 0, gy == lax.axis_size("gy") - 1

    def rower(self, ref):
        return lambda i, j: ref[i, pl.ds(j, 8, stride=self.T), :]

    def reader(self, load, start):
        seen = {}
        T = self.T

        def read(d, j):
            if (d, j) not in seen:
                if j == -1:
                    seen[d, j] = pltpu.roll(load(start + d, T - 1), 1, 0)
                elif j == T:
                    seen[d, j] = pltpu.roll(load(start + d, 0), 7, 0)
                else:
                    seen[d, j] = load(start + d, j)
            return seen[d, j]

        return read

    def up_lane(self, value):
        return pltpu.roll(value, self.right, 1)

    def down_lane(self, value):
        return pltpu.roll(value, 1, 1)

    def inner_up(self, value):
        return jnp.where(self.lane == self.right, 0.0, self.up_lane(value))

    def inner_down(self, value):
        return jnp.where(self.lane == 0, 0.0, self.down_lane(value))

    def change(self, v, d, j, wx, wxm, wy, wym, wz, s):
        c = v(d, j)
        along = (wx * v(d + 1, j) + wxm * v(d - 1, j)) + (wy * v(d, j + 1) + wym * v(d, j - 1))
        return along + (wz * self.up_lane(c) + self.down_lane(wz * c)) - s * c

    def prelude(self, loads, start, count, finish):
        k, u, g = (self.reader(load, start) for load in loads)
        for j in range(self.T):
            wx = {d: k(d, j) + k(d + 1, j) for d in range(-1, count)}
            flux = {d: (self.sign * g(d, j)) * wx[d] for d in range(-1, count)}
            for d in range(count):
                c = k(d, j)
                wy, wym = c + k(d, j + 1), c + k(d, j - 1)
                wzt, wzm = c + self.inner_up(c), c + self.inner_down(c)
                wz = jnp.where(self.lane == self.right, 0.0, wzt)
                s = ((wx[d] + wx[d - 1]) + (wy + wym)) + (wzt + wzm)
                e = self.change(u, d, j, wx[d], wx[d - 1], wy, wym, wz, s)
                finish(start + d, j, wx[d], wy, wz, s, e, flux[d] - flux[d - 1])

    def clear_rows(self, E, Wy, first, count):
        row = jnp.zeros((count, 1, self.cells[2]), jnp.float32)

        def clear(ref, r):
            at = r // self.T
            ref[first : first + count, r % self.T, at : at + 1, :] = row

        @pl.when(self.no_low)
        def _():
            clear(E, self.rows - 1)
            clear(Wy, self.rows - 1)

        @pl.when(self.no_high)
        def _():
            clear(E, self.cells[1])
            clear(Wy, self.cells[1] - 1)

    def sweep(self, loads, start, count, finish, boxes):
        le, lz, lwx, lwy, lwz, ls = loads
        e, z, wxs, wys = (self.reader(load, start) for load in (le, lz, lwx, lwy))
        for j in range(self.T):
            wanted = {d + o for d in range(count) if boxes[d] for o in (-1, 0, 1)}
            sums = {d: z(d, j) + (z(d, j + 1) + z(d, j - 1)) for d in sorted(wanted)}
            for d in range(count):
                i = start + d
                weights = (wxs(d, j), wxs(d - 1, j), wys(d, j), wys(d, j - 1), lwz(i, j), ls(i, j))
                em = self.change(e, d, j, *weights)
                zm = self.change(z, d, j, *weights)
                q = None
                if boxes[d]:
                    xs = sums[d - 1] + sums[d] + sums[d + 1]
                    xs = xs + (self.inner_up(xs) + self.inner_down(xs))
                    q = xs * (1.0 / 27.0) - z(d, j)
                finish(i, j, e(d, j), em, z(d, j), zm, q)

    def results(self, OI, OS, o, j, total, z):
        OI[o, pl.ds(j, 8, stride=self.T), :] = total * (-1.0 / (step_size * step_size))
        OS[o, pl.ds(j, 8, stride=self.T), :] = z * (1.0 / step_size)

    def leave(self, first, OI, OS, ind, sens, sems, p):
        pair = pl.ds(first, 2)
        return [
            pltpu.make_async_copy(source.at[pair, pl.ds(0, self.cells[1]), :], target.at[pair], sems.at[k, p])
            for k, (source, target) in enumerate(((OI, ind), (OS, sens)))
        ]


KEPT = (("EA", 5, 4), ("ZA", 5, 4), ("EB", 6, 2), ("ZB", 6, 2), ("Wx", 4, 4), ("Wy", 5, 3), ("Wz", 5, 3),
        ("S", 5, 3), ("M0", 6, 2), ("Q3", 6, 2), ("AC", 7, 1))
KEPT_PLANES = sum(count for _, _, count in KEPT)


def turns(count, body, together=3):
    full = count // together

    def turn(p, _):
        for d in range(together):
            body(together * p + d)
        return 0

    lax.fori_loop(0, full, turn, 0)
    for p in range(full * together, count):
        body(p)


def tiler(ref):
    return lambda i, j: ref[i, j]


def inner_kernel(initial, material, goal, table, from_low, from_high, near_a, near_b, ind, sens, edge, kept,
                 U, K, G, Wx, Wy, Wz, S, EA, EB, ZA, ZB, M0, Q3, AC, OI, OS, sems):
    cells_x, cells_y, cells_z = initial.shape
    H = HALO
    steps = Steps(cells_x, cells_y, cells_z)
    odd = steps.odd
    planes = cells_x + 2 * H
    low_half = lax.broadcasted_iota(jnp.int32, (8, cells_z), 0) < H
    near = Halves(near_a, near_b)
    side, step = odd * (planes - 1), 1 - 2 * odd

    def place(natural):
        return side + step * natural

    def own(p, _):
        ones = goal_tiles(p, cells_x, from_low, from_high, low_half)
        for d in range(2):
            i = 2 * p + d
            f = place(H + i)
            U[f, 0:cells_y, :] = initial[i]
            K[f, 0:cells_y, :] = gather_rows(table[0:1], material[i])
            G[f + 1 - odd, 0:cells_y, :] = goal[i].astype(jnp.float32)
            U[f, cells_y:, :], K[f, cells_y:, :] = halo_tiles(i, cells_x, from_low, from_high, low_half)
            G[f + 1 - odd, cells_y:, :] = ones[d]
        return 0

    lax.fori_loop(0, cells_x // 2, own, 0)
    for i in range(H):
        f = (1 - odd) * (H + cells_x + i) + odd * (planes - 1 - i)
        U[f] = near[i]
        K[f] = near[H + i]
        G[f + 1 - odd] = near[2 * H + i]
    for d in range(2):
        edge[d] = U[H + d]
        edge[2 + d] = K[H + d]
        edge[4 + d] = G[H + d + 1 - odd]

    def first_goal(i, j):
        return G[i + 1, pl.ds(j, 8, stride=steps.T), :]

    def begin(i, j, wx, wy, wz, s, e, z):
        Wx[i, j], Wy[i, j], Wz[i, j], S[i, j], EA[i, j], ZA[i, j] = wx, wy, wz, s, e, z

    def prelude(p):
        steps.prelude((steps.rower(K), steps.rower(U), first_goal), H + 1 + 2 * p, 2, begin)

    turns((planes - 2 - H) // 2, prelude)
    for j in range(steps.T):
        k = steps.rower(K)
        Wx[H, j] = k(H, j) + k(H + 1, j)
    steps.clear_rows(EA, Wy, H + 1, planes - 2 - H)

    def store_a(i, j, e, em, z, zm, q):
        EB[i, j] = e + em
        ZB[i, j] = z + zm
        if q is not None:
            M0[i - H, j] = em
            Q3[i - H, j] = q

    def store_b(i, j, e, em, z, zm, q):
        EA[i, j] = e + em
        ZA[i, j] = z + zm
        if q is not None:
            AC[i - H, j] = em * q

    def store_c(i, j, e, em, z, zm, q):
        o = i - H
        total = AC[o, j] + em * Q3[o, j] + M0[o, j] * q
        steps.results(OI, OS, place(i) - H, j, total, z + zm)

    weights = tuple(tiler(ref) for ref in (Wx, Wy, Wz, S))

    def sweep(E, Z, start, finish, boxes):
        steps.sweep((tiler(E), tiler(Z)) + weights, start, len(boxes), finish, boxes)

    def many(E, Z, start, pairs, finish):
        turns(pairs, lambda p: sweep(E, Z, start + 2 * p, finish, (True, True)))

    top = H + cells_x
    many(EA, ZA, H + 2, (cells_x - 2) // 2, store_a)
    sweep(EA, ZA, top, store_a, (False, False))
    many(EB, ZB, H + 3, (cells_x - 4) // 2, store_b)
    sweep(EB, ZB, top - 1, store_b, (True, False))

    def leave(p):
        f = H + 4 + 2 * p
        return steps.leave((1 - odd) * (f - H) + odd * (top - 2 - f), OI, OS, ind, sens, sems, p)

    def last(p):
        sweep(EA, ZA, H + 4 + 2 * p, store_c, (True, True))
        for move in leave(p):
            move.start()

    turns((cells_x - 4) // 2, last)
    refs = dict(EA=EA, ZA=ZA, EB=EB, ZB=ZB, Wx=Wx, Wy=Wy, Wz=Wz, S=S, M0=M0, Q3=Q3, AC=AC)
    at = 0
    for name, first, count in KEPT:
        shift = H if name in ("M0", "Q3", "AC") else 0
        for d in range(count):
            kept[at + d] = refs[name][first - shift + d]
        at += count

    def settle(p, _):
        for move in leave(p):
            move.wait()
        return 0

    lax.fori_loop(0, (cells_x - 4) // 2, settle, 0)


def outer_kernel(far, far_corner, edge, kept, ind_in, sens_in, ind, sens,
                 U, K, G, Wx, Wy, Wz, S, EA, EB, EC, ZA, ZB, ZC, M0, Q3, AC, OI, OS, sems):
    cells_x, cells_y, cells_z = ind.shape
    H = HALO
    steps = Steps(cells_x, cells_y, cells_z)
    odd = steps.odd
    for i in range(H):
        f = (1 - odd) * i + odd * (H - 1 - i)
        for field, (ref, at) in enumerate(((U, f), (K, f), (G, f + 1 - odd))):
            ref[at, 0:cells_y, :] = far[field * H + i]
            ref[at, cells_y:, :] = far_corner[field * H + i]
    for d in range(2):
        U[H + d] = edge[d]
        K[H + d] = edge[2 + d]
        G[H + d + 1 - odd] = edge[4 + d]

    places, at = {}, 0
    for name, first, count in KEPT:
        places[name] = (first, at)
        at += count

    def mixed(ref, name, own_first, own_last):
        first, offset = places[name]

        def load(i, j):
            if own_first <= i <= own_last:
                return ref[i, j]
            return kept[offset + i - first, j]

        return load

    def first_goal(i, j):
        return G[i + 1, pl.ds(j, 8, stride=steps.T), :]

    def begin(i, j, wx, wy, wz, s, e, z):
        Wx[i, j], Wy[i, j], Wz[i, j], S[i, j], EA[i, j], ZA[i, j] = wx, wy, wz, s, e, z

    for start in (1, 3):
        steps.prelude((steps.rower(K), steps.rower(U), first_goal), start, 2, begin)
    for j in range(steps.T):
        k = steps.rower(K)
        Wx[0, j] = k(0, j) + k(1, j)
    steps.clear_rows(EA, Wy, 1, H)

    @pl.when(steps.no_far)
    def _():
        plane = jnp.zeros((steps.T, 8, cells_z), jnp.float32)
        EA[H - 1] = plane
        ZA[H - 1] = plane
        Wx[H - 1] = plane

    weights = (mixed(Wx, "Wx", 0, H), mixed(Wy, "Wy", 1, H), mixed(Wz, "Wz", 1, H), mixed(S, "S", 1, H))

    def store_a(i, j, e, em, z, zm, q):
        EB[i, j] = e + em
        ZB[i, j] = z + zm
        if q is not None:
            M0[i, j] = em
            Q3[i, j] = q

    def store_b(i, j, e, em, z, zm, q):
        EC[i, j] = e + em
        ZC[i, j] = z + zm
        if q is not None:
            AC[i, j] = em * q

    top = H + cells_x
    m0, q3, ac = mixed(M0, "M0", H, H + 1), mixed(Q3, "Q3", H, H + 1), mixed(AC, "AC", H, H + 2)

    def store_c(i, j, e, em, z, zm, q):
        total = ac(i, j) + em * q3(i, j) + m0(i, j) * q
        steps.results(OI, OS, (1 - odd) * (i - H) + odd * (top - 1 - i), j, total, z + zm)

    first = (mixed(EA, "EA", 1, H), mixed(ZA, "ZA", 1, H)) + weights
    second = (mixed(EB, "EB", 2, H + 1), mixed(ZB, "ZB", 2, H + 1)) + weights
    third = (mixed(EC, "EA", 3, H + 2), mixed(ZC, "ZA", 3, H + 2)) + weights
    steps.sweep(first, 2, 2, store_a, (False, False))
    steps.sweep(first, 4, 2, store_a, (True, True))
    steps.sweep(second, 3, 2, store_b, (False, True))
    steps.sweep(second, 5, 2, store_b, (True, True))
    moves = []
    for p in range(2):
        f = H + 2 * p
        steps.sweep(third, f, 2, store_c, (True, True))
        moves += steps.leave((1 - odd) * (f - H) + odd * (top - 2 - f), OI, OS, ind, sens, sems, p)
        for move in moves[-2:]:
            move.start()
    for move in moves:
        move.wait()


def whole(memory=None):
    return pl.BlockSpec(memory_space=memory or pltpu.VMEM)


def exchange(up, down, axis):
    count = lax.axis_size(axis)
    forward = [(i, i + 1) for i in range(count - 1)]
    backward = [(b, a) for a, b in forward]
    return lax.ppermute(up, axis, forward), lax.ppermute(down, axis, backward)


def swap(pairs):
    return [(a, b) for a, b in pairs] + [(b, a) for a, b in pairs]


def per_device(initial, material, goal_faces, conductivity):
    cells_x, cells_y, cells_z = initial.shape
    f32 = jnp.float32
    params = pltpu.CompilerParams(vmem_limit_bytes=LIMIT)
    small = pltpu.CompilerParams(vmem_limit_bytes=LIMIT // 4)
    shape = jax.ShapeDtypeStruct
    hbm, vmem = whole(pltpu.HBM), whole()
    rows = cells_y + 8
    planes = cells_x + 2 * HALO
    send = shape((cells_x + cells_x // 2, 8, cells_z), f32)
    block = shape(initial.shape, f32)
    count = lax.axis_size("gx")
    far_pairs = [(i, i + 1) for i in range(1, count - 1, 2)]
    near_pairs = [(i, i + 1) for i in range(0, count, 2)]

    here = [pltpu.with_memory_space_constraint(x, pltpu.HBM) for x in (initial, material, goal_faces, conductivity)]
    ends = (2, cells_x, 8, cells_z)
    up, down, table = pl.pallas_call(
        edge_kernel,
        out_shape=(send, send, shape((8, cells_z), f32)),
        in_specs=[hbm] * 4,
        out_specs=(vmem, vmem, vmem),
        scratch_shapes=[
            pltpu.VMEM(ends, f32),
            pltpu.VMEM(ends, jnp.int32),
            pltpu.VMEM(ends, jnp.int32),
            pltpu.SMEM(conductivity.shape, f32),
            pltpu.SemaphoreType.DMA((7,)),
        ],
        compiler_params=small,
        name="edges",
    )(*here)
    from_low, from_high = exchange(up, down, "gy")
    far = pl.pallas_call(
        far_kernel,
        out_shape=shape((3 * HALO, cells_y, cells_z), f32),
        in_specs=[vmem] * 4 + [whole(pl.ANY)],
        out_specs=vmem,
        compiler_params=small,
        name="far",
    )(initial, material, goal_faces, table, up)
    far_sent = far
    far = lax.ppermute(far, "gx", swap(far_pairs))
    part = shape((3 * HALO // 2, rows, cells_z), f32)
    near_a, near_b, far_corner = pl.pallas_call(
        near_kernel,
        out_shape=(part, part, shape((3 * HALO, 8, cells_z), f32)),
        in_specs=[vmem] * 6 + [whole(pl.ANY)],
        out_specs=(vmem,) * 3,
        compiler_params=small,
        cost_estimate=pl.CostEstimate(flops=10**9, bytes_accessed=1000, transcendentals=0),
        name="near",
    )(initial, material, goal_faces, table, from_low, from_high, far_sent)
    near_a = lax.ppermute(near_a, "gx", swap(near_pairs))
    near_b = lax.ppermute(near_b, "gx", swap(near_pairs))
    far_corner = lax.ppermute(far_corner, "gx", swap(far_pairs))

    def tiles(count):
        return pltpu.VMEM((count, rows // 8, 8, cells_z), f32)

    def natural(count):
        return pltpu.VMEM((count, rows, cells_z), f32)

    ind, sens, edge, kept = pl.pallas_call(
        inner_kernel,
        out_shape=(block, block, shape((6, rows, cells_z), f32), shape((KEPT_PLANES, rows // 8, 8, cells_z), f32)),
        in_specs=[vmem] * 8,
        out_specs=(hbm, hbm, vmem, vmem),
        scratch_shapes=[natural(planes), natural(planes), natural(planes + 1)]
        + [tiles(planes)] * 8 + [tiles(cells_x)] * 3 + [natural(cells_x)] * 2
        + [pltpu.SemaphoreType.DMA((2, (cells_x - 4) // 2))],
        compiler_params=params,
        cost_estimate=pl.CostEstimate(flops=1000, bytes_accessed=1000, transcendentals=0),
        name="inner",
    )(initial, material, goal_faces, table, from_low, from_high, near_a, near_b)
    return pl.pallas_call(
        outer_kernel,
        out_shape=(block, block),
        in_specs=[vmem] * 4 + [hbm, hbm],
        out_specs=(hbm, hbm),
        scratch_shapes=[natural(HALO + 2), natural(HALO + 2), natural(HALO + 3)]
        + [tiles(2 * HALO)] * 13 + [natural(cells_x)] * 2 + [pltpu.SemaphoreType.DMA((2, 2))],
        input_output_aliases={4: 0, 5: 1},
        compiler_params=small,
        name="outer",
    )(far, far_corner, edge, kept, ind, sens)


def solution(mesh):
    placed = (P("gx", "gy", None), P("gx", "gy", None), P("gx", "gy", None), P())
    return jax.shard_map(
        per_device,
        mesh=mesh,
        in_specs=placed,
        out_specs=(P("gx", "gy", None), P("gx", "gy", None)),
        check_vma=False,
    )
```

```python
import functools

import jax
import jax.numpy as jnp
from jax import lax
from jax.experimental import pallas as pl
from jax.experimental.pallas import tpu as pltpu
from jax.sharding import PartitionSpec as P

step_size = 0.075
HALO = 4
LIMIT = 40 * 1024 * 1024


def lanes_of(shape):
    return lax.broadcasted_iota(jnp.int32, shape, len(shape) - 1)


def half_weights(cond, lanes):
    lane = lanes_of((1, lanes))
    table = jnp.zeros((1, lanes), jnp.float32)
    for which in range(cond.shape[0]):
        table = jnp.where(lane == which, cond[which] * (0.5 * step_size), table)
    return table


def gather_rows(table, index):
    return jnp.take_along_axis(jnp.broadcast_to(table, index.shape), index, axis=1, mode="promise_in_bounds")


def edge_kernel(initial, material, goal, cond, up, down, shared, u, ids, flags, values, sems):
    cells_x, cells_y, cells_z = initial.shape
    moves = [pltpu.make_async_copy(cond, values, sems.at[6])]
    for end, first in enumerate((0, cells_y - 8)):
        for k, (source, target) in enumerate(((material, ids), (initial, u), (goal, flags))):
            moves.append(pltpu.make_async_copy(
                source.at[:, pl.ds(first, 8), :], target.at[end], sems.at[3 * end + k]))
    for move in moves:
        move.start()
    low_half = lax.broadcasted_iota(jnp.int32, (8, cells_z), 0) < HALO
    moves[0].wait()
    table = half_weights(values, cells_z)
    shared[...] = jnp.broadcast_to(table, shared.shape)
    for move in moves[1:]:
        move.wait()
    for i in range(cells_x):
        k_low = pltpu.roll(gather_rows(table, ids[0, i]), HALO, 0)
        k_high = pltpu.roll(gather_rows(table, ids[1, i]), HALO, 0)
        up[i] = jnp.where(low_half, k_high, u[1, i])
        down[i] = jnp.where(low_half, u[0, i], k_low)
    for p in range(cells_x // 2):
        one, two = flags[1, 2 * p], pltpu.roll(flags[1, 2 * p + 1], HALO, 0)
        up[cells_x + p] = jnp.where(low_half, two, one).astype(jnp.float32)
        one, two = flags[0, 2 * p], pltpu.roll(flags[0, 2 * p + 1], HALO, 0)
        down[cells_x + p] = jnp.where(low_half, one, two).astype(jnp.float32)


def face_planes(send, start, u, material, goal, table):
    cells_y = u.shape[1]
    for i in range(HALO):
        send[i, 0:cells_y, :] = u[start + i]
        send[HALO + i, 0:cells_y, :] = gather_rows(table, material[start + i])
        send[2 * HALO + i, 0:cells_y, :] = goal[start + i].astype(jnp.float32)


def far_order(odd, cells_x):
    last = cells_x - HALO
    return (
        lambda f: odd * (last + f) + (1 - odd) * (HALO - 1 - f),
        lambda f: odd * (last + f) + (1 - odd) * max(HALO - 2 - f, 0),
    )


def far_kernel(u, material, goal, table, up, far):
    plane, cell = far_order(lax.axis_index("gx") % 2, u.shape[0])
    kappa = [gather_rows(table[0:1], material[plane(f)]) for f in range(HALO)]
    face = kappa[0] + kappa[1]
    far[3] = face * (u[plane(0)] - u[plane(1)])
    far[7] = face * goal[cell(0)].astype(jnp.float32)
    for f in range(1, HALO):
        far[f - 1] = u[plane(f)]
        far[3 + f] = kappa[f]
        far[7 + f] = goal[cell(f)].astype(jnp.float32)


def halo_tiles(plane, cells_x, from_low, from_high, low_half):
    below, above = from_low[plane], from_high[plane]
    u = jnp.where(low_half, above, below)
    k = pltpu.roll(jnp.where(low_half, below, above), HALO, 0)
    return u, k


def goal_tiles(pair, cells_x, from_low, from_high, low_half):
    below, above = from_low[cells_x + pair], from_high[cells_x + pair]
    one = jnp.where(low_half, above, below)
    two = pltpu.roll(jnp.where(low_half, below, above), HALO, 0)
    return one, two


def near_kernel(u, material, goal, table, from_low, from_high, far, near_a, near_b, far_corner):
    cells_x, cells_y, cells_z = u.shape
    low_half = lax.broadcasted_iota(jnp.int32, (8, cells_z), 0) < HALO
    odd = lax.axis_index("gx") % 2
    last = cells_x - HALO
    near = Halves(near_a, near_b)
    face_planes(near, (1 - odd) * last, u, material, goal, table[0:1])

    def all_tiles(start):
        us, ks, gs = [], [], []
        for i in range(HALO):
            hu, hk = halo_tiles(start + i, cells_x, from_low, from_high, low_half)
            us.append(hu)
            ks.append(hk)
        for i in range(0, HALO, 2):
            gs += goal_tiles(start // 2 + i // 2, cells_x, from_low, from_high, low_half)
        return us, ks, gs

    for field, tiles in enumerate(all_tiles((1 - odd) * last)):
        for i in range(HALO):
            near[field * HALO + i, pl.ds(cells_y, 8), :] = tiles[i]

    us, ks, gs = all_tiles(odd * last)
    is_odd = jnp.broadcast_to(odd == 1, low_half.shape)
    us, ks = [[jnp.where(is_odd, t[f], t[HALO - 1 - f]) for f in range(HALO)] for t in (us, ks)]
    gs = [jnp.where(is_odd, gs[f], gs[max(HALO - 2 - f, 0)]) for f in range(HALO)]
    flux = gs[0] * (ks[0] + ks[1])
    sub = lax.broadcasted_iota(jnp.int32, low_half.shape, 0)
    two, four = (sub == 3) | (sub == 4), (sub >= 2) & (sub <= 5)
    far_corner[0] = jnp.where(two, pltpu.roll(us[1], HALO, 0), us[3])
    far_corner[1] = ks[3]
    far_corner[2] = jnp.where(two, pltpu.roll(flux, HALO, 0), gs[3])
    far_corner[3] = ks[2]
    far_corner[4] = gs[2]
    far_corner[5] = jnp.where(four, pltpu.roll(ks[1], HALO, 0), us[2])
    far_corner[6] = gs[1]


class Halves:
    def __init__(self, *parts):
        self.parts, self.size = parts, parts[0].shape[0]

    def at_plane(self, index):
        plane, *rest = index if isinstance(index, tuple) else (index,)
        return self.parts[plane // self.size], (plane % self.size, *rest)

    def __getitem__(self, index):
        ref, inside = self.at_plane(index)
        return ref[inside]

    def __setitem__(self, index, value):
        ref, inside = self.at_plane(index)
        ref[inside] = value


class Steps:
    def __init__(self, cells_x, cells_y, cells_z):
        self.rows = cells_y + 8
        self.cells = (cells_x, cells_y, cells_z)
        self.T = self.rows // 8
        self.right = cells_z - 1
        self.lane = lanes_of((8, cells_z))
        gx, gy = lax.axis_index("gx"), lax.axis_index("gy")
        self.odd = gx % 2
        self.sign = (1 - 2 * self.odd).astype(jnp.float32)
        self.no_far = (gx == 0) | (gx == lax.axis_size("gx") - 1)
        self.no_low, self.no_high = gy == 0, gy == lax.axis_size("gy") - 1

    def rower(self, ref):
        return lambda i, j: ref[i, pl.ds(j, 8, stride=self.T), :]

    def reader(self, load, start):
        seen = {}
        T = self.T

        def read(d, j):
            if (d, j) not in seen:
                if j == -1:
                    seen[d, j] = pltpu.roll(load(start + d, T - 1), 1, 0)
                elif j == T:
                    seen[d, j] = pltpu.roll(load(start + d, 0), 7, 0)
                else:
                    seen[d, j] = load(start + d, j)
            return seen[d, j]

        return read

    def up_lane(self, value):
        return pltpu.roll(value, self.right, 1)

    def down_lane(self, value):
        return pltpu.roll(value, 1, 1)

    def inner_up(self, value):
        return jnp.where(self.lane == self.right, 0.0, self.up_lane(value))

    def inner_down(self, value):
        return jnp.where(self.lane == 0, 0.0, self.down_lane(value))

    def change(self, v, d, j, wx, wxm, wy, wym, wz, s, inflow=None):
        c = v(d, j)
        below = wxm * v(d - 1, j) if inflow is None else inflow
        along = (wx * v(d + 1, j) + below) + (wy * v(d, j + 1) + wym * v(d, j - 1))
        return along + (wz * self.up_lane(c) + self.down_lane(wz * c)) - s * c

    def prelude(self, loads, start, count, finish, outermost=None):
        k, u, g = (self.reader(load, start) for load in loads)
        for j in range(self.T):
            low = -1 if outermost is None else 0
            wx = {d: k(d, j) + k(d + 1, j) for d in range(low, count)}
            flux = {d: (self.sign * g(d, j)) * wx[d] for d in range(low, count)}
            inflow = None
            if outermost is not None:
                inflow, flux[-1] = outermost[0](j), self.sign * outermost[1](j)
            for d in range(count):
                c = k(d, j)
                wy, wym = c + k(d, j + 1), c + k(d, j - 1)
                wzt, wzm = c + self.inner_up(c), c + self.inner_down(c)
                wz = jnp.where(self.lane == self.right, 0.0, wzt)
                wxm = wx.get(d - 1)
                s = ((wx[d] if wxm is None else wx[d] + wxm) + (wy + wym)) + (wzt + wzm)
                e = self.change(u, d, j, wx[d], wxm, wy, wym, wz, s, inflow if d == 0 else None)
                finish(start + d, j, wx[d], wy, wz, s, e, flux[d] - flux[d - 1])

    def clear_rows(self, E, Wy, first, count):
        row = jnp.zeros((count, 1, self.cells[2]), jnp.float32)

        def clear(ref, r):
            at = r // self.T
            ref[first : first + count, r % self.T, at : at + 1, :] = row

        @pl.when(self.no_low)
        def _():
            clear(E, self.rows - 1)
            clear(Wy, self.rows - 1)

        @pl.when(self.no_high)
        def _():
            clear(E, self.cells[1])
            clear(Wy, self.cells[1] - 1)

    def sweep(self, loads, start, count, finish, boxes):
        le, lz, lwx, lwy, lwz, ls = loads
        e, z, wxs, wys = (self.reader(load, start) for load in (le, lz, lwx, lwy))
        for j in range(self.T):
            wanted = {d + o for d in range(count) if boxes[d] for o in (-1, 0, 1)}
            sums = {d: z(d, j) + (z(d, j + 1) + z(d, j - 1)) for d in sorted(wanted)}
            for d in range(count):
                i = start + d
                weights = (wxs(d, j), wxs(d - 1, j), wys(d, j), wys(d, j - 1), lwz(i, j), ls(i, j))
                em = self.change(e, d, j, *weights)
                zm = self.change(z, d, j, *weights)
                q = None
                if boxes[d]:
                    xs = sums[d - 1] + sums[d] + sums[d + 1]
                    xs = xs + (self.inner_up(xs) + self.inner_down(xs))
                    q = xs * (1.0 / 27.0) - z(d, j)
                finish(i, j, e(d, j), em, z(d, j), zm, q)

    def results(self, OI, OS, o, j, total, z):
        OI[o, pl.ds(j, 8, stride=self.T), :] = total * (-1.0 / (step_size * step_size))
        OS[o, pl.ds(j, 8, stride=self.T), :] = z * (1.0 / step_size)

    def leave(self, first, OI, OS, ind, sens, sems, p):
        pair = pl.ds(first, 2)
        return [
            pltpu.make_async_copy(source.at[pair, pl.ds(0, self.cells[1]), :], target.at[pair], sems.at[k, p])
            for k, (source, target) in enumerate(((OI, ind), (OS, sens)))
        ]


KEPT = (("EA", 5, 4), ("ZA", 5, 4), ("EB", 6, 2), ("ZB", 6, 2), ("Wx", 4, 4), ("Wy", 5, 3), ("Wz", 5, 3),
        ("S", 5, 3), ("M0", 6, 2), ("Q3", 6, 2), ("AC", 7, 1))
KEPT_PLANES = sum(count for _, _, count in KEPT)


def turns(count, body, together=3):
    full = count // together

    def turn(p, _):
        for d in range(together):
            body(together * p + d)
        return 0

    lax.fori_loop(0, full, turn, 0)
    for p in range(full * together, count):
        body(p)


def tiler(ref):
    return lambda i, j: ref[i, j]


def inner_kernel(initial, material, goal, table, from_low, from_high, near_a, near_b, ind, sens, edge, kept,
                 U, K, G, Wx, Wy, Wz, S, EA, EB, ZA, ZB, M0, Q3, AC, OI, OS, sems):
    cells_x, cells_y, cells_z = initial.shape
    H = HALO
    steps = Steps(cells_x, cells_y, cells_z)
    odd = steps.odd
    planes = cells_x + 2 * H
    low_half = lax.broadcasted_iota(jnp.int32, (8, cells_z), 0) < H
    near = Halves(near_a, near_b)
    side, step = odd * (planes - 1), 1 - 2 * odd

    def place(natural):
        return side + step * natural

    def own(p, _):
        ones = goal_tiles(p, cells_x, from_low, from_high, low_half)
        for d in range(2):
            i = 2 * p + d
            f = place(H + i)
            U[f, 0:cells_y, :] = initial[i]
            K[f, 0:cells_y, :] = gather_rows(table[0:1], material[i])
            G[f + 1 - odd, 0:cells_y, :] = goal[i].astype(jnp.float32)
            U[f, cells_y:, :], K[f, cells_y:, :] = halo_tiles(i, cells_x, from_low, from_high, low_half)
            G[f + 1 - odd, cells_y:, :] = ones[d]
        return 0

    lax.fori_loop(0, cells_x // 2, own, 0)
    for i in range(H):
        f = (1 - odd) * (H + cells_x + i) + odd * (planes - 1 - i)
        U[f] = near[i]
        K[f] = near[H + i]
        G[f + 1 - odd] = near[2 * H + i]
    for d in range(2):
        edge[d] = U[H + d]
        edge[2 + d] = K[H + d]
        edge[4 + d] = G[H + d + 1 - odd]

    def first_goal(i, j):
        return G[i + 1, pl.ds(j, 8, stride=steps.T), :]

    def begin(i, j, wx, wy, wz, s, e, z):
        Wx[i, j], Wy[i, j], Wz[i, j], S[i, j], EA[i, j], ZA[i, j] = wx, wy, wz, s, e, z

    def prelude(p):
        steps.prelude((steps.rower(K), steps.rower(U), first_goal), H + 1 + 2 * p, 2, begin)

    turns((planes - 2 - H) // 2, prelude)
    for j in range(steps.T):
        k = steps.rower(K)
        Wx[H, j] = k(H, j) + k(H + 1, j)
    steps.clear_rows(EA, Wy, H + 1, planes - 2 - H)

    def store_a(i, j, e, em, z, zm, q):
        EB[i, j] = e + em
        ZB[i, j] = z + zm
        if q is not None:
            M0[i - H, j] = em
            Q3[i - H, j] = q

    def store_b(i, j, e, em, z, zm, q):
        EA[i, j] = e + em
        ZA[i, j] = z + zm
        if q is not None:
            AC[i - H, j] = em * q

    def store_c(i, j, e, em, z, zm, q):
        o = i - H
        total = AC[o, j] + em * Q3[o, j] + M0[o, j] * q
        steps.results(OI, OS, place(i) - H, j, total, z + zm)

    weights = tuple(tiler(ref) for ref in (Wx, Wy, Wz, S))

    def sweep(E, Z, start, finish, boxes):
        steps.sweep((tiler(E), tiler(Z)) + weights, start, len(boxes), finish, boxes)

    def many(E, Z, start, pairs, finish):
        turns(pairs, lambda p: sweep(E, Z, start + 2 * p, finish, (True, True)))

    top = H + cells_x
    many(EA, ZA, H + 2, (cells_x - 2) // 2, store_a)
    sweep(EA, ZA, top, store_a, (False, False))
    many(EB, ZB, H + 3, (cells_x - 4) // 2, store_b)
    sweep(EB, ZB, top - 1, store_b, (True, False))

    def leave(p):
        f = H + 4 + 2 * p
        return steps.leave((1 - odd) * (f - H) + odd * (top - 2 - f), OI, OS, ind, sens, sems, p)

    def last(p):
        sweep(EA, ZA, H + 4 + 2 * p, store_c, (True, True))
        for move in leave(p):
            move.start()

    turns((cells_x - 4) // 2, last)
    refs = dict(EA=EA, ZA=ZA, EB=EB, ZB=ZB, Wx=Wx, Wy=Wy, Wz=Wz, S=S, M0=M0, Q3=Q3, AC=AC)
    at = 0
    for name, first, count in KEPT:
        shift = H if name in ("M0", "Q3", "AC") else 0
        for d in range(count):
            kept[at + d] = refs[name][first - shift + d]
        at += count

    def settle(p, _):
        for move in leave(p):
            move.wait()
        return 0

    lax.fori_loop(0, (cells_x - 4) // 2, settle, 0)


def outer_kernel(far, far_corner, edge, kept, ind_in, sens_in, ind, sens,
                 U, K, G, FU, FG, Wx, Wy, Wz, S, EA, EB, EC, ZA, ZB, ZC, M0, Q3, AC, OI, OS, sems):
    cells_x, cells_y, cells_z = ind.shape
    H = HALO
    steps = Steps(cells_x, cells_y, cells_z)
    odd = steps.odd
    FU[0:cells_y, :] = far[3]
    FU[cells_y:, :] = jnp.zeros((8, cells_z), jnp.float32)
    FG[0:cells_y, :] = far[7]
    for f in range(1, H):
        U[f, 0:cells_y, :] = far[f - 1]
        K[f, 0:cells_y, :] = far[3 + f]
        G[f + 1, 0:cells_y, :] = far[7 + f]
    tiles = [far_corner[i] for i in range(7)]
    turned = {i: pltpu.roll(tiles[i], HALO, 0) for i in (0, 2, 5)}
    for ref, values in (
        (U, (turned[0], tiles[5], tiles[0])),
        (K, (turned[5], tiles[3], tiles[1])),
        (G, (tiles[6], tiles[4], tiles[2])),
    ):
        for f in range(1, H):
            ref[f + 1 if ref is G else f, cells_y:, :] = values[f - 1]
    FG[cells_y:, :] = turned[2]
    for d in range(2):
        U[H + d] = edge[d]
        K[H + d] = edge[2 + d]
        G[H + d + 1 - odd] = edge[4 + d]

    places, at = {}, 0
    for name, first, count in KEPT:
        places[name] = (first, at)
        at += count

    def mixed(ref, name, own_first, own_last):
        first, offset = places[name]

        def load(i, j):
            if own_first <= i <= own_last:
                return ref[i, j]
            return kept[offset + i - first, j]

        return load

    def first_goal(i, j):
        return G[i + 1, pl.ds(j, 8, stride=steps.T), :]

    def begin(i, j, wx, wy, wz, s, e, z):
        Wx[i, j], Wy[i, j], Wz[i, j], S[i, j], EA[i, j], ZA[i, j] = wx, wy, wz, s, e, z

    def fluxes(ref):
        return lambda j: ref[pl.ds(j, 8, stride=steps.T), :]

    fields = (steps.rower(K), steps.rower(U), first_goal)
    steps.prelude(fields, 1, 2, begin, (fluxes(FU), fluxes(FG)))
    steps.prelude(fields, 3, 2, begin)
    steps.clear_rows(EA, Wy, 1, H)

    @pl.when(steps.no_far)
    def _():
        plane = jnp.zeros((steps.T, 8, cells_z), jnp.float32)
        EA[H - 1] = plane
        ZA[H - 1] = plane
        Wx[H - 1] = plane

    weights = (mixed(Wx, "Wx", 1, H), mixed(Wy, "Wy", 1, H), mixed(Wz, "Wz", 1, H), mixed(S, "S", 1, H))

    def store_a(i, j, e, em, z, zm, q):
        EB[i, j] = e + em
        ZB[i, j] = z + zm
        if q is not None:
            M0[i, j] = em
            Q3[i, j] = q

    def store_b(i, j, e, em, z, zm, q):
        EC[i, j] = e + em
        ZC[i, j] = z + zm
        if q is not None:
            AC[i, j] = em * q

    top = H + cells_x
    m0, q3, ac = mixed(M0, "M0", H, H + 1), mixed(Q3, "Q3", H, H + 1), mixed(AC, "AC", H, H + 2)

    def store_c(i, j, e, em, z, zm, q):
        total = ac(i, j) + em * q3(i, j) + m0(i, j) * q
        steps.results(OI, OS, (1 - odd) * (i - H) + odd * (top - 1 - i), j, total, z + zm)

    first = (mixed(EA, "EA", 1, H), mixed(ZA, "ZA", 1, H)) + weights
    second = (mixed(EB, "EB", 2, H + 1), mixed(ZB, "ZB", 2, H + 1)) + weights
    third = (mixed(EC, "EA", 3, H + 2), mixed(ZC, "ZA", 3, H + 2)) + weights
    steps.sweep(first, 2, 2, store_a, (False, False))
    steps.sweep(first, 4, 2, store_a, (True, True))
    steps.sweep(second, 3, 2, store_b, (False, True))
    steps.sweep(second, 5, 2, store_b, (True, True))
    moves = []
    for p in range(2):
        f = H + 2 * p
        steps.sweep(third, f, 2, store_c, (True, True))
        moves += steps.leave((1 - odd) * (f - H) + odd * (top - 2 - f), OI, OS, ind, sens, sems, p)
        for move in moves[-2:]:
            move.start()
    for move in moves:
        move.wait()


def whole(memory=None):
    return pl.BlockSpec(memory_space=memory or pltpu.VMEM)


def exchange(up, down, axis):
    count = lax.axis_size(axis)
    forward = [(i, i + 1) for i in range(count - 1)]
    backward = [(b, a) for a, b in forward]
    return lax.ppermute(up, axis, forward), lax.ppermute(down, axis, backward)


def swap(pairs):
    return [(a, b) for a, b in pairs] + [(b, a) for a, b in pairs]


def per_device(initial, material, goal_faces, conductivity):
    cells_x, cells_y, cells_z = initial.shape
    f32 = jnp.float32
    params = pltpu.CompilerParams(vmem_limit_bytes=LIMIT)
    small = pltpu.CompilerParams(vmem_limit_bytes=LIMIT // 4)
    shape = jax.ShapeDtypeStruct
    hbm, vmem = whole(pltpu.HBM), whole()
    rows = cells_y + 8
    planes = cells_x + 2 * HALO
    send = shape((cells_x + cells_x // 2, 8, cells_z), f32)
    block = shape(initial.shape, f32)
    count = lax.axis_size("gx")
    far_pairs = [(i, i + 1) for i in range(1, count - 1, 2)]
    near_pairs = [(i, i + 1) for i in range(0, count, 2)]

    here = [pltpu.with_memory_space_constraint(x, pltpu.HBM) for x in (initial, material, goal_faces, conductivity)]
    ends = (2, cells_x, 8, cells_z)
    up, down, table = pl.pallas_call(
        edge_kernel,
        out_shape=(send, send, shape((8, cells_z), f32)),
        in_specs=[hbm] * 4,
        out_specs=(vmem, vmem, vmem),
        scratch_shapes=[
            pltpu.VMEM(ends, f32),
            pltpu.VMEM(ends, jnp.int32),
            pltpu.VMEM(ends, jnp.int32),
            pltpu.SMEM(conductivity.shape, f32),
            pltpu.SemaphoreType.DMA((7,)),
        ],
        compiler_params=small,
        name="edges",
    )(*here)
    from_low, from_high = exchange(up, down, "gy")
    far = pl.pallas_call(
        far_kernel,
        out_shape=shape((3 * HALO - 1, cells_y, cells_z), f32),
        in_specs=[vmem] * 4 + [whole(pl.ANY)],
        out_specs=vmem,
        compiler_params=small,
        name="far",
    )(initial, material, goal_faces, table, up)
    far_sent = far
    far = lax.ppermute(far, "gx", swap(far_pairs))
    part = shape((3 * HALO // 2, rows, cells_z), f32)
    near_a, near_b, far_corner = pl.pallas_call(
        near_kernel,
        out_shape=(part, part, shape((7, 8, cells_z), f32)),
        in_specs=[vmem] * 6 + [whole(pl.ANY)],
        out_specs=(vmem,) * 3,
        compiler_params=small,
        cost_estimate=pl.CostEstimate(flops=10**9, bytes_accessed=1000, transcendentals=0),
        name="near",
    )(initial, material, goal_faces, table, from_low, from_high, far_sent)
    near_a = lax.ppermute(near_a, "gx", swap(near_pairs))
    near_b = lax.ppermute(near_b, "gx", swap(near_pairs))
    far_corner = lax.ppermute(far_corner, "gx", swap(far_pairs))

    def tiles(count):
        return pltpu.VMEM((count, rows // 8, 8, cells_z), f32)

    def natural(count):
        return pltpu.VMEM((count, rows, cells_z), f32)

    ind, sens, edge, kept = pl.pallas_call(
        inner_kernel,
        out_shape=(block, block, shape((6, rows, cells_z), f32), shape((KEPT_PLANES, rows // 8, 8, cells_z), f32)),
        in_specs=[vmem] * 8,
        out_specs=(hbm, hbm, vmem, vmem),
        scratch_shapes=[natural(planes), natural(planes), natural(planes + 1)]
        + [tiles(planes)] * 8 + [tiles(cells_x)] * 3 + [natural(cells_x)] * 2
        + [pltpu.SemaphoreType.DMA((2, (cells_x - 4) // 2))],
        compiler_params=params,
        cost_estimate=pl.CostEstimate(flops=1000, bytes_accessed=1000, transcendentals=0),
        name="inner",
    )(initial, material, goal_faces, table, from_low, from_high, near_a, near_b)
    return pl.pallas_call(
        outer_kernel,
        out_shape=(block, block),
        in_specs=[vmem] * 4 + [hbm, hbm],
        out_specs=(hbm, hbm),
        scratch_shapes=[natural(HALO + 2), natural(HALO + 2), natural(HALO + 3)]
        + [pltpu.VMEM((rows, cells_z), f32)] * 2 + [tiles(2 * HALO)] * 13 + [natural(cells_x)] * 2 + [pltpu.SemaphoreType.DMA((2, 2))],
        input_output_aliases={4: 0, 5: 1},
        compiler_params=small,
        name="outer",
    )(far, far_corner, edge, kept, ind, sens)


def solution(mesh):
    placed = (P("gx", "gy", None), P("gx", "gy", None), P("gx", "gy", None), P())
    return jax.shard_map(
        per_device,
        mesh=mesh,
        in_specs=placed,
        out_specs=(P("gx", "gy", None), P("gx", "gy", None)),
        check_vma=False,
    )
```

```python
import functools

import jax
import jax.numpy as jnp
from jax import lax
from jax.experimental import pallas as pl
from jax.experimental.pallas import tpu as pltpu
from jax.sharding import PartitionSpec as P

step_size = 0.075
HALO = 4
LIMIT = 40 * 1024 * 1024


def lanes_of(shape):
    return lax.broadcasted_iota(jnp.int32, shape, len(shape) - 1)


def half_weights(cond, lanes):
    lane = lanes_of((1, lanes))
    table = jnp.zeros((1, lanes), jnp.float32)
    for which in range(cond.shape[0]):
        table = jnp.where(lane == which, cond[which] * (0.5 * step_size), table)
    return table


def gather_rows(table, index):
    return jnp.take_along_axis(jnp.broadcast_to(table, index.shape), index, axis=1, mode="promise_in_bounds")


def edge_kernel(initial, material, goal, cond, up, down, shared, u, ids, flags, values, sems):
    cells_x, cells_y, cells_z = initial.shape
    moves = [pltpu.make_async_copy(cond, values, sems.at[6])]
    for end, first in enumerate((0, cells_y - 8)):
        for k, (source, target) in enumerate(((material, ids), (initial, u), (goal, flags))):
            moves.append(pltpu.make_async_copy(
                source.at[:, pl.ds(first, 8), :], target.at[end], sems.at[3 * end + k]))
    for move in moves:
        move.start()
    low_half = lax.broadcasted_iota(jnp.int32, (8, cells_z), 0) < HALO
    moves[0].wait()
    table = half_weights(values, cells_z)
    shared[...] = jnp.broadcast_to(table, shared.shape)
    for move in moves[1:]:
        move.wait()
    for i in range(cells_x):
        k_low = pltpu.roll(gather_rows(table, ids[0, i]), HALO, 0)
        k_high = pltpu.roll(gather_rows(table, ids[1, i]), HALO, 0)
        up[i] = jnp.where(low_half, k_high, u[1, i])
        down[i] = jnp.where(low_half, u[0, i], k_low)
    for p in range(cells_x // 2):
        one, two = flags[1, 2 * p], pltpu.roll(flags[1, 2 * p + 1], HALO, 0)
        up[cells_x + p] = jnp.where(low_half, two, one).astype(jnp.float32)
        one, two = flags[0, 2 * p], pltpu.roll(flags[0, 2 * p + 1], HALO, 0)
        down[cells_x + p] = jnp.where(low_half, one, two).astype(jnp.float32)


def face_planes(send, start, u, material, goal, table):
    cells_y = u.shape[1]
    for i in range(HALO):
        send[i, 0:cells_y, :] = u[start + i]
        send[HALO + i, 0:cells_y, :] = gather_rows(table, material[start + i])
        send[2 * HALO + i, 0:cells_y, :] = goal[start + i].astype(jnp.float32)


def far_order(odd, cells_x):
    last = cells_x - HALO
    return (
        lambda f: odd * (last + f) + (1 - odd) * (HALO - 1 - f),
        lambda f: odd * (last + f) + (1 - odd) * max(HALO - 2 - f, 0),
    )


def far_kernel(u, material, goal, table, up, far):
    plane, cell = far_order(lax.axis_index("gx") % 2, u.shape[0])
    kappa = [gather_rows(table[0:1], material[plane(f)]) for f in range(HALO)]
    face = kappa[0] + kappa[1]
    far[3] = face * (u[plane(0)] - u[plane(1)])
    far[7] = face * goal[cell(0)].astype(jnp.float32)
    for f in range(1, HALO):
        far[f - 1] = u[plane(f)]
        far[3 + f] = kappa[f]
        far[7 + f] = goal[cell(f)].astype(jnp.float32)


def halo_tiles(plane, cells_x, from_low, from_high, low_half):
    below, above = from_low[plane], from_high[plane]
    u = jnp.where(low_half, above, below)
    k = pltpu.roll(jnp.where(low_half, below, above), HALO, 0)
    return u, k


def goal_tiles(pair, cells_x, from_low, from_high, low_half):
    below, above = from_low[cells_x + pair], from_high[cells_x + pair]
    one = jnp.where(low_half, above, below)
    two = pltpu.roll(jnp.where(low_half, below, above), HALO, 0)
    return one, two


def near_kernel(u, material, goal, table, from_low, from_high, far, near_a, near_b, far_corner):
    cells_x, cells_y, cells_z = u.shape
    low_half = lax.broadcasted_iota(jnp.int32, (8, cells_z), 0) < HALO
    odd = lax.axis_index("gx") % 2
    last = cells_x - HALO
    near = Halves(near_a, near_b)
    face_planes(near, (1 - odd) * last, u, material, goal, table[0:1])

    def all_tiles(start):
        us, ks, gs = [], [], []
        for i in range(HALO):
            hu, hk = halo_tiles(start + i, cells_x, from_low, from_high, low_half)
            us.append(hu)
            ks.append(hk)
        for i in range(0, HALO, 2):
            gs += goal_tiles(start // 2 + i // 2, cells_x, from_low, from_high, low_half)
        return us, ks, gs

    for field, tiles in enumerate(all_tiles((1 - odd) * last)):
        for i in range(HALO):
            near[field * HALO + i, pl.ds(cells_y, 8), :] = tiles[i]

    us, ks, gs = all_tiles(odd * last)
    is_odd = jnp.broadcast_to(odd == 1, low_half.shape)
    us, ks = [[jnp.where(is_odd, t[f], t[HALO - 1 - f]) for f in range(HALO)] for t in (us, ks)]
    gs = [jnp.where(is_odd, gs[f], gs[max(HALO - 2 - f, 0)]) for f in range(HALO)]
    flux = gs[0] * (ks[0] + ks[1])
    sub = lax.broadcasted_iota(jnp.int32, low_half.shape, 0)
    two, four = (sub == 3) | (sub == 4), (sub >= 2) & (sub <= 5)
    far_corner[0] = jnp.where(two, pltpu.roll(us[1], HALO, 0), us[3])
    far_corner[1] = ks[3]
    far_corner[2] = jnp.where(two, pltpu.roll(flux, HALO, 0), gs[3])
    far_corner[3] = ks[2]
    far_corner[4] = gs[2]
    far_corner[5] = jnp.where(four, pltpu.roll(ks[1], HALO, 0), us[2])
    far_corner[6] = gs[1]


class Halves:
    def __init__(self, *parts):
        self.parts, self.size = parts, parts[0].shape[0]

    def at_plane(self, index):
        plane, *rest = index if isinstance(index, tuple) else (index,)
        return self.parts[plane // self.size], (plane % self.size, *rest)

    def __getitem__(self, index):
        ref, inside = self.at_plane(index)
        return ref[inside]

    def __setitem__(self, index, value):
        ref, inside = self.at_plane(index)
        ref[inside] = value


class Steps:
    def __init__(self, cells_x, cells_y, cells_z):
        self.rows = cells_y + 8
        self.cells = (cells_x, cells_y, cells_z)
        self.T = self.rows // 8
        self.right = cells_z - 1
        self.lane = lanes_of((8, cells_z))
        gx, gy = lax.axis_index("gx"), lax.axis_index("gy")
        self.odd = gx % 2
        self.sign = (1 - 2 * self.odd).astype(jnp.float32)
        self.no_far = (gx == 0) | (gx == lax.axis_size("gx") - 1)
        self.no_low, self.no_high = gy == 0, gy == lax.axis_size("gy") - 1

    def rower(self, ref):
        return lambda i, j: ref[i, pl.ds(j, 8, stride=self.T), :]

    def reader(self, load, start):
        seen = {}
        T = self.T

        def read(d, j):
            if (d, j) not in seen:
                if j == -1:
                    seen[d, j] = pltpu.roll(load(start + d, T - 1), 1, 0)
                elif j == T:
                    seen[d, j] = pltpu.roll(load(start + d, 0), 7, 0)
                else:
                    seen[d, j] = load(start + d, j)
            return seen[d, j]

        return read

    def up_lane(self, value):
        return pltpu.roll(value, self.right, 1)

    def down_lane(self, value):
        return pltpu.roll(value, 1, 1)

    def inner_up(self, value):
        return jnp.where(self.lane == self.right, 0.0, self.up_lane(value))

    def inner_down(self, value):
        return jnp.where(self.lane == 0, 0.0, self.down_lane(value))

    def change(self, v, d, j, wx, wxm, wy, wym, wz, s, inflow=None):
        c = v(d, j)
        below = wxm * v(d - 1, j) if inflow is None else inflow
        along = (wx * v(d + 1, j) + below) + (wy * v(d, j + 1) + wym * v(d, j - 1))
        return along + (wz * self.up_lane(c) + self.down_lane(wz * c)) - s * c

    def prelude(self, loads, start, count, finish, outermost=None):
        k, u, g = (self.reader(load, start) for load in loads)
        for j in range(self.T):
            low = -1 if outermost is None else 0
            wx = {d: k(d, j) + k(d + 1, j) for d in range(low, count)}
            flux = {d: (self.sign * g(d, j)) * wx[d] for d in range(low, count)}
            inflow = None
            if outermost is not None:
                inflow, flux[-1] = outermost[0](j), self.sign * outermost[1](j)
            for d in range(count):
                c = k(d, j)
                wy, wym = c + k(d, j + 1), c + k(d, j - 1)
                wzt, wzm = c + self.inner_up(c), c + self.inner_down(c)
                wz = jnp.where(self.lane == self.right, 0.0, wzt)
                wxm = wx.get(d - 1)
                s = ((wx[d] if wxm is None else wx[d] + wxm) + (wy + wym)) + (wzt + wzm)
                e = self.change(u, d, j, wx[d], wxm, wy, wym, wz, s, inflow if d == 0 else None)
                finish(start + d, j, wx[d], wy, wz, s, e, flux[d] - flux[d - 1])

    def clear_rows(self, E, Wy, first, count):
        row = jnp.zeros((count, 1, self.cells[2]), jnp.float32)

        def clear(ref, r):
            at = r // self.T
            ref[first : first + count, r % self.T, at : at + 1, :] = row

        @pl.when(self.no_low)
        def _():
            clear(E, self.rows - 1)
            clear(Wy, self.rows - 1)

        @pl.when(self.no_high)
        def _():
            clear(E, self.cells[1])
            clear(Wy, self.cells[1] - 1)

    def sweep(self, loads, start, count, finish, boxes):
        le, lz, lwx, lwy, lwz, ls = loads
        e, z, wxs, wys = (self.reader(load, start) for load in (le, lz, lwx, lwy))
        for j in range(self.T):
            wanted = {d + o for d in range(count) if boxes[d] for o in (-1, 0, 1)}
            sums = {d: z(d, j) + (z(d, j + 1) + z(d, j - 1)) for d in sorted(wanted)}
            for d in range(count):
                i = start + d
                weights = (wxs(d, j), wxs(d - 1, j), wys(d, j), wys(d, j - 1), lwz(i, j), ls(i, j))
                em = self.change(e, d, j, *weights)
                zm = self.change(z, d, j, *weights)
                q = None
                if boxes[d]:
                    xs = sums[d - 1] + sums[d] + sums[d + 1]
                    xs = xs + (self.inner_up(xs) + self.inner_down(xs))
                    q = xs * (1.0 / 27.0) - z(d, j)
                finish(i, j, e(d, j), em, z(d, j), zm, q)

    def results(self, OI, OS, o, j, total, z):
        OI[o, pl.ds(j, 8, stride=self.T), :] = total * (-1.0 / (step_size * step_size))
        OS[o, pl.ds(j, 8, stride=self.T), :] = z * (1.0 / step_size)

    def leave(self, first, OI, OS, ind, sens, sems, p):
        pair = pl.ds(first, 2)
        return [
            pltpu.make_async_copy(source.at[pair, pl.ds(0, self.cells[1]), :], target.at[pair], sems.at[k, p])
            for k, (source, target) in enumerate(((OI, ind), (OS, sens)))
        ]


KEPT = (("EA", 5, 4), ("ZA", 5, 4), ("EB", 6, 2), ("ZB", 6, 2), ("Wx", 4, 4), ("Wy", 5, 3), ("Wz", 5, 3),
        ("S", 5, 3), ("M0", 6, 2), ("Q3", 6, 2), ("AC", 7, 1))
KEPT_PLANES = sum(count for _, _, count in KEPT)


def turns(count, body, together=3):
    full = count // together

    def turn(p, _):
        for d in range(together):
            body(together * p + d)
        return 0

    lax.fori_loop(0, full, turn, 0)
    for p in range(full * together, count):
        body(p)


def tiler(ref):
    return lambda i, j: ref[i, j]


def inner_kernel(initial, material, goal, table, from_low, from_high, near_a, near_b, OI, OS, edge, kept,
                 U, K, G, Wx, Wy, Wz, S, EA, EB, ZA, ZB, M0, Q3, AC):
    cells_x, cells_y, cells_z = initial.shape
    H = HALO
    steps = Steps(cells_x, cells_y, cells_z)
    odd = steps.odd
    planes = cells_x + 2 * H
    low_half = lax.broadcasted_iota(jnp.int32, (8, cells_z), 0) < H
    near = Halves(near_a, near_b)
    side, step = odd * (planes - 1), 1 - 2 * odd

    def place(natural):
        return side + step * natural

    def own(p, _):
        ones = goal_tiles(p, cells_x, from_low, from_high, low_half)
        for d in range(2):
            i = 2 * p + d
            f = place(H + i)
            U[f, 0:cells_y, :] = initial[i]
            K[f, 0:cells_y, :] = gather_rows(table[0:1], material[i])
            G[f + 1 - odd, 0:cells_y, :] = goal[i].astype(jnp.float32)
            U[f, cells_y:, :], K[f, cells_y:, :] = halo_tiles(i, cells_x, from_low, from_high, low_half)
            G[f + 1 - odd, cells_y:, :] = ones[d]
        return 0

    lax.fori_loop(0, cells_x // 2, own, 0)
    for i in range(H):
        f = (1 - odd) * (H + cells_x + i) + odd * (planes - 1 - i)
        U[f] = near[i]
        K[f] = near[H + i]
        G[f + 1 - odd] = near[2 * H + i]
    for d in range(2):
        edge[d] = U[H + d]
        edge[2 + d] = K[H + d]
        edge[4 + d] = G[H + d + 1 - odd]

    def first_goal(i, j):
        return G[i + 1, pl.ds(j, 8, stride=steps.T), :]

    def begin(i, j, wx, wy, wz, s, e, z):
        Wx[i, j], Wy[i, j], Wz[i, j], S[i, j], EA[i, j], ZA[i, j] = wx, wy, wz, s, e, z

    def prelude(p):
        steps.prelude((steps.rower(K), steps.rower(U), first_goal), H + 1 + 2 * p, 2, begin)

    turns((planes - 2 - H) // 2, prelude)
    for j in range(steps.T):
        k = steps.rower(K)
        Wx[H, j] = k(H, j) + k(H + 1, j)
    steps.clear_rows(EA, Wy, H + 1, planes - 2 - H)

    def store_a(i, j, e, em, z, zm, q):
        EB[i, j] = e + em
        ZB[i, j] = z + zm
        if q is not None:
            M0[i - H, j] = em
            Q3[i - H, j] = q

    def store_b(i, j, e, em, z, zm, q):
        EA[i, j] = e + em
        ZA[i, j] = z + zm
        if q is not None:
            AC[i - H, j] = em * q

    def store_c(i, j, e, em, z, zm, q):
        o = i - H
        total = AC[o, j] + em * Q3[o, j] + M0[o, j] * q
        steps.results(OI, OS, place(i) - H, j, total, z + zm)

    weights = tuple(tiler(ref) for ref in (Wx, Wy, Wz, S))

    def sweep(E, Z, start, finish, boxes):
        steps.sweep((tiler(E), tiler(Z)) + weights, start, len(boxes), finish, boxes)

    def many(E, Z, start, pairs, finish):
        turns(pairs, lambda p: sweep(E, Z, start + 2 * p, finish, (True, True)))

    top = H + cells_x
    many(EA, ZA, H + 2, (cells_x - 2) // 2, store_a)
    sweep(EA, ZA, top, store_a, (False, False))
    many(EB, ZB, H + 3, (cells_x - 4) // 2, store_b)
    sweep(EB, ZB, top - 1, store_b, (True, False))

    turns((cells_x - 4) // 2, lambda p: sweep(EA, ZA, H + 4 + 2 * p, store_c, (True, True)))
    refs = dict(EA=EA, ZA=ZA, EB=EB, ZB=ZB, Wx=Wx, Wy=Wy, Wz=Wz, S=S, M0=M0, Q3=Q3, AC=AC)
    at = 0
    for name, first, count in KEPT:
        shift = H if name in ("M0", "Q3", "AC") else 0
        for d in range(count):
            kept[at + d] = refs[name][first - shift + d]
        at += count


def outer_kernel(far, far_corner, edge, kept, inner_ind, inner_sens, ind, sens,
                 U, K, G, FU, FG, Wx, Wy, Wz, S, EA, EB, EC, ZA, ZB, ZC, M0, Q3, AC, OI, OS, sems):
    cells_x, cells_y, cells_z = ind.shape
    H = HALO
    steps = Steps(cells_x, cells_y, cells_z)
    odd = steps.odd
    done = pl.ds((1 - odd) * H, cells_x - H)
    moves = [
        pltpu.make_async_copy(source.at[done, pl.ds(0, cells_y), :], target.at[done], sems.at[k, 2])
        for k, (source, target) in enumerate(((inner_ind, ind), (inner_sens, sens)))
    ]
    for move in moves:
        move.start()
    FU[0:cells_y, :] = far[3]
    FU[cells_y:, :] = jnp.zeros((8, cells_z), jnp.float32)
    FG[0:cells_y, :] = far[7]
    for f in range(1, H):
        U[f, 0:cells_y, :] = far[f - 1]
        K[f, 0:cells_y, :] = far[3 + f]
        G[f + 1, 0:cells_y, :] = far[7 + f]
    tiles = [far_corner[i] for i in range(7)]
    turned = {i: pltpu.roll(tiles[i], HALO, 0) for i in (0, 2, 5)}
    for ref, values in (
        (U, (turned[0], tiles[5], tiles[0])),
        (K, (turned[5], tiles[3], tiles[1])),
        (G, (tiles[6], tiles[4], tiles[2])),
    ):
        for f in range(1, H):
            ref[f + 1 if ref is G else f, cells_y:, :] = values[f - 1]
    FG[cells_y:, :] = turned[2]
    for d in range(2):
        U[H + d] = edge[d]
        K[H + d] = edge[2 + d]
        G[H + d + 1 - odd] = edge[4 + d]

    places, at = {}, 0
    for name, first, count in KEPT:
        places[name] = (first, at)
        at += count

    def mixed(ref, name, own_first, own_last):
        first, offset = places[name]

        def load(i, j):
            if own_first <= i <= own_last:
                return ref[i, j]
            return kept[offset + i - first, j]

        return load

    def first_goal(i, j):
        return G[i + 1, pl.ds(j, 8, stride=steps.T), :]

    sub = lax.broadcasted_iota(jnp.int32, (8, cells_z), 0)
    T = steps.T
    no_far, no_low, no_high = (
        jnp.broadcast_to(flag, sub.shape) for flag in (steps.no_far, steps.no_low, steps.no_high))

    def cleared(value, j, r, flag):
        if r % T != j:
            return value
        return jnp.where((sub == r // T) & flag, 0.0, value)

    def begin(i, j, wx, wy, wz, s, e, z):
        e = cleared(cleared(e, j, steps.rows - 1, no_low), j, cells_y, no_high)
        wy = cleared(cleared(wy, j, steps.rows - 1, no_low), j, cells_y - 1, no_high)
        if i == H - 1:
            wx, e, z = (jnp.where(no_far, 0.0, value) for value in (wx, e, z))
        Wx[i, j], Wy[i, j], Wz[i, j], S[i, j], EA[i, j], ZA[i, j] = wx, wy, wz, s, e, z

    def fluxes(ref):
        return lambda j: ref[pl.ds(j, 8, stride=steps.T), :]

    fields = (steps.rower(K), steps.rower(U), first_goal)
    steps.prelude(fields, 1, 2, begin, (fluxes(FU), fluxes(FG)))
    steps.prelude(fields, 3, 2, begin)
    weights = (mixed(Wx, "Wx", 1, H), mixed(Wy, "Wy", 1, H), mixed(Wz, "Wz", 1, H), mixed(S, "S", 1, H))

    def store_a(i, j, e, em, z, zm, q):
        EB[i, j] = e + em
        ZB[i, j] = z + zm
        if q is not None:
            M0[i, j] = em
            Q3[i, j] = q

    def store_b(i, j, e, em, z, zm, q):
        EC[i, j] = e + em
        ZC[i, j] = z + zm
        if q is not None:
            AC[i, j] = em * q

    top = H + cells_x
    m0, q3, ac = mixed(M0, "M0", H, H + 1), mixed(Q3, "Q3", H, H + 1), mixed(AC, "AC", H, H + 2)

    def store_c(i, j, e, em, z, zm, q):
        total = ac(i, j) + em * q3(i, j) + m0(i, j) * q
        steps.results(OI, OS, (1 - odd) * (i - H) + odd * (top - 1 - i), j, total, z + zm)

    first = (mixed(EA, "EA", 1, H), mixed(ZA, "ZA", 1, H)) + weights
    second = (mixed(EB, "EB", 2, H + 1), mixed(ZB, "ZB", 2, H + 1)) + weights
    third = (mixed(EC, "EA", 3, H + 2), mixed(ZC, "ZA", 3, H + 2)) + weights
    steps.sweep(first, 2, 2, store_a, (False, False))
    steps.sweep(first, 4, 2, store_a, (True, True))
    steps.sweep(second, 3, 2, store_b, (False, True))
    steps.sweep(second, 5, 2, store_b, (True, True))
    for p in range(2):
        f = H + 2 * p
        steps.sweep(third, f, 2, store_c, (True, True))
        moves += steps.leave((1 - odd) * (f - H) + odd * (top - 2 - f), OI, OS, ind, sens, sems, p)
        for move in moves[-2:]:
            move.start()
    for move in moves:
        move.wait()


def whole(memory=None):
    return pl.BlockSpec(memory_space=memory or pltpu.VMEM)


def exchange(up, down, axis):
    count = lax.axis_size(axis)
    forward = [(i, i + 1) for i in range(count - 1)]
    backward = [(b, a) for a, b in forward]
    return lax.ppermute(up, axis, forward), lax.ppermute(down, axis, backward)


def swap(pairs):
    return [(a, b) for a, b in pairs] + [(b, a) for a, b in pairs]


def per_device(initial, material, goal_faces, conductivity):
    cells_x, cells_y, cells_z = initial.shape
    f32 = jnp.float32
    params = pltpu.CompilerParams(vmem_limit_bytes=LIMIT)
    small = pltpu.CompilerParams(vmem_limit_bytes=LIMIT // 4)
    shape = jax.ShapeDtypeStruct
    hbm, vmem = whole(pltpu.HBM), whole()
    rows = cells_y + 8
    planes = cells_x + 2 * HALO
    send = shape((cells_x + cells_x // 2, 8, cells_z), f32)
    block = shape(initial.shape, f32)
    count = lax.axis_size("gx")
    far_pairs = [(i, i + 1) for i in range(1, count - 1, 2)]
    near_pairs = [(i, i + 1) for i in range(0, count, 2)]

    here = [pltpu.with_memory_space_constraint(x, pltpu.HBM) for x in (initial, material, goal_faces, conductivity)]
    ends = (2, cells_x, 8, cells_z)
    up, down, table = pl.pallas_call(
        edge_kernel,
        out_shape=(send, send, shape((8, cells_z), f32)),
        in_specs=[hbm] * 4,
        out_specs=(vmem, vmem, vmem),
        scratch_shapes=[
            pltpu.VMEM(ends, f32),
            pltpu.VMEM(ends, jnp.int32),
            pltpu.VMEM(ends, jnp.int32),
            pltpu.SMEM(conductivity.shape, f32),
            pltpu.SemaphoreType.DMA((7,)),
        ],
        compiler_params=small,
        name="edges",
    )(*here)
    from_low, from_high = exchange(up, down, "gy")
    far = pl.pallas_call(
        far_kernel,
        out_shape=shape((3 * HALO - 1, cells_y, cells_z), f32),
        in_specs=[vmem] * 4 + [whole(pl.ANY)],
        out_specs=vmem,
        compiler_params=small,
        name="far",
    )(initial, material, goal_faces, table, up)
    far_sent = far
    far = lax.ppermute(far, "gx", swap(far_pairs))
    part = shape((3 * HALO // 2, rows, cells_z), f32)
    near_a, near_b, far_corner = pl.pallas_call(
        near_kernel,
        out_shape=(part, part, shape((7, 8, cells_z), f32)),
        in_specs=[vmem] * 6 + [whole(pl.ANY)],
        out_specs=(vmem,) * 3,
        compiler_params=small,
        cost_estimate=pl.CostEstimate(flops=10**9, bytes_accessed=1000, transcendentals=0),
        name="near",
    )(initial, material, goal_faces, table, from_low, from_high, far_sent)
    near_a = lax.ppermute(near_a, "gx", swap(near_pairs))
    near_b = lax.ppermute(near_b, "gx", swap(near_pairs))
    far_corner = lax.ppermute(far_corner, "gx", swap(far_pairs))

    def tiles(count):
        return pltpu.VMEM((count, rows // 8, 8, cells_z), f32)

    def natural(count):
        return pltpu.VMEM((count, rows, cells_z), f32)

    wide_block = shape((cells_x, rows, cells_z), f32)
    ind, sens, edge, kept = pl.pallas_call(
        inner_kernel,
        out_shape=(wide_block, wide_block, shape((6, rows, cells_z), f32), shape((KEPT_PLANES, rows // 8, 8, cells_z), f32)),
        in_specs=[vmem] * 8,
        out_specs=(vmem,) * 4,
        scratch_shapes=[natural(planes), natural(planes), natural(planes + 1)]
        + [tiles(planes)] * 8 + [tiles(cells_x)] * 3,
        compiler_params=params,
        cost_estimate=pl.CostEstimate(flops=1000, bytes_accessed=1000, transcendentals=0),
        name="inner",
    )(initial, material, goal_faces, table, from_low, from_high, near_a, near_b)
    return pl.pallas_call(
        outer_kernel,
        out_shape=(block, block),
        in_specs=[vmem] * 6,
        out_specs=(hbm, hbm),
        scratch_shapes=[natural(HALO + 2), natural(HALO + 2), natural(HALO + 3)]
        + [pltpu.VMEM((rows, cells_z), f32)] * 2 + [tiles(2 * HALO)] * 13 + [natural(cells_x)] * 2 + [pltpu.SemaphoreType.DMA((2, 3))],
        compiler_params=small,
        name="outer",
    )(far, far_corner, edge, kept, ind, sens)


def solution(mesh):
    placed = (P("gx", "gy", None), P("gx", "gy", None), P("gx", "gy", None), P())
    return jax.shard_map(
        per_device,
        mesh=mesh,
        in_specs=placed,
        out_specs=(P("gx", "gy", None), P("gx", "gy", None)),
        check_vma=False,
    )
```

```python
import functools

import jax
import jax.numpy as jnp
from jax import lax
from jax.experimental import pallas as pl
from jax.experimental.pallas import tpu as pltpu
from jax.sharding import PartitionSpec as P

step_size = 0.075
HALO = 4
LIMIT = 40 * 1024 * 1024


def lanes_of(shape):
    return lax.broadcasted_iota(jnp.int32, shape, len(shape) - 1)


def half_weights(cond, lanes):
    lane = lanes_of((1, lanes))
    table = jnp.zeros((1, lanes), jnp.float32)
    for which in range(cond.shape[0]):
        table = jnp.where(lane == which, cond[which] * (0.5 * step_size), table)
    return table


def gather_rows(table, index):
    return jnp.take_along_axis(jnp.broadcast_to(table, index.shape), index, axis=1, mode="promise_in_bounds")


def edge_kernel(initial, material, goal, cond, up, down, shared, u, ids, flags, values, sems):
    cells_x, cells_y, cells_z = initial.shape
    moves = [pltpu.make_async_copy(cond, values, sems.at[6])]
    for end, first in enumerate((0, cells_y - 8)):
        for k, (source, target) in enumerate(((material, ids), (initial, u), (goal, flags))):
            moves.append(pltpu.make_async_copy(
                source.at[:, pl.ds(first, 8), :], target.at[end], sems.at[3 * end + k]))
    for move in moves:
        move.start()
    low_half = lax.broadcasted_iota(jnp.int32, (8, cells_z), 0) < HALO
    moves[0].wait()
    table = half_weights(values, cells_z)
    shared[...] = jnp.broadcast_to(table, shared.shape)
    for move in moves[1:]:
        move.wait()
    for i in range(cells_x):
        k_low = pltpu.roll(gather_rows(table, ids[0, i]), HALO, 0)
        k_high = pltpu.roll(gather_rows(table, ids[1, i]), HALO, 0)
        up[i] = jnp.where(low_half, k_high, u[1, i])
        down[i] = jnp.where(low_half, u[0, i], k_low)
    for p in range(cells_x // 2):
        one, two = flags[1, 2 * p], pltpu.roll(flags[1, 2 * p + 1], HALO, 0)
        up[cells_x + p] = jnp.where(low_half, two, one).astype(jnp.float32)
        one, two = flags[0, 2 * p], pltpu.roll(flags[0, 2 * p + 1], HALO, 0)
        down[cells_x + p] = jnp.where(low_half, one, two).astype(jnp.float32)


def face_planes(send, start, u, material, goal, table):
    cells_y = u.shape[1]
    for i in range(HALO):
        send[i, 0:cells_y, :] = u[start + i]
        send[HALO + i, 0:cells_y, :] = gather_rows(table, material[start + i])
        send[2 * HALO + i, 0:cells_y, :] = goal[start + i].astype(jnp.float32)


def far_order(odd, cells_x):
    last = cells_x - HALO
    return (
        lambda f: odd * (last + f) + (1 - odd) * (HALO - 1 - f),
        lambda f: odd * (last + f) + (1 - odd) * max(HALO - 2 - f, 0),
    )


def far_kernel(u, material, goal, table, up, far):
    plane, cell = far_order(lax.axis_index("gx") % 2, u.shape[0])
    kappa = [gather_rows(table[0:1], material[plane(f)]) for f in range(HALO)]
    face = kappa[0] + kappa[1]
    far[3] = face * (u[plane(0)] - u[plane(1)])
    far[7] = face * goal[cell(0)].astype(jnp.float32)
    for f in range(1, HALO):
        far[f - 1] = u[plane(f)]
        far[3 + f] = kappa[f]
        far[7 + f] = goal[cell(f)].astype(jnp.float32)


def halo_tiles(plane, cells_x, from_low, from_high, low_half):
    below, above = from_low[plane], from_high[plane]
    u = jnp.where(low_half, above, below)
    k = pltpu.roll(jnp.where(low_half, below, above), HALO, 0)
    return u, k


def goal_tiles(pair, cells_x, from_low, from_high, low_half):
    below, above = from_low[cells_x + pair], from_high[cells_x + pair]
    one = jnp.where(low_half, above, below)
    two = pltpu.roll(jnp.where(low_half, below, above), HALO, 0)
    return one, two


def near_kernel(u, material, goal, table, from_low, from_high, far, near_a, near_b, far_corner):
    cells_x, cells_y, cells_z = u.shape
    low_half = lax.broadcasted_iota(jnp.int32, (8, cells_z), 0) < HALO
    odd = lax.axis_index("gx") % 2
    last = cells_x - HALO
    near = Halves(near_a, near_b)
    face_planes(near, (1 - odd) * last, u, material, goal, table[0:1])

    def all_tiles(start):
        us, ks, gs = [], [], []
        for i in range(HALO):
            hu, hk = halo_tiles(start + i, cells_x, from_low, from_high, low_half)
            us.append(hu)
            ks.append(hk)
        for i in range(0, HALO, 2):
            gs += goal_tiles(start // 2 + i // 2, cells_x, from_low, from_high, low_half)
        return us, ks, gs

    for field, tiles in enumerate(all_tiles((1 - odd) * last)):
        for i in range(HALO):
            near[field * HALO + i, pl.ds(cells_y, 8), :] = tiles[i]

    us, ks, gs = all_tiles(odd * last)
    is_odd = jnp.broadcast_to(odd == 1, low_half.shape)
    us, ks = [[jnp.where(is_odd, t[f], t[HALO - 1 - f]) for f in range(HALO)] for t in (us, ks)]
    gs = [jnp.where(is_odd, gs[f], gs[max(HALO - 2 - f, 0)]) for f in range(HALO)]
    flux = gs[0] * (ks[0] + ks[1])
    sub = lax.broadcasted_iota(jnp.int32, low_half.shape, 0)
    two, four = (sub == 3) | (sub == 4), (sub >= 2) & (sub <= 5)
    far_corner[0] = jnp.where(two, pltpu.roll(us[1], HALO, 0), us[3])
    far_corner[1] = ks[3]
    far_corner[2] = jnp.where(two, pltpu.roll(flux, HALO, 0), gs[3])
    far_corner[3] = ks[2]
    far_corner[4] = gs[2]
    far_corner[5] = jnp.where(four, pltpu.roll(ks[1], HALO, 0), us[2])
    far_corner[6] = gs[1]


class Halves:
    def __init__(self, *parts):
        self.parts, self.size = parts, parts[0].shape[0]

    def at_plane(self, index):
        plane, *rest = index if isinstance(index, tuple) else (index,)
        return self.parts[plane // self.size], (plane % self.size, *rest)

    def __getitem__(self, index):
        ref, inside = self.at_plane(index)
        return ref[inside]

    def __setitem__(self, index, value):
        ref, inside = self.at_plane(index)
        ref[inside] = value


class Steps:
    def __init__(self, cells_x, cells_y, cells_z):
        self.rows = cells_y + 8
        self.cells = (cells_x, cells_y, cells_z)
        self.T = self.rows // 8
        self.right = cells_z - 1
        self.lane = lanes_of((8, cells_z))
        gx, gy = lax.axis_index("gx"), lax.axis_index("gy")
        self.odd = gx % 2
        self.sign = (1 - 2 * self.odd).astype(jnp.float32)
        self.no_far = (gx == 0) | (gx == lax.axis_size("gx") - 1)
        self.no_low, self.no_high = gy == 0, gy == lax.axis_size("gy") - 1

    def rower(self, ref):
        return lambda i, j: ref[i, pl.ds(j, 8, stride=self.T), :]

    def reader(self, load, start):
        seen = {}
        T = self.T

        def read(d, j):
            if (d, j) not in seen:
                if j == -1:
                    seen[d, j] = pltpu.roll(load(start + d, T - 1), 1, 0)
                elif j == T:
                    seen[d, j] = pltpu.roll(load(start + d, 0), 7, 0)
                else:
                    seen[d, j] = load(start + d, j)
            return seen[d, j]

        return read

    def up_lane(self, value):
        return pltpu.roll(value, self.right, 1)

    def down_lane(self, value):
        return pltpu.roll(value, 1, 1)

    def inner_up(self, value):
        return jnp.where(self.lane == self.right, 0.0, self.up_lane(value))

    def inner_down(self, value):
        return jnp.where(self.lane == 0, 0.0, self.down_lane(value))

    def change(self, v, d, j, wx, wxm, wy, wym, wz, s, inflow=None):
        c = v(d, j)
        below = wxm * v(d - 1, j) if inflow is None else inflow
        along = (wx * v(d + 1, j) + below) + (wy * v(d, j + 1) + wym * v(d, j - 1))
        return along + (wz * self.up_lane(c) + self.down_lane(wz * c)) - s * c

    def prelude(self, loads, start, count, finish, outermost=None):
        k, u, g = (self.reader(load, start) for load in loads)
        for j in range(self.T):
            low = -1 if outermost is None else 0
            wx = {d: k(d, j) + k(d + 1, j) for d in range(low, count)}
            flux = {d: (self.sign * g(d, j)) * wx[d] for d in range(low, count)}
            inflow = None
            if outermost is not None:
                inflow, flux[-1] = outermost[0](j), self.sign * outermost[1](j)
            for d in range(count):
                c = k(d, j)
                wy, wym = c + k(d, j + 1), c + k(d, j - 1)
                wzt, wzm = c + self.inner_up(c), c + self.inner_down(c)
                wz = jnp.where(self.lane == self.right, 0.0, wzt)
                wxm = wx.get(d - 1)
                s = ((wx[d] if wxm is None else wx[d] + wxm) + (wy + wym)) + (wzt + wzm)
                e = self.change(u, d, j, wx[d], wxm, wy, wym, wz, s, inflow if d == 0 else None)
                finish(start + d, j, wx[d], wy, wz, s, e, flux[d] - flux[d - 1])

    def clear_rows(self, E, Wy, first, count):
        row = jnp.zeros((count, 1, self.cells[2]), jnp.float32)

        def clear(ref, r):
            at = r // self.T
            ref[first : first + count, r % self.T, at : at + 1, :] = row

        @pl.when(self.no_low)
        def _():
            clear(E, self.rows - 1)
            clear(Wy, self.rows - 1)

        @pl.when(self.no_high)
        def _():
            clear(E, self.cells[1])
            clear(Wy, self.cells[1] - 1)

    def sweep(self, loads, start, count, finish, boxes):
        le, lz, lwx, lwy, lwz, ls = loads
        e, z, wxs, wys = (self.reader(load, start) for load in (le, lz, lwx, lwy))
        for j in range(self.T):
            wanted = {d + o for d in range(count) if boxes[d] for o in (-1, 0, 1)}
            sums = {d: z(d, j) + (z(d, j + 1) + z(d, j - 1)) for d in sorted(wanted)}
            for d in range(count):
                i = start + d
                weights = (wxs(d, j), wxs(d - 1, j), wys(d, j), wys(d, j - 1), lwz(i, j), ls(i, j))
                em = self.change(e, d, j, *weights)
                zm = self.change(z, d, j, *weights)
                q = None
                if boxes[d]:
                    xs = sums[d - 1] + sums[d] + sums[d + 1]
                    xs = xs + (self.inner_up(xs) + self.inner_down(xs))
                    q = xs * (1.0 / 27.0) - z(d, j)
                finish(i, j, e(d, j), em, z(d, j), zm, q)

    def results(self, OI, OS, o, j, total, z):
        OI[o, pl.ds(j, 8, stride=self.T), :] = total * (-1.0 / (step_size * step_size))
        OS[o, pl.ds(j, 8, stride=self.T), :] = z * (1.0 / step_size)

    def leave(self, first, OI, OS, ind, sens, sems, p):
        pair = pl.ds(first, 2)
        return [
            pltpu.make_async_copy(source.at[pair, pl.ds(0, self.cells[1]), :], target.at[pair], sems.at[k, p])
            for k, (source, target) in enumerate(((OI, ind), (OS, sens)))
        ]


KEPT = (("EA", 5, 4), ("ZA", 5, 4), ("EB", 6, 2), ("ZB", 6, 2), ("Wx", 4, 4), ("Wy", 5, 3), ("Wz", 5, 3),
        ("S", 5, 3), ("M0", 6, 2), ("Q3", 6, 2), ("AC", 7, 1))
KEPT_PLANES = sum(count for _, _, count in KEPT)


def turns(count, body, together=9):
    full = count // together

    def turn(p, _):
        for d in range(together):
            body(together * p + d)
        return 0

    lax.fori_loop(0, full, turn, 0)
    for p in range(full * together, count):
        body(p)


def tiler(ref):
    return lambda i, j: ref[i, j]


def inner_kernel(initial, material, goal, table, from_low, from_high, near_a, near_b, OI, OS, edge, kept,
                 U, K, G, Wx, Wy, Wz, S, EA, EB, ZA, ZB, M0, Q3, AC):
    cells_x, cells_y, cells_z = initial.shape
    H = HALO
    steps = Steps(cells_x, cells_y, cells_z)
    odd = steps.odd
    planes = cells_x + 2 * H
    low_half = lax.broadcasted_iota(jnp.int32, (8, cells_z), 0) < H
    near = Halves(near_a, near_b)
    side, step = odd * (planes - 1), 1 - 2 * odd

    def place(natural):
        return side + step * natural

    def own(p, _):
        ones = goal_tiles(p, cells_x, from_low, from_high, low_half)
        for d in range(2):
            i = 2 * p + d
            f = place(H + i)
            U[f, 0:cells_y, :] = initial[i]
            K[f, 0:cells_y, :] = gather_rows(table[0:1], material[i])
            G[f + 1 - odd, 0:cells_y, :] = goal[i].astype(jnp.float32)
            U[f, cells_y:, :], K[f, cells_y:, :] = halo_tiles(i, cells_x, from_low, from_high, low_half)
            G[f + 1 - odd, cells_y:, :] = ones[d]
        return 0

    lax.fori_loop(0, cells_x // 2, own, 0)
    for i in range(H):
        f = (1 - odd) * (H + cells_x + i) + odd * (planes - 1 - i)
        U[f] = near[i]
        K[f] = near[H + i]
        G[f + 1 - odd] = near[2 * H + i]
    for d in range(2):
        edge[d] = U[H + d]
        edge[2 + d] = K[H + d]
        edge[4 + d] = G[H + d + 1 - odd]

    def first_goal(i, j):
        return G[i + 1, pl.ds(j, 8, stride=steps.T), :]

    def begin(i, j, wx, wy, wz, s, e, z):
        Wx[i, j], Wy[i, j], Wz[i, j], S[i, j], EA[i, j], ZA[i, j] = wx, wy, wz, s, e, z

    def prelude(p):
        steps.prelude((steps.rower(K), steps.rower(U), first_goal), H + 1 + 2 * p, 2, begin)

    turns((planes - 2 - H) // 2, prelude)
    for j in range(steps.T):
        k = steps.rower(K)
        Wx[H, j] = k(H, j) + k(H + 1, j)
    steps.clear_rows(EA, Wy, H + 1, planes - 2 - H)

    def store_a(i, j, e, em, z, zm, q):
        EB[i, j] = e + em
        ZB[i, j] = z + zm
        if q is not None:
            M0[i - H, j] = em
            Q3[i - H, j] = q

    def store_b(i, j, e, em, z, zm, q):
        EA[i, j] = e + em
        ZA[i, j] = z + zm
        if q is not None:
            AC[i - H, j] = em * q

    def store_c(i, j, e, em, z, zm, q):
        o = i - H
        total = AC[o, j] + em * Q3[o, j] + M0[o, j] * q
        steps.results(OI, OS, place(i) - H, j, total, z + zm)

    weights = tuple(tiler(ref) for ref in (Wx, Wy, Wz, S))

    def sweep(E, Z, start, finish, boxes):
        steps.sweep((tiler(E), tiler(Z)) + weights, start, len(boxes), finish, boxes)

    def many(E, Z, start, pairs, finish):
        turns(pairs, lambda p: sweep(E, Z, start + 2 * p, finish, (True, True)))

    top = H + cells_x
    many(EA, ZA, H + 2, (cells_x - 2) // 2, store_a)
    sweep(EA, ZA, top, store_a, (False, False))
    many(EB, ZB, H + 3, (cells_x - 4) // 2, store_b)
    sweep(EB, ZB, top - 1, store_b, (True, False))

    turns((cells_x - 4) // 2, lambda p: sweep(EA, ZA, H + 4 + 2 * p, store_c, (True, True)))
    refs = dict(EA=EA, ZA=ZA, EB=EB, ZB=ZB, Wx=Wx, Wy=Wy, Wz=Wz, S=S, M0=M0, Q3=Q3, AC=AC)
    at = 0
    for name, first, count in KEPT:
        shift = H if name in ("M0", "Q3", "AC") else 0
        for d in range(count):
            kept[at + d] = refs[name][first - shift + d]
        at += count


def outer_kernel(far, far_corner, edge, kept, inner_ind, inner_sens, ind, sens,
                 U, K, G, FU, FG, Wx, Wy, Wz, S, EA, EB, EC, ZA, ZB, ZC, M0, Q3, AC, OI, OS, sems):
    cells_x, cells_y, cells_z = ind.shape
    H = HALO
    steps = Steps(cells_x, cells_y, cells_z)
    odd = steps.odd
    done = pl.ds((1 - odd) * H, cells_x - H)
    moves = [
        pltpu.make_async_copy(source.at[done, pl.ds(0, cells_y), :], target.at[done], sems.at[k, 2])
        for k, (source, target) in enumerate(((inner_ind, ind), (inner_sens, sens)))
    ]
    for move in moves:
        move.start()
    FU[0:cells_y, :] = far[3]
    FU[cells_y:, :] = jnp.zeros((8, cells_z), jnp.float32)
    FG[0:cells_y, :] = far[7]
    for f in range(1, H):
        U[f, 0:cells_y, :] = far[f - 1]
        K[f, 0:cells_y, :] = far[3 + f]
        G[f + 1, 0:cells_y, :] = far[7 + f]
    tiles = [far_corner[i] for i in range(7)]
    turned = {i: pltpu.roll(tiles[i], HALO, 0) for i in (0, 2, 5)}
    for ref, values in (
        (U, (turned[0], tiles[5], tiles[0])),
        (K, (turned[5], tiles[3], tiles[1])),
        (G, (tiles[6], tiles[4], tiles[2])),
    ):
        for f in range(1, H):
            ref[f + 1 if ref is G else f, cells_y:, :] = values[f - 1]
    FG[cells_y:, :] = turned[2]
    for d in range(2):
        U[H + d] = edge[d]
        K[H + d] = edge[2 + d]
        G[H + d + 1 - odd] = edge[4 + d]

    places, at = {}, 0
    for name, first, count in KEPT:
        places[name] = (first, at)
        at += count

    def mixed(ref, name, own_first, own_last):
        first, offset = places[name]

        def load(i, j):
            if own_first <= i <= own_last:
                return ref[i, j]
            return kept[offset + i - first, j]

        return load

    def first_goal(i, j):
        return G[i + 1, pl.ds(j, 8, stride=steps.T), :]

    sub = lax.broadcasted_iota(jnp.int32, (8, cells_z), 0)
    T = steps.T
    no_far, no_low, no_high = (
        jnp.broadcast_to(flag, sub.shape) for flag in (steps.no_far, steps.no_low, steps.no_high))

    def cleared(value, j, r, flag):
        if r % T != j:
            return value
        return jnp.where((sub == r // T) & flag, 0.0, value)

    def begin(i, j, wx, wy, wz, s, e, z):
        e = cleared(cleared(e, j, steps.rows - 1, no_low), j, cells_y, no_high)
        wy = cleared(cleared(wy, j, steps.rows - 1, no_low), j, cells_y - 1, no_high)
        if i == H - 1:
            wx, e, z = (jnp.where(no_far, 0.0, value) for value in (wx, e, z))
        Wx[i, j], Wy[i, j], Wz[i, j], S[i, j], EA[i, j], ZA[i, j] = wx, wy, wz, s, e, z

    def fluxes(ref):
        return lambda j: ref[pl.ds(j, 8, stride=steps.T), :]

    fields = (steps.rower(K), steps.rower(U), first_goal)
    steps.prelude(fields, 3, 2, begin)
    steps.prelude(fields, 1, 2, begin, (fluxes(FU), fluxes(FG)))
    weights = (mixed(Wx, "Wx", 1, H), mixed(Wy, "Wy", 1, H), mixed(Wz, "Wz", 1, H), mixed(S, "S", 1, H))

    def store_a(i, j, e, em, z, zm, q):
        EB[i, j] = e + em
        ZB[i, j] = z + zm
        if q is not None:
            M0[i, j] = em
            Q3[i, j] = q

    def store_b(i, j, e, em, z, zm, q):
        EC[i, j] = e + em
        ZC[i, j] = z + zm
        if q is not None:
            AC[i, j] = em * q

    top = H + cells_x
    m0, q3, ac = mixed(M0, "M0", H, H + 1), mixed(Q3, "Q3", H, H + 1), mixed(AC, "AC", H, H + 2)

    def store_c(i, j, e, em, z, zm, q):
        total = ac(i, j) + em * q3(i, j) + m0(i, j) * q
        steps.results(OI, OS, (1 - odd) * (i - H) + odd * (top - 1 - i), j, total, z + zm)

    first = (mixed(EA, "EA", 1, H), mixed(ZA, "ZA", 1, H)) + weights
    second = (mixed(EB, "EB", 2, H + 1), mixed(ZB, "ZB", 2, H + 1)) + weights
    third = (mixed(EC, "EA", 3, H + 2), mixed(ZC, "ZA", 3, H + 2)) + weights
    steps.sweep(first, 4, 2, store_a, (True, True))
    steps.sweep(first, 2, 2, store_a, (False, False))
    steps.sweep(second, 5, 2, store_b, (True, True))
    steps.sweep(second, 3, 2, store_b, (False, True))
    for p in (1, 0):
        f = H + 2 * p
        steps.sweep(third, f, 2, store_c, (True, True))
        moves += steps.leave((1 - odd) * (f - H) + odd * (top - 2 - f), OI, OS, ind, sens, sems, p)
        for move in moves[-2:]:
            move.start()
    for move in moves:
        move.wait()


def whole(memory=None):
    return pl.BlockSpec(memory_space=memory or pltpu.VMEM)


def exchange(up, down, axis):
    count = lax.axis_size(axis)
    forward = [(i, i + 1) for i in range(count - 1)]
    backward = [(b, a) for a, b in forward]
    return lax.ppermute(up, axis, forward), lax.ppermute(down, axis, backward)


def swap(pairs):
    return [(a, b) for a, b in pairs] + [(b, a) for a, b in pairs]


def per_device(initial, material, goal_faces, conductivity):
    cells_x, cells_y, cells_z = initial.shape
    f32 = jnp.float32
    params = pltpu.CompilerParams(vmem_limit_bytes=LIMIT)
    small = pltpu.CompilerParams(vmem_limit_bytes=LIMIT // 4)
    shape = jax.ShapeDtypeStruct
    hbm, vmem = whole(pltpu.HBM), whole()
    rows = cells_y + 8
    planes = cells_x + 2 * HALO
    send = shape((cells_x + cells_x // 2, 8, cells_z), f32)
    block = shape(initial.shape, f32)
    count = lax.axis_size("gx")
    far_pairs = [(i, i + 1) for i in range(1, count - 1, 2)]
    near_pairs = [(i, i + 1) for i in range(0, count, 2)]

    here = [pltpu.with_memory_space_constraint(x, pltpu.HBM) for x in (initial, material, goal_faces, conductivity)]
    ends = (2, cells_x, 8, cells_z)
    up, down, table = pl.pallas_call(
        edge_kernel,
        out_shape=(send, send, shape((8, cells_z), f32)),
        in_specs=[hbm] * 4,
        out_specs=(vmem, vmem, vmem),
        scratch_shapes=[
            pltpu.VMEM(ends, f32),
            pltpu.VMEM(ends, jnp.int32),
            pltpu.VMEM(ends, jnp.int32),
            pltpu.SMEM(conductivity.shape, f32),
            pltpu.SemaphoreType.DMA((7,)),
        ],
        compiler_params=small,
        name="edges",
    )(*here)
    from_low, from_high = exchange(up, down, "gy")
    far = pl.pallas_call(
        far_kernel,
        out_shape=shape((3 * HALO - 1, cells_y, cells_z), f32),
        in_specs=[vmem] * 4 + [whole(pl.ANY)],
        out_specs=vmem,
        compiler_params=small,
        name="far",
    )(initial, material, goal_faces, table, up)
    far_sent = far
    far = lax.ppermute(far, "gx", swap(far_pairs))
    part = shape((3 * HALO // 2, rows, cells_z), f32)
    near_a, near_b, far_corner = pl.pallas_call(
        near_kernel,
        out_shape=(part, part, shape((7, 8, cells_z), f32)),
        in_specs=[vmem] * 6 + [whole(pl.ANY)],
        out_specs=(vmem,) * 3,
        compiler_params=small,
        cost_estimate=pl.CostEstimate(flops=10**9, bytes_accessed=1000, transcendentals=0),
        name="near",
    )(initial, material, goal_faces, table, from_low, from_high, far_sent)
    near_a = lax.ppermute(near_a, "gx", swap(near_pairs))
    near_b = lax.ppermute(near_b, "gx", swap(near_pairs))
    far_corner = lax.ppermute(far_corner, "gx", swap(far_pairs))

    def tiles(count):
        return pltpu.VMEM((count, rows // 8, 8, cells_z), f32)

    def natural(count):
        return pltpu.VMEM((count, rows, cells_z), f32)

    wide_block = shape((cells_x, rows, cells_z), f32)
    ind, sens, edge, kept = pl.pallas_call(
        inner_kernel,
        out_shape=(wide_block, wide_block, shape((6, rows, cells_z), f32), shape((KEPT_PLANES, rows // 8, 8, cells_z), f32)),
        in_specs=[vmem] * 8,
        out_specs=(vmem,) * 4,
        scratch_shapes=[natural(planes), natural(planes), natural(planes + 1)]
        + [tiles(planes)] * 8 + [tiles(cells_x)] * 3,
        compiler_params=params,
        cost_estimate=pl.CostEstimate(flops=1000, bytes_accessed=1000, transcendentals=0),
        name="inner",
    )(initial, material, goal_faces, table, from_low, from_high, near_a, near_b)
    return pl.pallas_call(
        outer_kernel,
        out_shape=(block, block),
        in_specs=[vmem] * 6,
        out_specs=(hbm, hbm),
        scratch_shapes=[natural(HALO + 2), natural(HALO + 2), natural(HALO + 3)]
        + [pltpu.VMEM((rows, cells_z), f32)] * 2 + [tiles(2 * HALO)] * 13 + [natural(cells_x)] * 2 + [pltpu.SemaphoreType.DMA((2, 3))],
        compiler_params=small,
        name="outer",
    )(far, far_corner, edge, kept, ind, sens)


def solution(mesh):
    placed = (P("gx", "gy", None), P("gx", "gy", None), P("gx", "gy", None), P())
    return jax.shard_map(
        per_device,
        mesh=mesh,
        in_specs=placed,
        out_specs=(P("gx", "gy", None), P("gx", "gy", None)),
        check_vma=False,
    )
```

```python
import functools

import jax
import jax.numpy as jnp
from jax import lax
from jax.experimental import pallas as pl
from jax.experimental.pallas import tpu as pltpu
from jax.sharding import PartitionSpec as P

step_size = 0.075
HALO = 4
LIMIT = 40 * 1024 * 1024


def lanes_of(shape):
    return lax.broadcasted_iota(jnp.int32, shape, len(shape) - 1)


def half_weights(cond, lanes):
    lane = lanes_of((1, lanes))
    table = jnp.zeros((1, lanes), jnp.float32)
    for which in range(cond.shape[0]):
        table = jnp.where(lane == which, cond[which] * (0.5 * step_size), table)
    return table


def gather_rows(table, index):
    return jnp.take_along_axis(jnp.broadcast_to(table, index.shape), index, axis=1, mode="promise_in_bounds")


def edge_kernel(initial, material, goal, cond, first, second, shared, u, ids, flags, values, sems):
    cells_x, cells_y, cells_z = initial.shape
    moves = [pltpu.make_async_copy(cond, values, sems.at[6])]
    for end, row in enumerate((0, cells_y - 8)):
        for k, (source, target) in enumerate(((material, ids), (initial, u), (goal, flags))):
            moves.append(pltpu.make_async_copy(
                source.at[:, pl.ds(row, 8), :], target.at[end], sems.at[3 * end + k]))
    for move in moves:
        move.start()
    low_half = lax.broadcasted_iota(jnp.int32, (8, cells_z), 0) < HALO
    moves[0].wait()
    table = half_weights(values, cells_z)
    shared[...] = jnp.broadcast_to(table, shared.shape)
    for move in moves[1:]:
        move.wait()
    even = jnp.broadcast_to(lax.axis_index("gy") % 2 == 0, low_half.shape)

    def put(i, up, down):
        first[i] = jnp.where(even, up, down)
        second[i] = jnp.where(even, down, up)

    for i in range(cells_x):
        k_low = pltpu.roll(gather_rows(table, ids[0, i]), HALO, 0)
        k_high = pltpu.roll(gather_rows(table, ids[1, i]), HALO, 0)
        put(i, jnp.where(low_half, k_high, u[1, i]), jnp.where(low_half, u[0, i], k_low))
    for p in range(cells_x // 2):
        high_one, high_two = flags[1, 2 * p], pltpu.roll(flags[1, 2 * p + 1], HALO, 0)
        low_one, low_two = flags[0, 2 * p], pltpu.roll(flags[0, 2 * p + 1], HALO, 0)
        put(cells_x + p, jnp.where(low_half, high_two, high_one).astype(jnp.float32),
            jnp.where(low_half, low_one, low_two).astype(jnp.float32))


def face_planes(send, start, u, material, goal, table):
    cells_y = u.shape[1]
    for i in range(HALO):
        send[i, 0:cells_y, :] = u[start + i]
        send[HALO + i, 0:cells_y, :] = gather_rows(table, material[start + i])
        send[2 * HALO + i, 0:cells_y, :] = goal[start + i].astype(jnp.float32)


def far_order(odd, cells_x):
    last = cells_x - HALO
    return (
        lambda f: odd * (last + f) + (1 - odd) * (HALO - 1 - f),
        lambda f: odd * (last + f) + (1 - odd) * max(HALO - 2 - f, 0),
    )


def far_kernel(u, material, goal, table, sent, far):
    plane, cell = far_order(lax.axis_index("gx") % 2, u.shape[0])
    kappa = [gather_rows(table[0:1], material[plane(f)]) for f in range(HALO)]
    face = kappa[0] + kappa[1]
    far[3] = face * (u[plane(0)] - u[plane(1)])
    far[7] = face * goal[cell(0)].astype(jnp.float32)
    for f in range(1, HALO):
        far[f - 1] = u[plane(f)]
        far[3 + f] = kappa[f]
        far[7 + f] = goal[cell(f)].astype(jnp.float32)


def from_first(cells_z):
    low_half = lax.broadcasted_iota(jnp.int32, (8, cells_z), 0) < HALO
    even = jnp.broadcast_to(lax.axis_index("gy") % 2 == 0, low_half.shape)
    return low_half == even


def halo_tiles(plane, cells_x, first, second, chosen):
    one, two = first[plane], second[plane]
    return jnp.where(chosen, one, two), pltpu.roll(jnp.where(chosen, two, one), HALO, 0)


def goal_tiles(pair, cells_x, first, second, chosen):
    return halo_tiles(cells_x + pair, cells_x, first, second, chosen)


def near_kernel(u, material, goal, table, first, second, far, near_a, near_b, far_corner):
    cells_x, cells_y, cells_z = u.shape
    chosen = from_first(cells_z)
    odd = lax.axis_index("gx") % 2
    last = cells_x - HALO
    near = Halves(near_a, near_b)
    face_planes(near, (1 - odd) * last, u, material, goal, table[0:1])

    def all_tiles(start):
        us, ks, gs = [], [], []
        for i in range(HALO):
            hu, hk = halo_tiles(start + i, cells_x, first, second, chosen)
            us.append(hu)
            ks.append(hk)
        for i in range(0, HALO, 2):
            gs += goal_tiles(start // 2 + i // 2, cells_x, first, second, chosen)
        return us, ks, gs

    for field, tiles in enumerate(all_tiles((1 - odd) * last)):
        for i in range(HALO):
            near[field * HALO + i, pl.ds(cells_y, 8), :] = tiles[i]

    us, ks, gs = all_tiles(odd * last)
    is_odd = jnp.broadcast_to(odd == 1, chosen.shape)
    us, ks = [[jnp.where(is_odd, t[f], t[HALO - 1 - f]) for f in range(HALO)] for t in (us, ks)]
    gs = [jnp.where(is_odd, gs[f], gs[max(HALO - 2 - f, 0)]) for f in range(HALO)]
    flux = gs[0] * (ks[0] + ks[1])
    sub = lax.broadcasted_iota(jnp.int32, chosen.shape, 0)
    two, four = (sub == 3) | (sub == 4), (sub >= 2) & (sub <= 5)
    far_corner[0] = jnp.where(two, pltpu.roll(us[1], HALO, 0), us[3])
    far_corner[1] = ks[3]
    far_corner[2] = jnp.where(two, pltpu.roll(flux, HALO, 0), gs[3])
    far_corner[3] = ks[2]
    far_corner[4] = gs[2]
    far_corner[5] = jnp.where(four, pltpu.roll(ks[1], HALO, 0), us[2])
    far_corner[6] = gs[1]


class Halves:
    def __init__(self, *parts):
        self.parts, self.size = parts, parts[0].shape[0]

    def at_plane(self, index):
        plane, *rest = index if isinstance(index, tuple) else (index,)
        return self.parts[plane // self.size], (plane % self.size, *rest)

    def __getitem__(self, index):
        ref, inside = self.at_plane(index)
        return ref[inside]

    def __setitem__(self, index, value):
        ref, inside = self.at_plane(index)
        ref[inside] = value


class Steps:
    def __init__(self, cells_x, cells_y, cells_z):
        self.rows = cells_y + 8
        self.cells = (cells_x, cells_y, cells_z)
        self.T = self.rows // 8
        self.right = cells_z - 1
        self.lane = lanes_of((8, cells_z))
        gx, gy = lax.axis_index("gx"), lax.axis_index("gy")
        self.odd = gx % 2
        self.sign = (1 - 2 * self.odd).astype(jnp.float32)
        self.no_far = (gx == 0) | (gx == lax.axis_size("gx") - 1)
        self.no_low, self.no_high = gy == 0, gy == lax.axis_size("gy") - 1

    def rower(self, ref):
        return lambda i, j: ref[i, pl.ds(j, 8, stride=self.T), :]

    def reader(self, load, start):
        seen = {}
        T = self.T

        def read(d, j):
            if (d, j) not in seen:
                if j == -1:
                    seen[d, j] = pltpu.roll(load(start + d, T - 1), 1, 0)
                elif j == T:
                    seen[d, j] = pltpu.roll(load(start + d, 0), 7, 0)
                else:
                    seen[d, j] = load(start + d, j)
            return seen[d, j]

        return read

    def up_lane(self, value):
        return pltpu.roll(value, self.right, 1)

    def down_lane(self, value):
        return pltpu.roll(value, 1, 1)

    def inner_up(self, value):
        return jnp.where(self.lane == self.right, 0.0, self.up_lane(value))

    def inner_down(self, value):
        return jnp.where(self.lane == 0, 0.0, self.down_lane(value))

    def change(self, v, d, j, wx, wxm, wy, wym, wz, s, inflow=None):
        c = v(d, j)
        below = wxm * v(d - 1, j) if inflow is None else inflow
        along = (wx * v(d + 1, j) + below) + (wy * v(d, j + 1) + wym * v(d, j - 1))
        return along + (wz * self.up_lane(c) + self.down_lane(wz * c)) - s * c

    def prelude(self, loads, start, count, finish, outermost=None):
        k, u, g = (self.reader(load, start) for load in loads)
        for j in range(self.T):
            low = -1 if outermost is None else 0
            wx = {d: k(d, j) + k(d + 1, j) for d in range(low, count)}
            flux = {d: (self.sign * g(d, j)) * wx[d] for d in range(low, count)}
            inflow = None
            if outermost is not None:
                inflow, flux[-1] = outermost[0](j), self.sign * outermost[1](j)
            for d in range(count):
                c = k(d, j)
                wy, wym = c + k(d, j + 1), c + k(d, j - 1)
                wzt, wzm = c + self.inner_up(c), c + self.inner_down(c)
                wz = jnp.where(self.lane == self.right, 0.0, wzt)
                wxm = wx.get(d - 1)
                s = ((wx[d] if wxm is None else wx[d] + wxm) + (wy + wym)) + (wzt + wzm)
                e = self.change(u, d, j, wx[d], wxm, wy, wym, wz, s, inflow if d == 0 else None)
                finish(start + d, j, wx[d], wy, wz, s, e, flux[d] - flux[d - 1])

    def clear_rows(self, E, Wy, first, count):
        row = jnp.zeros((count, 1, self.cells[2]), jnp.float32)

        def clear(ref, r):
            at = r // self.T
            ref[first : first + count, r % self.T, at : at + 1, :] = row

        @pl.when(self.no_low)
        def _():
            clear(E, self.rows - 1)
            clear(Wy, self.rows - 1)

        @pl.when(self.no_high)
        def _():
            clear(E, self.cells[1])
            clear(Wy, self.cells[1] - 1)

    def sweep(self, loads, start, count, finish, boxes):
        le, lz, lwx, lwy, lwz, ls = loads
        e, z, wxs, wys = (self.reader(load, start) for load in (le, lz, lwx, lwy))
        for j in range(self.T):
            wanted = {d + o for d in range(count) if boxes[d] for o in (-1, 0, 1)}
            sums = {d: z(d, j) + (z(d, j + 1) + z(d, j - 1)) for d in sorted(wanted)}
            for d in range(count):
                i = start + d
                weights = (wxs(d, j), wxs(d - 1, j), wys(d, j), wys(d, j - 1), lwz(i, j), ls(i, j))
                em = self.change(e, d, j, *weights)
                zm = self.change(z, d, j, *weights)
                q = None
                if boxes[d]:
                    xs = sums[d - 1] + sums[d] + sums[d + 1]
                    xs = xs + (self.inner_up(xs) + self.inner_down(xs))
                    q = xs * (1.0 / 27.0) - z(d, j)
                finish(i, j, e(d, j), em, z(d, j), zm, q)

    def results(self, OI, OS, o, j, total, z):
        OI[o, pl.ds(j, 8, stride=self.T), :] = total * (-1.0 / (step_size * step_size))
        OS[o, pl.ds(j, 8, stride=self.T), :] = z * (1.0 / step_size)

    def leave(self, first, OI, OS, ind, sens, sems, p):
        pair = pl.ds(first, 2)
        return [
            pltpu.make_async_copy(source.at[pair, pl.ds(0, self.cells[1]), :], target.at[pair], sems.at[k, p])
            for k, (source, target) in enumerate(((OI, ind), (OS, sens)))
        ]


KEPT = (("EA", 5, 4), ("ZA", 5, 4), ("EB", 6, 2), ("ZB", 6, 2), ("Wx", 4, 4), ("Wy", 5, 3), ("Wz", 5, 3),
        ("S", 5, 3), ("M0", 6, 2), ("Q3", 6, 2), ("AC", 7, 1))
KEPT_PLANES = sum(count for _, _, count in KEPT)


def turns(count, body, together=9):
    full = count // together

    def turn(p, _):
        for d in range(together):
            body(together * p + d)
        return 0

    lax.fori_loop(0, full, turn, 0)
    for p in range(full * together, count):
        body(p)


def tiler(ref):
    return lambda i, j: ref[i, j]


def inner_kernel(initial, material, goal, table, first, second, near_a, near_b, OI, OS, edge, kept,
                 U, K, G, Wx, Wy, Wz, S, EA, EB, ZA, ZB, M0, Q3, AC):
    cells_x, cells_y, cells_z = initial.shape
    H = HALO
    steps = Steps(cells_x, cells_y, cells_z)
    odd = steps.odd
    planes = cells_x + 2 * H
    chosen = from_first(cells_z)
    near = Halves(near_a, near_b)
    side, step = odd * (planes - 1), 1 - 2 * odd

    def place(natural):
        return side + step * natural

    def own(p, _):
        ones = goal_tiles(p, cells_x, first, second, chosen)
        for d in range(2):
            i = 2 * p + d
            f = place(H + i)
            U[f, 0:cells_y, :] = initial[i]
            K[f, 0:cells_y, :] = gather_rows(table[0:1], material[i])
            G[f + 1 - odd, 0:cells_y, :] = goal[i].astype(jnp.float32)
            U[f, cells_y:, :], K[f, cells_y:, :] = halo_tiles(i, cells_x, first, second, chosen)
            G[f + 1 - odd, cells_y:, :] = ones[d]
        return 0

    lax.fori_loop(0, cells_x // 2, own, 0)
    for i in range(H):
        f = (1 - odd) * (H + cells_x + i) + odd * (planes - 1 - i)
        U[f] = near[i]
        K[f] = near[H + i]
        G[f + 1 - odd] = near[2 * H + i]
    for d in range(2):
        edge[d] = U[H + d]
        edge[2 + d] = K[H + d]
        edge[4 + d] = G[H + d + 1 - odd]

    def first_goal(i, j):
        return G[i + 1, pl.ds(j, 8, stride=steps.T), :]

    def begin(i, j, wx, wy, wz, s, e, z):
        Wx[i, j], Wy[i, j], Wz[i, j], S[i, j], EA[i, j], ZA[i, j] = wx, wy, wz, s, e, z

    def prelude(p):
        steps.prelude((steps.rower(K), steps.rower(U), first_goal), H + 1 + 2 * p, 2, begin)

    turns((planes - 2 - H) // 2, prelude)
    for j in range(steps.T):
        k = steps.rower(K)
        Wx[H, j] = k(H, j) + k(H + 1, j)
    steps.clear_rows(EA, Wy, H + 1, planes - 2 - H)

    def store_a(i, j, e, em, z, zm, q):
        EB[i, j] = e + em
        ZB[i, j] = z + zm
        if q is not None:
            M0[i - H, j] = em
            Q3[i - H, j] = q

    def store_b(i, j, e, em, z, zm, q):
        EA[i, j] = e + em
        ZA[i, j] = z + zm
        if q is not None:
            AC[i - H, j] = em * q

    def store_c(i, j, e, em, z, zm, q):
        o = i - H
        total = AC[o, j] + em * Q3[o, j] + M0[o, j] * q
        steps.results(OI, OS, place(i) - H, j, total, z + zm)

    weights = tuple(tiler(ref) for ref in (Wx, Wy, Wz, S))

    def sweep(E, Z, start, finish, boxes):
        steps.sweep((tiler(E), tiler(Z)) + weights, start, len(boxes), finish, boxes)

    def many(E, Z, start, pairs, finish):
        turns(pairs, lambda p: sweep(E, Z, start + 2 * p, finish, (True, True)))

    top = H + cells_x
    many(EA, ZA, H + 2, (cells_x - 2) // 2, store_a)
    sweep(EA, ZA, top, store_a, (False, False))
    many(EB, ZB, H + 3, (cells_x - 4) // 2, store_b)
    sweep(EB, ZB, top - 1, store_b, (True, False))

    turns((cells_x - 4) // 2, lambda p: sweep(EA, ZA, H + 4 + 2 * p, store_c, (True, True)))
    refs = dict(EA=EA, ZA=ZA, EB=EB, ZB=ZB, Wx=Wx, Wy=Wy, Wz=Wz, S=S, M0=M0, Q3=Q3, AC=AC)
    at = 0
    for name, start, count in KEPT:
        shift = H if name in ("M0", "Q3", "AC") else 0
        for d in range(count):
            kept[at + d] = refs[name][start - shift + d]
        at += count


def outer_kernel(far, far_corner, edge, kept, inner_ind, inner_sens, ind, sens,
                 U, K, G, FU, FG, Wx, Wy, Wz, S, EA, EB, EC, ZA, ZB, ZC, M0, Q3, AC, OI, OS, sems):
    cells_x, cells_y, cells_z = ind.shape
    H = HALO
    steps = Steps(cells_x, cells_y, cells_z)
    odd = steps.odd
    done = pl.ds((1 - odd) * H, cells_x - H)
    moves = [
        pltpu.make_async_copy(source.at[done, pl.ds(0, cells_y), :], target.at[done], sems.at[k, 2])
        for k, (source, target) in enumerate(((inner_ind, ind), (inner_sens, sens)))
    ]
    for move in moves:
        move.start()
    FU[0:cells_y, :] = far[3]
    FU[cells_y:, :] = jnp.zeros((8, cells_z), jnp.float32)
    FG[0:cells_y, :] = far[7]
    for f in range(1, H):
        U[f, 0:cells_y, :] = far[f - 1]
        K[f, 0:cells_y, :] = far[3 + f]
        G[f + 1, 0:cells_y, :] = far[7 + f]
    tiles = [far_corner[i] for i in range(7)]
    turned = {i: pltpu.roll(tiles[i], HALO, 0) for i in (0, 2, 5)}
    for ref, values in (
        (U, (turned[0], tiles[5], tiles[0])),
        (K, (turned[5], tiles[3], tiles[1])),
        (G, (tiles[6], tiles[4], tiles[2])),
    ):
        for f in range(1, H):
            ref[f + 1 if ref is G else f, cells_y:, :] = values[f - 1]
    FG[cells_y:, :] = turned[2]
    for d in range(2):
        U[H + d] = edge[d]
        K[H + d] = edge[2 + d]
        G[H + d + 1 - odd] = edge[4 + d]

    places, at = {}, 0
    for name, first, count in KEPT:
        places[name] = (first, at)
        at += count

    def mixed(ref, name, own_first, own_last):
        first, offset = places[name]

        def load(i, j):
            if own_first <= i <= own_last:
                return ref[i, j]
            return kept[offset + i - first, j]

        return load

    def first_goal(i, j):
        return G[i + 1, pl.ds(j, 8, stride=steps.T), :]

    sub = lax.broadcasted_iota(jnp.int32, (8, cells_z), 0)
    T = steps.T
    no_far, no_low, no_high = (
        jnp.broadcast_to(flag, sub.shape) for flag in (steps.no_far, steps.no_low, steps.no_high))

    def cleared(value, j, r, flag):
        if r % T != j:
            return value
        return jnp.where((sub == r // T) & flag, 0.0, value)

    def begin(i, j, wx, wy, wz, s, e, z):
        e = cleared(cleared(e, j, steps.rows - 1, no_low), j, cells_y, no_high)
        wy = cleared(cleared(wy, j, steps.rows - 1, no_low), j, cells_y - 1, no_high)
        if i == H - 1:
            wx, e, z = (jnp.where(no_far, 0.0, value) for value in (wx, e, z))
        Wx[i, j], Wy[i, j], Wz[i, j], S[i, j], EA[i, j], ZA[i, j] = wx, wy, wz, s, e, z

    def fluxes(ref):
        return lambda j: ref[pl.ds(j, 8, stride=steps.T), :]

    fields = (steps.rower(K), steps.rower(U), first_goal)
    steps.prelude(fields, 3, 2, begin)
    steps.prelude(fields, 1, 2, begin, (fluxes(FU), fluxes(FG)))
    weights = (mixed(Wx, "Wx", 1, H), mixed(Wy, "Wy", 1, H), mixed(Wz, "Wz", 1, H), mixed(S, "S", 1, H))

    def store_a(i, j, e, em, z, zm, q):
        EB[i, j] = e + em
        ZB[i, j] = z + zm
        if q is not None:
            M0[i, j] = em
            Q3[i, j] = q

    def store_b(i, j, e, em, z, zm, q):
        EC[i, j] = e + em
        ZC[i, j] = z + zm
        if q is not None:
            AC[i, j] = em * q

    top = H + cells_x
    m0, q3, ac = mixed(M0, "M0", H, H + 1), mixed(Q3, "Q3", H, H + 1), mixed(AC, "AC", H, H + 2)

    def store_c(i, j, e, em, z, zm, q):
        total = ac(i, j) + em * q3(i, j) + m0(i, j) * q
        steps.results(OI, OS, (1 - odd) * (i - H) + odd * (top - 1 - i), j, total, z + zm)

    first = (mixed(EA, "EA", 1, H), mixed(ZA, "ZA", 1, H)) + weights
    second = (mixed(EB, "EB", 2, H + 1), mixed(ZB, "ZB", 2, H + 1)) + weights
    third = (mixed(EC, "EA", 3, H + 2), mixed(ZC, "ZA", 3, H + 2)) + weights
    steps.sweep(first, 4, 2, store_a, (True, True))
    steps.sweep(first, 2, 2, store_a, (False, False))
    steps.sweep(second, 5, 2, store_b, (True, True))
    steps.sweep(second, 3, 2, store_b, (False, True))
    for p in (1, 0):
        f = H + 2 * p
        steps.sweep(third, f, 2, store_c, (True, True))
        moves += steps.leave((1 - odd) * (f - H) + odd * (top - 2 - f), OI, OS, ind, sens, sems, p)
        for move in moves[-2:]:
            move.start()
    for move in moves:
        move.wait()


def whole(memory=None):
    return pl.BlockSpec(memory_space=memory or pltpu.VMEM)


def swap(pairs):
    return [(a, b) for a, b in pairs] + [(b, a) for a, b in pairs]


def per_device(initial, material, goal_faces, conductivity):
    cells_x, cells_y, cells_z = initial.shape
    f32 = jnp.float32
    params = pltpu.CompilerParams(vmem_limit_bytes=LIMIT)
    small = pltpu.CompilerParams(vmem_limit_bytes=LIMIT // 4)
    shape = jax.ShapeDtypeStruct
    hbm, vmem = whole(pltpu.HBM), whole()
    rows = cells_y + 8
    planes = cells_x + 2 * HALO
    send = shape((cells_x + cells_x // 2, 8, cells_z), f32)
    block = shape(initial.shape, f32)
    count = lax.axis_size("gx")
    far_pairs = [(i, i + 1) for i in range(1, count - 1, 2)]
    near_pairs = [(i, i + 1) for i in range(0, count, 2)]

    here = [pltpu.with_memory_space_constraint(x, pltpu.HBM) for x in (initial, material, goal_faces, conductivity)]
    ends = (2, cells_x, 8, cells_z)
    first, second, table = pl.pallas_call(
        edge_kernel,
        out_shape=(send, send, shape((8, cells_z), f32)),
        in_specs=[hbm] * 4,
        out_specs=(vmem, vmem, vmem),
        scratch_shapes=[
            pltpu.VMEM(ends, f32),
            pltpu.VMEM(ends, jnp.int32),
            pltpu.VMEM(ends, jnp.int32),
            pltpu.SMEM(conductivity.shape, f32),
            pltpu.SemaphoreType.DMA((7,)),
        ],
        compiler_params=small,
        name="edges",
    )(*here)
    first_sent = first
    rows_y = lax.axis_size("gy")
    first, second = (
        lax.ppermute(value, "gy", swap([(i, i + 1) for i in range(start, rows_y - 1, 2)]))
        for start, value in enumerate((first, second))
    )
    far = pl.pallas_call(
        far_kernel,
        out_shape=shape((3 * HALO - 1, cells_y, cells_z), f32),
        in_specs=[vmem] * 4 + [whole(pl.ANY)],
        out_specs=vmem,
        compiler_params=small,
        name="far",
    )(initial, material, goal_faces, table, first_sent)
    far_sent = far
    far = lax.ppermute(far, "gx", swap(far_pairs))
    part = shape((3 * HALO // 2, rows, cells_z), f32)
    near_a, near_b, far_corner = pl.pallas_call(
        near_kernel,
        out_shape=(part, part, shape((7, 8, cells_z), f32)),
        in_specs=[vmem] * 6 + [whole(pl.ANY)],
        out_specs=(vmem,) * 3,
        compiler_params=small,
        cost_estimate=pl.CostEstimate(flops=10**9, bytes_accessed=1000, transcendentals=0),
        name="near",
    )(initial, material, goal_faces, table, first, second, far_sent)
    near_a = lax.ppermute(near_a, "gx", swap(near_pairs))
    near_b = lax.ppermute(near_b, "gx", swap(near_pairs))
    far_corner = lax.ppermute(far_corner, "gx", swap(far_pairs))

    def tiles(count):
        return pltpu.VMEM((count, rows // 8, 8, cells_z), f32)

    def natural(count):
        return pltpu.VMEM((count, rows, cells_z), f32)

    wide_block = shape((cells_x, rows, cells_z), f32)
    ind, sens, edge, kept = pl.pallas_call(
        inner_kernel,
        out_shape=(wide_block, wide_block, shape((6, rows, cells_z), f32), shape((KEPT_PLANES, rows // 8, 8, cells_z), f32)),
        in_specs=[vmem] * 8,
        out_specs=(vmem,) * 4,
        scratch_shapes=[natural(planes), natural(planes), natural(planes + 1)]
        + [tiles(planes)] * 8 + [tiles(cells_x)] * 3,
        compiler_params=params,
        cost_estimate=pl.CostEstimate(flops=1000, bytes_accessed=1000, transcendentals=0),
        name="inner",
    )(initial, material, goal_faces, table, first, second, near_a, near_b)
    return pl.pallas_call(
        outer_kernel,
        out_shape=(block, block),
        in_specs=[vmem] * 6,
        out_specs=(hbm, hbm),
        scratch_shapes=[natural(HALO + 2), natural(HALO + 2), natural(HALO + 3)]
        + [pltpu.VMEM((rows, cells_z), f32)] * 2 + [tiles(2 * HALO)] * 13 + [natural(cells_x)] * 2 + [pltpu.SemaphoreType.DMA((2, 3))],
        compiler_params=small,
        name="outer",
    )(far, far_corner, edge, kept, ind, sens)


def solution(mesh):
    placed = (P("gx", "gy", None), P("gx", "gy", None), P("gx", "gy", None), P())
    return jax.shard_map(
        per_device,
        mesh=mesh,
        in_specs=placed,
        out_specs=(P("gx", "gy", None), P("gx", "gy", None)),
        check_vma=False,
    )
```

```python
import functools

import jax
import jax.numpy as jnp
from jax import lax
from jax.experimental import pallas as pl
from jax.experimental.pallas import tpu as pltpu
from jax.sharding import PartitionSpec as P

step_size = 0.075
HALO = 4
LIMIT = 40 * 1024 * 1024


def lanes_of(shape):
    return lax.broadcasted_iota(jnp.int32, shape, len(shape) - 1)


def half_weights(cond, lanes):
    lane = lanes_of((1, lanes))
    table = jnp.zeros((1, lanes), jnp.float32)
    for which in range(cond.shape[0]):
        table = jnp.where(lane == which, cond[which] * (0.5 * step_size), table)
    return table


def gather_rows(table, index):
    return jnp.take_along_axis(jnp.broadcast_to(table, index.shape), index, axis=1, mode="promise_in_bounds")


def edge_kernel(initial, material, goal, cond, first, second, shared, u, ids, flags, values, sems):
    cells_x, cells_y, cells_z = initial.shape
    moves = [pltpu.make_async_copy(cond, values, sems.at[6])]
    for end, row in enumerate((0, cells_y - 8)):
        for k, (source, target) in enumerate(((material, ids), (initial, u), (goal, flags))):
            moves.append(pltpu.make_async_copy(
                source.at[:, pl.ds(row, 8), :], target.at[end], sems.at[3 * end + k]))
    for move in moves:
        move.start()
    low_half = lax.broadcasted_iota(jnp.int32, (8, cells_z), 0) < HALO
    moves[0].wait()
    table = half_weights(values, cells_z)
    shared[...] = jnp.broadcast_to(table, shared.shape)
    for move in moves[1:]:
        move.wait()
    even = jnp.broadcast_to(lax.axis_index("gy") % 2 == 0, low_half.shape)

    def put(i, up, down):
        first[i] = jnp.where(even, up, down)
        second[i] = jnp.where(even, down, up)

    for i in range(cells_x):
        k_low = pltpu.roll(gather_rows(table, ids[0, i]), HALO, 0)
        k_high = pltpu.roll(gather_rows(table, ids[1, i]), HALO, 0)
        put(i, jnp.where(low_half, k_high, u[1, i]), jnp.where(low_half, u[0, i], k_low))
    for p in range(cells_x // 2):
        high_one, high_two = flags[1, 2 * p], pltpu.roll(flags[1, 2 * p + 1], HALO, 0)
        low_one, low_two = flags[0, 2 * p], pltpu.roll(flags[0, 2 * p + 1], HALO, 0)
        put(cells_x + p, jnp.where(low_half, high_two, high_one).astype(jnp.float32),
            jnp.where(low_half, low_one, low_two).astype(jnp.float32))


def face_planes(send, start, u, material, goal, table):
    cells_y = u.shape[1]
    for i in range(HALO):
        send[i, 0:cells_y, :] = u[start + i]
        send[HALO + i, 0:cells_y, :] = gather_rows(table, material[start + i])
        send[2 * HALO + i, 0:cells_y, :] = goal[start + i].astype(jnp.float32)


def far_order(odd, cells_x):
    last = cells_x - HALO
    return (
        lambda f: odd * (last + f) + (1 - odd) * (HALO - 1 - f),
        lambda f: odd * (last + f) + (1 - odd) * max(HALO - 2 - f, 0),
    )


def far_kernel(u, material, goal, table, sent, far):
    plane, cell = far_order(lax.axis_index("gx") % 2, u.shape[0])
    kappa = [gather_rows(table[0:1], material[plane(f)]) for f in range(HALO)]
    face = kappa[0] + kappa[1]
    far[3] = face * (u[plane(0)] - u[plane(1)])
    far[7] = face * goal[cell(0)].astype(jnp.float32)
    for f in range(1, HALO):
        far[f - 1] = u[plane(f)]
        far[3 + f] = kappa[f]
        far[7 + f] = goal[cell(f)].astype(jnp.float32)


def from_first(cells_z):
    low_half = lax.broadcasted_iota(jnp.int32, (8, cells_z), 0) < HALO
    even = jnp.broadcast_to(lax.axis_index("gy") % 2 == 0, low_half.shape)
    return low_half == even


def halo_tiles(plane, cells_x, first, second, chosen):
    one, two = first[plane], second[plane]
    return jnp.where(chosen, one, two), pltpu.roll(jnp.where(chosen, two, one), HALO, 0)


def goal_tiles(pair, cells_x, first, second, chosen):
    return halo_tiles(cells_x + pair, cells_x, first, second, chosen)


def near_kernel(u, material, goal, table, first, second, far, near_a, near_b, far_corner):
    cells_x, cells_y, cells_z = u.shape
    chosen = from_first(cells_z)
    odd = lax.axis_index("gx") % 2
    last = cells_x - HALO
    near = Halves(near_a, near_b)
    face_planes(near, (1 - odd) * last, u, material, goal, table[0:1])

    def all_tiles(start):
        us, ks, gs = [], [], []
        for i in range(HALO):
            hu, hk = halo_tiles(start + i, cells_x, first, second, chosen)
            us.append(hu)
            ks.append(hk)
        for i in range(0, HALO, 2):
            gs += goal_tiles(start // 2 + i // 2, cells_x, first, second, chosen)
        return us, ks, gs

    for field, tiles in enumerate(all_tiles((1 - odd) * last)):
        for i in range(HALO):
            near[field * HALO + i, pl.ds(cells_y, 8), :] = tiles[i]

    us, ks, gs = all_tiles(odd * last)
    is_odd = jnp.broadcast_to(odd == 1, chosen.shape)
    us, ks = [[jnp.where(is_odd, t[f], t[HALO - 1 - f]) for f in range(HALO)] for t in (us, ks)]
    gs = [jnp.where(is_odd, gs[f], gs[max(HALO - 2 - f, 0)]) for f in range(HALO)]
    flux = gs[0] * (ks[0] + ks[1])
    sub = lax.broadcasted_iota(jnp.int32, chosen.shape, 0)
    two, four = (sub == 3) | (sub == 4), (sub >= 2) & (sub <= 5)
    far_corner[0] = jnp.where(two, pltpu.roll(us[1], HALO, 0), us[3])
    far_corner[1] = ks[3]
    far_corner[2] = jnp.where(two, pltpu.roll(flux, HALO, 0), gs[3])
    far_corner[3] = ks[2]
    far_corner[4] = gs[2]
    far_corner[5] = jnp.where(four, pltpu.roll(ks[1], HALO, 0), us[2])
    far_corner[6] = gs[1]


class Halves:
    def __init__(self, *parts):
        self.parts, self.size = parts, parts[0].shape[0]

    def at_plane(self, index):
        plane, *rest = index if isinstance(index, tuple) else (index,)
        return self.parts[plane // self.size], (plane % self.size, *rest)

    def __getitem__(self, index):
        ref, inside = self.at_plane(index)
        return ref[inside]

    def __setitem__(self, index, value):
        ref, inside = self.at_plane(index)
        ref[inside] = value


class Steps:
    def __init__(self, cells_x, cells_y, cells_z):
        self.rows = cells_y + 8
        self.cells = (cells_x, cells_y, cells_z)
        self.T = self.rows // 8
        self.right = cells_z - 1
        self.lane = lanes_of((8, cells_z))
        gx, gy = lax.axis_index("gx"), lax.axis_index("gy")
        self.odd = gx % 2
        self.sign = (1 - 2 * self.odd).astype(jnp.float32)
        self.no_far = (gx == 0) | (gx == lax.axis_size("gx") - 1)
        self.no_low, self.no_high = gy == 0, gy == lax.axis_size("gy") - 1

    def rower(self, ref):
        return lambda i, j: ref[i, pl.ds(j, 8, stride=self.T), :]

    def reader(self, load, start):
        seen = {}
        T = self.T

        def read(d, j):
            if (d, j) not in seen:
                if j == -1:
                    seen[d, j] = pltpu.roll(load(start + d, T - 1), 1, 0)
                elif j == T:
                    seen[d, j] = pltpu.roll(load(start + d, 0), 7, 0)
                else:
                    seen[d, j] = load(start + d, j)
            return seen[d, j]

        return read

    def up_lane(self, value):
        return pltpu.roll(value, self.right, 1)

    def down_lane(self, value):
        return pltpu.roll(value, 1, 1)

    def inner_up(self, value):
        return jnp.where(self.lane == self.right, 0.0, self.up_lane(value))

    def inner_down(self, value):
        return jnp.where(self.lane == 0, 0.0, self.down_lane(value))

    def change(self, v, d, j, wx, wxm, wy, wym, wz, s, inflow=None):
        c = v(d, j)
        below = wxm * v(d - 1, j) if inflow is None else inflow
        along = (wx * v(d + 1, j) + below) + (wy * v(d, j + 1) + wym * v(d, j - 1))
        return along + (wz * self.up_lane(c) + self.down_lane(wz * c)) - s * c

    def prelude(self, loads, start, count, finish, outermost=None):
        k, u, g = (self.reader(load, start) for load in loads)
        for j in range(self.T):
            low = -1 if outermost is None else 0
            wx = {d: k(d, j) + k(d + 1, j) for d in range(low, count)}
            flux = {d: (self.sign * g(d, j)) * wx[d] for d in range(low, count)}
            inflow = None
            if outermost is not None:
                inflow, flux[-1] = outermost[0](j), self.sign * outermost[1](j)
            for d in range(count):
                c = k(d, j)
                wy, wym = c + k(d, j + 1), c + k(d, j - 1)
                wzt, wzm = c + self.inner_up(c), c + self.inner_down(c)
                wz = jnp.where(self.lane == self.right, 0.0, wzt)
                wxm = wx.get(d - 1)
                s = ((wx[d] if wxm is None else wx[d] + wxm) + (wy + wym)) + (wzt + wzm)
                e = self.change(u, d, j, wx[d], wxm, wy, wym, wz, s, inflow if d == 0 else None)
                finish(start + d, j, wx[d], wy, wz, s, e, flux[d] - flux[d - 1])

    def clear_rows(self, E, Wy, first, count):
        row = jnp.zeros((count, 1, self.cells[2]), jnp.float32)

        def clear(ref, r):
            at = r // self.T
            ref[first : first + count, r % self.T, at : at + 1, :] = row

        @pl.when(self.no_low)
        def _():
            clear(E, self.rows - 1)
            clear(Wy, self.rows - 1)

        @pl.when(self.no_high)
        def _():
            clear(E, self.cells[1])
            clear(Wy, self.cells[1] - 1)

    def sweep(self, loads, start, count, finish, boxes):
        le, lz, lwx, lwy, lwz, ls = loads
        e, z, wxs, wys = (self.reader(load, start) for load in (le, lz, lwx, lwy))
        for j in range(self.T):
            wanted = {d + o for d in range(count) if boxes[d] for o in (-1, 0, 1)}
            sums = {d: z(d, j) + (z(d, j + 1) + z(d, j - 1)) for d in sorted(wanted)}
            for d in range(count):
                i = start + d
                weights = (wxs(d, j), wxs(d - 1, j), wys(d, j), wys(d, j - 1), lwz(i, j), ls(i, j))
                em = self.change(e, d, j, *weights)
                zm = self.change(z, d, j, *weights)
                q = None
                if boxes[d]:
                    xs = sums[d - 1] + sums[d] + sums[d + 1]
                    xs = xs + (self.inner_up(xs) + self.inner_down(xs))
                    q = xs * (1.0 / 27.0) - z(d, j)
                finish(i, j, e(d, j), em, z(d, j), zm, q)

    def results(self, OI, OS, o, j, total, z):
        OI[o, pl.ds(j, 8, stride=self.T), :] = total * (-1.0 / (step_size * step_size))
        OS[o, pl.ds(j, 8, stride=self.T), :] = z * (1.0 / step_size)

    def leave(self, first, OI, OS, ind, sens, sems, p):
        pair = pl.ds(first, 2)
        return [
            pltpu.make_async_copy(source.at[pair, pl.ds(0, self.cells[1]), :], target.at[pair], sems.at[k, p])
            for k, (source, target) in enumerate(((OI, ind), (OS, sens)))
        ]


KEPT = (("EA", 5, 4), ("ZA", 5, 4), ("EB", 6, 2), ("ZB", 6, 2), ("Wx", 4, 4), ("Wy", 5, 3), ("Wz", 5, 3),
        ("S", 5, 3), ("M0", 6, 2), ("Q3", 6, 2), ("AC", 7, 1))
KEPT_PLANES = sum(count for _, _, count in KEPT)


def turns(count, body, together=9):
    full = count // together

    def turn(p, _):
        for d in range(together):
            body(together * p + d)
        return 0

    lax.fori_loop(0, full, turn, 0)
    for p in range(full * together, count):
        body(p)


def tiler(ref):
    return lambda i, j: ref[i, j]


def inner_kernel(initial, material, goal, table, first, second, near_a, near_b, OI, OS, edge, kept,
                 U, K, G, Wx, Wy, Wz, S, EA, EB, ZA, ZB, M0, Q3, AC):
    cells_x, cells_y, cells_z = initial.shape
    H = HALO
    steps = Steps(cells_x, cells_y, cells_z)
    odd = steps.odd
    planes = cells_x + 2 * H
    chosen = from_first(cells_z)
    near = Halves(near_a, near_b)
    side, step = odd * (planes - 1), 1 - 2 * odd

    def place(natural):
        return side + step * natural

    def own(p):
        ones = goal_tiles(p, cells_x, first, second, chosen)
        for d in range(2):
            i = 2 * p + d
            f = place(H + i)
            U[f, 0:cells_y, :] = initial[i]
            K[f, 0:cells_y, :] = gather_rows(table[0:1], material[i])
            G[f + 1 - odd, 0:cells_y, :] = goal[i].astype(jnp.float32)
            U[f, cells_y:, :], K[f, cells_y:, :] = halo_tiles(i, cells_x, first, second, chosen)
            G[f + 1 - odd, cells_y:, :] = ones[d]

    turns(cells_x // 2, own)
    for i in range(H):
        f = (1 - odd) * (H + cells_x + i) + odd * (planes - 1 - i)
        U[f] = near[i]
        K[f] = near[H + i]
        G[f + 1 - odd] = near[2 * H + i]
    for d in range(2):
        for j in range(steps.T):
            here = pl.ds(j, 8, stride=steps.T)
            edge[d, j] = U[H + d, here, :]
            edge[2 + d, j] = K[H + d, here, :]
            edge[4 + d, j] = G[H + d + 1 - odd, here, :]

    def first_goal(i, j):
        return G[i + 1, pl.ds(j, 8, stride=steps.T), :]

    def begin(i, j, wx, wy, wz, s, e, z):
        Wx[i, j], Wy[i, j], Wz[i, j], S[i, j], EA[i, j], ZA[i, j] = wx, wy, wz, s, e, z

    def prelude(p):
        steps.prelude((steps.rower(K), steps.rower(U), first_goal), H + 1 + 2 * p, 2, begin)

    turns((planes - 2 - H) // 2, prelude)
    for j in range(steps.T):
        k = steps.rower(K)
        Wx[H, j] = k(H, j) + k(H + 1, j)
    steps.clear_rows(EA, Wy, H + 1, planes - 2 - H)

    def store_a(i, j, e, em, z, zm, q):
        EB[i, j] = e + em
        ZB[i, j] = z + zm
        if q is not None:
            M0[i - H, j] = em
            Q3[i - H, j] = q

    def store_b(i, j, e, em, z, zm, q):
        EA[i, j] = e + em
        ZA[i, j] = z + zm
        if q is not None:
            AC[i - H, j] = em * q

    def store_c(i, j, e, em, z, zm, q):
        o = i - H
        total = AC[o, j] + em * Q3[o, j] + M0[o, j] * q
        steps.results(OI, OS, place(i) - H, j, total, z + zm)

    weights = tuple(tiler(ref) for ref in (Wx, Wy, Wz, S))

    def sweep(E, Z, start, finish, boxes):
        steps.sweep((tiler(E), tiler(Z)) + weights, start, len(boxes), finish, boxes)

    def many(E, Z, start, pairs, finish):
        turns(pairs, lambda p: sweep(E, Z, start + 2 * p, finish, (True, True)))

    top = H + cells_x
    many(EA, ZA, H + 2, (cells_x - 2) // 2, store_a)
    sweep(EA, ZA, top, store_a, (False, False))
    many(EB, ZB, H + 3, (cells_x - 4) // 2, store_b)
    sweep(EB, ZB, top - 1, store_b, (True, False))

    turns((cells_x - 4) // 2, lambda p: sweep(EA, ZA, H + 4 + 2 * p, store_c, (True, True)))
    refs = dict(EA=EA, ZA=ZA, EB=EB, ZB=ZB, Wx=Wx, Wy=Wy, Wz=Wz, S=S, M0=M0, Q3=Q3, AC=AC)
    at = 0
    for name, start, count in KEPT:
        shift = H if name in ("M0", "Q3", "AC") else 0
        for d in range(count):
            kept[at + d] = refs[name][start - shift + d]
        at += count


def outer_kernel(far, far_corner, edge, kept, inner_ind, inner_sens, ind, sens,
                 U, K, G, FU, FG, Wx, Wy, Wz, S, EA, EB, EC, ZA, ZB, ZC, M0, Q3, AC, OI, OS, sems):
    cells_x, cells_y, cells_z = ind.shape
    H = HALO
    steps = Steps(cells_x, cells_y, cells_z)
    odd = steps.odd
    done = pl.ds((1 - odd) * H, cells_x - H)
    moves = [
        pltpu.make_async_copy(source.at[done, pl.ds(0, cells_y), :], target.at[done], sems.at[k, 2])
        for k, (source, target) in enumerate(((inner_ind, ind), (inner_sens, sens)))
    ]
    for move in moves:
        move.start()
    FU[0:cells_y, :] = far[3]
    FU[cells_y:, :] = jnp.zeros((8, cells_z), jnp.float32)
    FG[0:cells_y, :] = far[7]
    for f in range(1, H):
        U[f, 0:cells_y, :] = far[f - 1]
        K[f, 0:cells_y, :] = far[3 + f]
        G[f + 1, 0:cells_y, :] = far[7 + f]
    tiles = [far_corner[i] for i in range(7)]
    turned = {i: pltpu.roll(tiles[i], HALO, 0) for i in (0, 2, 5)}
    for ref, values in (
        (U, (turned[0], tiles[5], tiles[0])),
        (K, (turned[5], tiles[3], tiles[1])),
        (G, (tiles[6], tiles[4], tiles[2])),
    ):
        for f in range(1, H):
            ref[f + 1 if ref is G else f, cells_y:, :] = values[f - 1]
    FG[cells_y:, :] = turned[2]

    places, at = {}, 0
    for name, first, count in KEPT:
        places[name] = (first, at)
        at += count

    def mixed(ref, name, own_first, own_last):
        first, offset = places[name]

        def load(i, j):
            if own_first <= i <= own_last:
                return ref[i, j]
            return kept[offset + i - first, j]

        return load

    sub_shape = (8, cells_z)
    is_odd = jnp.broadcast_to(odd == 1, sub_shape)

    def beside(ref, at):
        rows = steps.rower(ref)
        return lambda i, j: rows(i, j) if i < H else edge[at + i - H, j]

    def first_goal(i, j):
        if i < H - 1:
            return G[i + 1, pl.ds(j, 8, stride=steps.T), :]
        other = edge[4, j] if i == H else G[H, pl.ds(j, 8, stride=steps.T), :]
        return jnp.where(is_odd, edge[5 + i - H, j], other)

    sub = lax.broadcasted_iota(jnp.int32, (8, cells_z), 0)
    T = steps.T
    no_far, no_low, no_high = (
        jnp.broadcast_to(flag, sub.shape) for flag in (steps.no_far, steps.no_low, steps.no_high))

    def cleared(value, j, r, flag):
        if r % T != j:
            return value
        return jnp.where((sub == r // T) & flag, 0.0, value)

    def begin(i, j, wx, wy, wz, s, e, z):
        e = cleared(cleared(e, j, steps.rows - 1, no_low), j, cells_y, no_high)
        wy = cleared(cleared(wy, j, steps.rows - 1, no_low), j, cells_y - 1, no_high)
        if i == H - 1:
            wx, e, z = (jnp.where(no_far, 0.0, value) for value in (wx, e, z))
        Wx[i, j], Wy[i, j], Wz[i, j], S[i, j], EA[i, j], ZA[i, j] = wx, wy, wz, s, e, z

    def fluxes(ref):
        return lambda j: ref[pl.ds(j, 8, stride=steps.T), :]

    fields = (beside(K, 2), beside(U, 0), first_goal)
    steps.prelude(fields, 3, 2, begin)
    steps.prelude(fields, 1, 2, begin, (fluxes(FU), fluxes(FG)))
    weights = (mixed(Wx, "Wx", 1, H), mixed(Wy, "Wy", 1, H), mixed(Wz, "Wz", 1, H), mixed(S, "S", 1, H))

    def store_a(i, j, e, em, z, zm, q):
        EB[i, j] = e + em
        ZB[i, j] = z + zm
        if q is not None:
            M0[i, j] = em
            Q3[i, j] = q

    def store_b(i, j, e, em, z, zm, q):
        EC[i, j] = e + em
        ZC[i, j] = z + zm
        if q is not None:
            AC[i, j] = em * q

    top = H + cells_x
    m0, q3, ac = mixed(M0, "M0", H, H + 1), mixed(Q3, "Q3", H, H + 1), mixed(AC, "AC", H, H + 2)

    def store_c(i, j, e, em, z, zm, q):
        total = ac(i, j) + em * q3(i, j) + m0(i, j) * q
        steps.results(OI, OS, (1 - odd) * (i - H) + odd * (top - 1 - i), j, total, z + zm)

    first = (mixed(EA, "EA", 1, H), mixed(ZA, "ZA", 1, H)) + weights
    second = (mixed(EB, "EB", 2, H + 1), mixed(ZB, "ZB", 2, H + 1)) + weights
    third = (mixed(EC, "EA", 3, H + 2), mixed(ZC, "ZA", 3, H + 2)) + weights
    steps.sweep(first, 4, 2, store_a, (True, True))
    steps.sweep(first, 2, 2, store_a, (False, False))
    steps.sweep(second, 5, 2, store_b, (True, True))
    steps.sweep(second, 3, 2, store_b, (False, True))
    for p in (1, 0):
        f = H + 2 * p
        steps.sweep(third, f, 2, store_c, (True, True))
        moves += steps.leave((1 - odd) * (f - H) + odd * (top - 2 - f), OI, OS, ind, sens, sems, p)
        for move in moves[-2:]:
            move.start()
    for move in moves:
        move.wait()


def whole(memory=None):
    return pl.BlockSpec(memory_space=memory or pltpu.VMEM)


def swap(pairs):
    return [(a, b) for a, b in pairs] + [(b, a) for a, b in pairs]


def per_device(initial, material, goal_faces, conductivity):
    cells_x, cells_y, cells_z = initial.shape
    f32 = jnp.float32
    params = pltpu.CompilerParams(vmem_limit_bytes=LIMIT)
    small = pltpu.CompilerParams(vmem_limit_bytes=LIMIT // 4)
    shape = jax.ShapeDtypeStruct
    hbm, vmem = whole(pltpu.HBM), whole()
    rows = cells_y + 8
    planes = cells_x + 2 * HALO
    send = shape((cells_x + cells_x // 2, 8, cells_z), f32)
    block = shape(initial.shape, f32)
    count = lax.axis_size("gx")
    far_pairs = [(i, i + 1) for i in range(1, count - 1, 2)]
    near_pairs = [(i, i + 1) for i in range(0, count, 2)]

    here = [pltpu.with_memory_space_constraint(x, pltpu.HBM) for x in (initial, material, goal_faces, conductivity)]
    ends = (2, cells_x, 8, cells_z)
    first, second, table = pl.pallas_call(
        edge_kernel,
        out_shape=(send, send, shape((8, cells_z), f32)),
        in_specs=[hbm] * 4,
        out_specs=(vmem, vmem, vmem),
        scratch_shapes=[
            pltpu.VMEM(ends, f32),
            pltpu.VMEM(ends, jnp.int32),
            pltpu.VMEM(ends, jnp.int32),
            pltpu.SMEM(conductivity.shape, f32),
            pltpu.SemaphoreType.DMA((7,)),
        ],
        compiler_params=small,
        name="edges",
    )(*here)
    first_sent = first
    rows_y = lax.axis_size("gy")
    first, second = (
        lax.ppermute(value, "gy", swap([(i, i + 1) for i in range(start, rows_y - 1, 2)]))
        for start, value in enumerate((first, second))
    )
    far = pl.pallas_call(
        far_kernel,
        out_shape=shape((3 * HALO - 1, cells_y, cells_z), f32),
        in_specs=[vmem] * 4 + [whole(pl.ANY)],
        out_specs=vmem,
        compiler_params=small,
        name="far",
    )(initial, material, goal_faces, table, first_sent)
    far_sent = far
    far = lax.ppermute(far, "gx", swap(far_pairs))
    part = shape((3 * HALO // 2, rows, cells_z), f32)
    near_a, near_b, far_corner = pl.pallas_call(
        near_kernel,
        out_shape=(part, part, shape((7, 8, cells_z), f32)),
        in_specs=[vmem] * 6 + [whole(pl.ANY)],
        out_specs=(vmem,) * 3,
        compiler_params=small,
        cost_estimate=pl.CostEstimate(flops=10**9, bytes_accessed=1000, transcendentals=0),
        name="near",
    )(initial, material, goal_faces, table, first, second, far_sent)
    near_a = lax.ppermute(near_a, "gx", swap(near_pairs))
    near_b = lax.ppermute(near_b, "gx", swap(near_pairs))
    far_corner = lax.ppermute(far_corner, "gx", swap(far_pairs))

    def tiles(count):
        return pltpu.VMEM((count, rows // 8, 8, cells_z), f32)

    def natural(count):
        return pltpu.VMEM((count, rows, cells_z), f32)

    wide_block = shape((cells_x, rows, cells_z), f32)
    ind, sens, edge, kept = pl.pallas_call(
        inner_kernel,
        out_shape=(wide_block, wide_block, shape((6, rows // 8, 8, cells_z), f32), shape((KEPT_PLANES, rows // 8, 8, cells_z), f32)),
        in_specs=[vmem] * 8,
        out_specs=(vmem,) * 4,
        scratch_shapes=[natural(planes), natural(planes), natural(planes + 1)]
        + [tiles(planes)] * 8 + [tiles(cells_x)] * 3,
        compiler_params=params,
        cost_estimate=pl.CostEstimate(flops=1000, bytes_accessed=1000, transcendentals=0),
        name="inner",
    )(initial, material, goal_faces, table, first, second, near_a, near_b)
    return pl.pallas_call(
        outer_kernel,
        out_shape=(block, block),
        in_specs=[vmem] * 6,
        out_specs=(hbm, hbm),
        scratch_shapes=[natural(HALO), natural(HALO), natural(HALO + 1)]
        + [pltpu.VMEM((rows, cells_z), f32)] * 2 + [tiles(2 * HALO)] * 13 + [natural(cells_x)] * 2 + [pltpu.SemaphoreType.DMA((2, 3))],
        compiler_params=small,
        name="outer",
    )(far, far_corner, edge, kept, ind, sens)


def solution(mesh):
    placed = (P("gx", "gy", None), P("gx", "gy", None), P("gx", "gy", None), P())
    return jax.shard_map(
        per_device,
        mesh=mesh,
        in_specs=placed,
        out_specs=(P("gx", "gy", None), P("gx", "gy", None)),
        check_vma=False,
    )
```

```python
import functools

import jax
import jax.numpy as jnp
from jax import lax
from jax.experimental import pallas as pl
from jax.experimental.pallas import tpu as pltpu
from jax.sharding import PartitionSpec as P

step_size = 0.075
HALO = 4
LIMIT = 40 * 1024 * 1024


def lanes_of(shape):
    return lax.broadcasted_iota(jnp.int32, shape, len(shape) - 1)


def half_weights(cond, lanes):
    lane = lanes_of((1, lanes))
    table = jnp.zeros((1, lanes), jnp.float32)
    for which in range(cond.shape[0]):
        table = jnp.where(lane == which, cond[which] * (0.5 * step_size), table)
    return table


def gather_rows(table, index):
    return jnp.take_along_axis(jnp.broadcast_to(table, index.shape), index, axis=1, mode="promise_in_bounds")


def edge_kernel(initial, material, goal, cond, first, second, shared, u, ids, flags, values, sems):
    cells_x, cells_y, cells_z = initial.shape
    moves = [pltpu.make_async_copy(cond, values, sems.at[6])]
    for end, row in enumerate((0, cells_y - 8)):
        for k, (source, target) in enumerate(((material, ids), (initial, u), (goal, flags))):
            moves.append(pltpu.make_async_copy(
                source.at[:, pl.ds(row, 8), :], target.at[end], sems.at[3 * end + k]))
    for move in moves:
        move.start()
    low_half = lax.broadcasted_iota(jnp.int32, (8, cells_z), 0) < HALO
    moves[0].wait()
    table = half_weights(values, cells_z)
    shared[...] = jnp.broadcast_to(table, shared.shape)
    for move in moves[1:]:
        move.wait()
    upward = jnp.broadcast_to(lax.axis_index("gy") % 2 == 1, low_half.shape)

    def put(i, up, down):
        first[i] = jnp.where(upward, up, down)
        second[i] = jnp.where(upward, down, up)

    for i in range(cells_x):
        k_low = pltpu.roll(gather_rows(table, ids[0, i]), HALO, 0)
        k_high = pltpu.roll(gather_rows(table, ids[1, i]), HALO, 0)
        put(i, jnp.where(low_half, k_high, u[1, i]), jnp.where(low_half, u[0, i], k_low))
    for p in range(cells_x // 2):
        high_one, high_two = flags[1, 2 * p], pltpu.roll(flags[1, 2 * p + 1], HALO, 0)
        low_one, low_two = flags[0, 2 * p], pltpu.roll(flags[0, 2 * p + 1], HALO, 0)
        put(cells_x + p, jnp.where(low_half, high_two, high_one).astype(jnp.float32),
            jnp.where(low_half, low_one, low_two).astype(jnp.float32))


def face_planes(send, start, u, material, goal, table):
    cells_y = u.shape[1]
    for i in range(HALO):
        send[i, 0:cells_y, :] = u[start + i]
        send[HALO + i, 0:cells_y, :] = gather_rows(table, material[start + i])
        send[2 * HALO + i, 0:cells_y, :] = goal[start + i].astype(jnp.float32)


def far_order(odd, cells_x):
    last = cells_x - HALO
    return (
        lambda f: odd * (last + f) + (1 - odd) * (HALO - 1 - f),
        lambda f: odd * (last + f) + (1 - odd) * max(HALO - 2 - f, 0),
    )


def far_kernel(u, material, goal, table, sent, far):
    plane, cell = far_order(lax.axis_index("gx") % 2, u.shape[0])
    kappa = [gather_rows(table[0:1], material[plane(f)]) for f in range(HALO)]
    face = kappa[0] + kappa[1]
    far[3] = face * (u[plane(0)] - u[plane(1)])
    far[7] = face * goal[cell(0)].astype(jnp.float32)
    for f in range(1, HALO):
        far[f - 1] = u[plane(f)]
        far[3 + f] = kappa[f]
        far[7 + f] = goal[cell(f)].astype(jnp.float32)


def from_first(cells_z):
    low_half = lax.broadcasted_iota(jnp.int32, (8, cells_z), 0) < HALO
    upward = jnp.broadcast_to(lax.axis_index("gy") % 2 == 1, low_half.shape)
    return low_half == upward


def halo_tiles(plane, cells_x, first, second, chosen):
    one, two = first[plane], second[plane]
    return jnp.where(chosen, one, two), pltpu.roll(jnp.where(chosen, two, one), HALO, 0)


def goal_tiles(pair, cells_x, first, second, chosen):
    return halo_tiles(cells_x + pair, cells_x, first, second, chosen)


def near_kernel(u, material, goal, table, first, second, far, near_a, near_b, far_corner):
    cells_x, cells_y, cells_z = u.shape
    chosen = from_first(cells_z)
    odd = lax.axis_index("gx") % 2
    last = cells_x - HALO
    near = Halves(near_a, near_b)
    face_planes(near, (1 - odd) * last, u, material, goal, table[0:1])

    def all_tiles(start):
        us, ks, gs = [], [], []
        for i in range(HALO):
            hu, hk = halo_tiles(start + i, cells_x, first, second, chosen)
            us.append(hu)
            ks.append(hk)
        for i in range(0, HALO, 2):
            gs += goal_tiles(start // 2 + i // 2, cells_x, first, second, chosen)
        return us, ks, gs

    for field, tiles in enumerate(all_tiles((1 - odd) * last)):
        for i in range(HALO):
            near[field * HALO + i, pl.ds(cells_y, 8), :] = tiles[i]

    us, ks, gs = all_tiles(odd * last)
    is_odd = jnp.broadcast_to(odd == 1, chosen.shape)
    us, ks = [[jnp.where(is_odd, t[f], t[HALO - 1 - f]) for f in range(HALO)] for t in (us, ks)]
    gs = [jnp.where(is_odd, gs[f], gs[max(HALO - 2 - f, 0)]) for f in range(HALO)]
    flux = gs[0] * (ks[0] + ks[1])
    sub = lax.broadcasted_iota(jnp.int32, chosen.shape, 0)
    two, four = (sub == 3) | (sub == 4), (sub >= 2) & (sub <= 5)
    far_corner[0] = jnp.where(two, pltpu.roll(us[1], HALO, 0), us[3])
    far_corner[1] = ks[3]
    far_corner[2] = jnp.where(two, pltpu.roll(flux, HALO, 0), gs[3])
    far_corner[3] = ks[2]
    far_corner[4] = gs[2]
    far_corner[5] = jnp.where(four, pltpu.roll(ks[1], HALO, 0), us[2])
    far_corner[6] = gs[1]


class Halves:
    def __init__(self, *parts):
        self.parts, self.size = parts, parts[0].shape[0]

    def at_plane(self, index):
        plane, *rest = index if isinstance(index, tuple) else (index,)
        return self.parts[plane // self.size], (plane % self.size, *rest)

    def __getitem__(self, index):
        ref, inside = self.at_plane(index)
        return ref[inside]

    def __setitem__(self, index, value):
        ref, inside = self.at_plane(index)
        ref[inside] = value


class Steps:
    def __init__(self, cells_x, cells_y, cells_z):
        self.rows = cells_y + 8
        self.cells = (cells_x, cells_y, cells_z)
        self.T = self.rows // 8
        self.right = cells_z - 1
        self.lane = lanes_of((8, cells_z))
        gx, gy = lax.axis_index("gx"), lax.axis_index("gy")
        self.odd = gx % 2
        self.sign = (1 - 2 * self.odd).astype(jnp.float32)
        self.no_far = (gx == 0) | (gx == lax.axis_size("gx") - 1)
        self.no_low, self.no_high = gy == 0, gy == lax.axis_size("gy") - 1

    def rower(self, ref):
        return lambda i, j: ref[i, pl.ds(j, 8, stride=self.T), :]

    def reader(self, load, start):
        seen = {}
        T = self.T

        def read(d, j):
            if (d, j) not in seen:
                if j == -1:
                    seen[d, j] = pltpu.roll(load(start + d, T - 1), 1, 0)
                elif j == T:
                    seen[d, j] = pltpu.roll(load(start + d, 0), 7, 0)
                else:
                    seen[d, j] = load(start + d, j)
            return seen[d, j]

        return read

    def up_lane(self, value):
        return pltpu.roll(value, self.right, 1)

    def down_lane(self, value):
        return pltpu.roll(value, 1, 1)

    def inner_up(self, value):
        return jnp.where(self.lane == self.right, 0.0, self.up_lane(value))

    def inner_down(self, value):
        return jnp.where(self.lane == 0, 0.0, self.down_lane(value))

    def change(self, v, d, j, wx, wxm, wy, wym, wz, s, inflow=None):
        c = v(d, j)
        below = wxm * v(d - 1, j) if inflow is None else inflow
        along = (wx * v(d + 1, j) + below) + (wy * v(d, j + 1) + wym * v(d, j - 1))
        return along + (wz * self.up_lane(c) + self.down_lane(wz * c)) - s * c

    def prelude(self, loads, start, count, finish, outermost=None):
        k, u, g = (self.reader(load, start) for load in loads)
        for j in range(self.T):
            low = -1 if outermost is None else 0
            wx = {d: k(d, j) + k(d + 1, j) for d in range(low, count)}
            flux = {d: (self.sign * g(d, j)) * wx[d] for d in range(low, count)}
            inflow = None
            if outermost is not None:
                inflow, flux[-1] = outermost[0](j), self.sign * outermost[1](j)
            for d in range(count):
                c = k(d, j)
                wy, wym = c + k(d, j + 1), c + k(d, j - 1)
                wzt, wzm = c + self.inner_up(c), c + self.inner_down(c)
                wz = jnp.where(self.lane == self.right, 0.0, wzt)
                wxm = wx.get(d - 1)
                s = ((wx[d] if wxm is None else wx[d] + wxm) + (wy + wym)) + (wzt + wzm)
                e = self.change(u, d, j, wx[d], wxm, wy, wym, wz, s, inflow if d == 0 else None)
                finish(start + d, j, wx[d], wy, wz, s, e, flux[d] - flux[d - 1])

    def clear_rows(self, E, Wy, first, count):
        row = jnp.zeros((count, 1, self.cells[2]), jnp.float32)

        def clear(ref, r):
            at = r // self.T
            ref[first : first + count, r % self.T, at : at + 1, :] = row

        @pl.when(self.no_low)
        def _():
            clear(E, self.rows - 1)
            clear(Wy, self.rows - 1)

        @pl.when(self.no_high)
        def _():
            clear(E, self.cells[1])
            clear(Wy, self.cells[1] - 1)

    def sweep(self, loads, start, count, finish, boxes):
        le, lz, lwx, lwy, lwz, ls = loads
        e, z, wxs, wys = (self.reader(load, start) for load in (le, lz, lwx, lwy))
        for j in range(self.T):
            wanted = {d + o for d in range(count) if boxes[d] for o in (-1, 0, 1)}
            sums = {d: z(d, j) + (z(d, j + 1) + z(d, j - 1)) for d in sorted(wanted)}
            for d in range(count):
                i = start + d
                weights = (wxs(d, j), wxs(d - 1, j), wys(d, j), wys(d, j - 1), lwz(i, j), ls(i, j))
                em = self.change(e, d, j, *weights)
                zm = self.change(z, d, j, *weights)
                q = None
                if boxes[d]:
                    xs = sums[d - 1] + sums[d] + sums[d + 1]
                    xs = xs + (self.inner_up(xs) + self.inner_down(xs))
                    q = xs * (1.0 / 27.0) - z(d, j)
                finish(i, j, e(d, j), em, z(d, j), zm, q)

    def results(self, OI, OS, o, j, total, z):
        OI[o, pl.ds(j, 8, stride=self.T), :] = total * (-1.0 / (step_size * step_size))
        OS[o, pl.ds(j, 8, stride=self.T), :] = z * (1.0 / step_size)

    def leave(self, first, OI, OS, ind, sens, sems, p):
        pair = pl.ds(first, 2)
        return [
            pltpu.make_async_copy(source.at[pair, pl.ds(0, self.cells[1]), :], target.at[pair], sems.at[k, p])
            for k, (source, target) in enumerate(((OI, ind), (OS, sens)))
        ]


KEPT = (("EA", 5, 4), ("ZA", 5, 4), ("EB", 6, 2), ("ZB", 6, 2), ("Wx", 4, 4), ("Wy", 5, 3), ("Wz", 5, 3),
        ("S", 5, 3), ("M0", 6, 2), ("Q3", 6, 2), ("AC", 7, 1))
KEPT_PLANES = sum(count for _, _, count in KEPT)


def turns(count, body, together=9):
    full = count // together

    def turn(p, _):
        for d in range(together):
            body(together * p + d)
        return 0

    lax.fori_loop(0, full, turn, 0)
    for p in range(full * together, count):
        body(p)


def tiler(ref):
    return lambda i, j: ref[i, j]


def inner_kernel(initial, material, goal, table, first, second, near_a, near_b, OI, OS, edge, kept,
                 U, K, G, Wx, Wy, Wz, S, EA, EB, ZA, ZB, M0, Q3, AC):
    cells_x, cells_y, cells_z = initial.shape
    H = HALO
    steps = Steps(cells_x, cells_y, cells_z)
    odd = steps.odd
    planes = cells_x + 2 * H
    chosen = from_first(cells_z)
    near = Halves(near_a, near_b)
    side, step = odd * (planes - 1), 1 - 2 * odd

    def place(natural):
        return side + step * natural

    def own(p):
        ones = goal_tiles(p, cells_x, first, second, chosen)
        for d in range(2):
            i = 2 * p + d
            f = place(H + i)
            U[f, 0:cells_y, :] = initial[i]
            K[f, 0:cells_y, :] = gather_rows(table[0:1], material[i])
            G[f + 1 - odd, 0:cells_y, :] = goal[i].astype(jnp.float32)
            U[f, cells_y:, :], K[f, cells_y:, :] = halo_tiles(i, cells_x, first, second, chosen)
            G[f + 1 - odd, cells_y:, :] = ones[d]

    turns(cells_x // 2, own)
    for i in range(H):
        f = (1 - odd) * (H + cells_x + i) + odd * (planes - 1 - i)
        U[f] = near[i]
        K[f] = near[H + i]
        G[f + 1 - odd] = near[2 * H + i]
    for d in range(2):
        for j in range(steps.T):
            here = pl.ds(j, 8, stride=steps.T)
            edge[d, j] = U[H + d, here, :]
            edge[2 + d, j] = K[H + d, here, :]
            edge[4 + d, j] = G[H + d + 1 - odd, here, :]

    def first_goal(i, j):
        return G[i + 1, pl.ds(j, 8, stride=steps.T), :]

    def begin(i, j, wx, wy, wz, s, e, z):
        Wx[i, j], Wy[i, j], Wz[i, j], S[i, j], EA[i, j], ZA[i, j] = wx, wy, wz, s, e, z

    def prelude(p):
        steps.prelude((steps.rower(K), steps.rower(U), first_goal), H + 1 + 2 * p, 2, begin)

    turns((planes - 2 - H) // 2, prelude)
    for j in range(steps.T):
        k = steps.rower(K)
        Wx[H, j] = k(H, j) + k(H + 1, j)
    steps.clear_rows(EA, Wy, H + 1, planes - 2 - H)

    def store_a(i, j, e, em, z, zm, q):
        EB[i, j] = e + em
        ZB[i, j] = z + zm
        if q is not None:
            M0[i - H, j] = em
            Q3[i - H, j] = q

    def store_b(i, j, e, em, z, zm, q):
        EA[i, j] = e + em
        ZA[i, j] = z + zm
        if q is not None:
            AC[i - H, j] = em * q

    def store_c(i, j, e, em, z, zm, q):
        o = i - H
        total = AC[o, j] + em * Q3[o, j] + M0[o, j] * q
        steps.results(OI, OS, place(i) - H, j, total, z + zm)

    weights = tuple(tiler(ref) for ref in (Wx, Wy, Wz, S))

    def sweep(E, Z, start, finish, boxes):
        steps.sweep((tiler(E), tiler(Z)) + weights, start, len(boxes), finish, boxes)

    def many(E, Z, start, pairs, finish):
        turns(pairs, lambda p: sweep(E, Z, start + 2 * p, finish, (True, True)))

    top = H + cells_x
    many(EA, ZA, H + 2, (cells_x - 2) // 2, store_a)
    sweep(EA, ZA, top, store_a, (False, False))
    many(EB, ZB, H + 3, (cells_x - 4) // 2, store_b)
    sweep(EB, ZB, top - 1, store_b, (True, False))

    turns((cells_x - 4) // 2, lambda p: sweep(EA, ZA, H + 4 + 2 * p, store_c, (True, True)))
    refs = dict(EA=EA, ZA=ZA, EB=EB, ZB=ZB, Wx=Wx, Wy=Wy, Wz=Wz, S=S, M0=M0, Q3=Q3, AC=AC)
    at = 0
    for name, start, count in KEPT:
        shift = H if name in ("M0", "Q3", "AC") else 0
        for d in range(count):
            kept[at + d] = refs[name][start - shift + d]
        at += count


def outer_kernel(far, far_corner, edge, kept, inner_ind, inner_sens, ind, sens,
                 U, K, G, FU, FG, Wx, Wy, Wz, S, EA, EB, EC, ZA, ZB, ZC, M0, Q3, AC, OI, OS, sems):
    cells_x, cells_y, cells_z = ind.shape
    H = HALO
    steps = Steps(cells_x, cells_y, cells_z)
    odd = steps.odd
    done = pl.ds((1 - odd) * H, cells_x - H)
    moves = [
        pltpu.make_async_copy(source.at[done, pl.ds(0, cells_y), :], target.at[done], sems.at[k, 2])
        for k, (source, target) in enumerate(((inner_ind, ind), (inner_sens, sens)))
    ]
    for move in moves:
        move.start()
    FU[0:cells_y, :] = far[3]
    FU[cells_y:, :] = jnp.zeros((8, cells_z), jnp.float32)
    FG[0:cells_y, :] = far[7]
    for f in range(1, H):
        U[f, 0:cells_y, :] = far[f - 1]
        K[f, 0:cells_y, :] = far[3 + f]
        G[f + 1, 0:cells_y, :] = far[7 + f]
    tiles = [far_corner[i] for i in range(7)]
    turned = {i: pltpu.roll(tiles[i], HALO, 0) for i in (0, 2, 5)}
    for ref, values in (
        (U, (turned[0], tiles[5], tiles[0])),
        (K, (turned[5], tiles[3], tiles[1])),
        (G, (tiles[6], tiles[4], tiles[2])),
    ):
        for f in range(1, H):
            ref[f + 1 if ref is G else f, cells_y:, :] = values[f - 1]
    FG[cells_y:, :] = turned[2]

    places, at = {}, 0
    for name, first, count in KEPT:
        places[name] = (first, at)
        at += count

    def mixed(ref, name, own_first, own_last):
        first, offset = places[name]

        def load(i, j):
            if own_first <= i <= own_last:
                return ref[i, j]
            return kept[offset + i - first, j]

        return load

    sub_shape = (8, cells_z)
    is_odd = jnp.broadcast_to(odd == 1, sub_shape)

    def beside(ref, at):
        rows = steps.rower(ref)
        return lambda i, j: rows(i, j) if i < H else edge[at + i - H, j]

    def first_goal(i, j):
        if i < H - 1:
            return G[i + 1, pl.ds(j, 8, stride=steps.T), :]
        other = edge[4, j] if i == H else G[H, pl.ds(j, 8, stride=steps.T), :]
        return jnp.where(is_odd, edge[5 + i - H, j], other)

    sub = lax.broadcasted_iota(jnp.int32, (8, cells_z), 0)
    T = steps.T
    no_far, no_low, no_high = (
        jnp.broadcast_to(flag, sub.shape) for flag in (steps.no_far, steps.no_low, steps.no_high))

    def cleared(value, j, r, flag):
        if r % T != j:
            return value
        return jnp.where((sub == r // T) & flag, 0.0, value)

    def begin(i, j, wx, wy, wz, s, e, z):
        e = cleared(cleared(e, j, steps.rows - 1, no_low), j, cells_y, no_high)
        wy = cleared(cleared(wy, j, steps.rows - 1, no_low), j, cells_y - 1, no_high)
        if i == H - 1:
            wx, e, z = (jnp.where(no_far, 0.0, value) for value in (wx, e, z))
        Wx[i, j], Wy[i, j], Wz[i, j], S[i, j], EA[i, j], ZA[i, j] = wx, wy, wz, s, e, z

    def fluxes(ref):
        return lambda j: ref[pl.ds(j, 8, stride=steps.T), :]

    fields = (beside(K, 2), beside(U, 0), first_goal)
    steps.prelude(fields, 3, 2, begin)
    steps.prelude(fields, 1, 2, begin, (fluxes(FU), fluxes(FG)))
    weights = (mixed(Wx, "Wx", 1, H), mixed(Wy, "Wy", 1, H), mixed(Wz, "Wz", 1, H), mixed(S, "S", 1, H))

    def store_a(i, j, e, em, z, zm, q):
        EB[i, j] = e + em
        ZB[i, j] = z + zm
        if q is not None:
            M0[i, j] = em
            Q3[i, j] = q

    def store_b(i, j, e, em, z, zm, q):
        EC[i, j] = e + em
        ZC[i, j] = z + zm
        if q is not None:
            AC[i, j] = em * q

    top = H + cells_x
    m0, q3, ac = mixed(M0, "M0", H, H + 1), mixed(Q3, "Q3", H, H + 1), mixed(AC, "AC", H, H + 2)

    def store_c(i, j, e, em, z, zm, q):
        total = ac(i, j) + em * q3(i, j) + m0(i, j) * q
        steps.results(OI, OS, (1 - odd) * (i - H) + odd * (top - 1 - i), j, total, z + zm)

    first = (mixed(EA, "EA", 1, H), mixed(ZA, "ZA", 1, H)) + weights
    second = (mixed(EB, "EB", 2, H + 1), mixed(ZB, "ZB", 2, H + 1)) + weights
    third = (mixed(EC, "EA", 3, H + 2), mixed(ZC, "ZA", 3, H + 2)) + weights
    steps.sweep(first, 4, 2, store_a, (True, True))
    steps.sweep(first, 2, 2, store_a, (False, False))
    steps.sweep(second, 5, 2, store_b, (True, True))
    steps.sweep(second, 3, 2, store_b, (False, True))
    for p in (1, 0):
        f = H + 2 * p
        steps.sweep(third, f, 2, store_c, (True, True))
        moves += steps.leave((1 - odd) * (f - H) + odd * (top - 2 - f), OI, OS, ind, sens, sems, p)
        for move in moves[-2:]:
            move.start()
    for move in moves:
        move.wait()


def whole(memory=None):
    return pl.BlockSpec(memory_space=memory or pltpu.VMEM)


def swap(pairs):
    return [(a, b) for a, b in pairs] + [(b, a) for a, b in pairs]


def per_device(initial, material, goal_faces, conductivity):
    cells_x, cells_y, cells_z = initial.shape
    f32 = jnp.float32
    params = pltpu.CompilerParams(vmem_limit_bytes=LIMIT)
    small = pltpu.CompilerParams(vmem_limit_bytes=LIMIT // 4)
    shape = jax.ShapeDtypeStruct
    hbm, vmem = whole(pltpu.HBM), whole()
    rows = cells_y + 8
    planes = cells_x + 2 * HALO
    send = shape((cells_x + cells_x // 2, 8, cells_z), f32)
    block = shape(initial.shape, f32)
    count = lax.axis_size("gx")
    far_pairs = [(i, i + 1) for i in range(1, count - 1, 2)]
    near_pairs = [(i, i + 1) for i in range(0, count, 2)]

    here = [pltpu.with_memory_space_constraint(x, pltpu.HBM) for x in (initial, material, goal_faces, conductivity)]
    ends = (2, cells_x, 8, cells_z)
    first, second, table = pl.pallas_call(
        edge_kernel,
        out_shape=(send, send, shape((8, cells_z), f32)),
        in_specs=[hbm] * 4,
        out_specs=(vmem, vmem, vmem),
        scratch_shapes=[
            pltpu.VMEM(ends, f32),
            pltpu.VMEM(ends, jnp.int32),
            pltpu.VMEM(ends, jnp.int32),
            pltpu.SMEM(conductivity.shape, f32),
            pltpu.SemaphoreType.DMA((7,)),
        ],
        compiler_params=small,
        name="edges",
    )(*here)
    first_sent = first
    rows_y = lax.axis_size("gy")
    first, second = (
        lax.ppermute(value, "gy", swap([(i, i + 1) for i in range(start, rows_y - 1, 2)]))
        for start, value in ((1, first), (0, second))
    )
    far = pl.pallas_call(
        far_kernel,
        out_shape=shape((3 * HALO - 1, cells_y, cells_z), f32),
        in_specs=[vmem] * 4 + [whole(pl.ANY)],
        out_specs=vmem,
        compiler_params=small,
        name="far",
    )(initial, material, goal_faces, table, first_sent)
    far_sent = far
    far = lax.ppermute(far, "gx", swap(far_pairs))
    part = shape((3 * HALO // 2, rows, cells_z), f32)
    near_a, near_b, far_corner = pl.pallas_call(
        near_kernel,
        out_shape=(part, part, shape((7, 8, cells_z), f32)),
        in_specs=[vmem] * 6 + [whole(pl.ANY)],
        out_specs=(vmem,) * 3,
        compiler_params=small,
        cost_estimate=pl.CostEstimate(flops=10**9, bytes_accessed=1000, transcendentals=0),
        name="near",
    )(initial, material, goal_faces, table, first, second, far_sent)
    near_a = lax.ppermute(near_a, "gx", swap(near_pairs))
    near_b = lax.ppermute(near_b, "gx", swap(near_pairs))
    far_corner = lax.ppermute(far_corner, "gx", swap(far_pairs))

    def tiles(count):
        return pltpu.VMEM((count, rows // 8, 8, cells_z), f32)

    def natural(count):
        return pltpu.VMEM((count, rows, cells_z), f32)

    wide_block = shape((cells_x, rows, cells_z), f32)
    ind, sens, edge, kept = pl.pallas_call(
        inner_kernel,
        out_shape=(wide_block, wide_block, shape((6, rows // 8, 8, cells_z), f32), shape((KEPT_PLANES, rows // 8, 8, cells_z), f32)),
        in_specs=[vmem] * 8,
        out_specs=(vmem,) * 4,
        scratch_shapes=[natural(planes), natural(planes), natural(planes + 1)]
        + [tiles(planes)] * 8 + [tiles(cells_x)] * 3,
        compiler_params=params,
        cost_estimate=pl.CostEstimate(flops=1000, bytes_accessed=1000, transcendentals=0),
        name="inner",
    )(initial, material, goal_faces, table, first, second, near_a, near_b)
    return pl.pallas_call(
        outer_kernel,
        out_shape=(block, block),
        in_specs=[vmem] * 6,
        out_specs=(hbm, hbm),
        scratch_shapes=[natural(HALO), natural(HALO), natural(HALO + 1)]
        + [pltpu.VMEM((rows, cells_z), f32)] * 2 + [tiles(2 * HALO)] * 13 + [natural(cells_x)] * 2 + [pltpu.SemaphoreType.DMA((2, 3))],
        compiler_params=small,
        name="outer",
    )(far, far_corner, edge, kept, ind, sens)


def solution(mesh):
    placed = (P("gx", "gy", None), P("gx", "gy", None), P("gx", "gy", None), P())
    return jax.shard_map(
        per_device,
        mesh=mesh,
        in_specs=placed,
        out_specs=(P("gx", "gy", None), P("gx", "gy", None)),
        check_vma=False,
    )
```

```python
import functools

import jax
import jax.numpy as jnp
from jax import lax
from jax.experimental import pallas as pl
from jax.experimental.pallas import tpu as pltpu
from jax.sharding import PartitionSpec as P

step_size = 0.075
HALO = 4
LIMIT = 40 * 1024 * 1024


def lanes_of(shape):
    return lax.broadcasted_iota(jnp.int32, shape, len(shape) - 1)


def half_weights(cond, lanes):
    lane = lanes_of((1, lanes))
    table = jnp.zeros((1, lanes), jnp.float32)
    for which in range(cond.shape[0]):
        table = jnp.where(lane == which, cond[which] * (0.5 * step_size), table)
    return table


def gather_rows(table, index):
    return jnp.take_along_axis(jnp.broadcast_to(table, index.shape), index, axis=1, mode="promise_in_bounds")


def edge_kernel(initial, material, goal, cond, first, second, shared, u, ids, flags, values, sems):
    cells_x, cells_y, cells_z = initial.shape
    moves = [pltpu.make_async_copy(cond, values, sems.at[6])]
    for end, row in enumerate((0, cells_y - 8)):
        for k, (source, target) in enumerate(((material, ids), (initial, u), (goal, flags))):
            moves.append(pltpu.make_async_copy(
                source.at[:, pl.ds(row, 8), :], target.at[end], sems.at[3 * end + k]))
    for move in moves:
        move.start()
    low_half = lax.broadcasted_iota(jnp.int32, (8, cells_z), 0) < HALO
    moves[0].wait()
    table = half_weights(values, cells_z)
    shared[...] = jnp.broadcast_to(table, shared.shape)
    for move in moves[1:]:
        move.wait()
    even = jnp.broadcast_to(lax.axis_index("gy") % 2 == 0, low_half.shape)

    def put(i, up, down):
        first[i] = jnp.where(even, up, down)
        second[i] = jnp.where(even, down, up)

    for i in range(cells_x):
        k_low = pltpu.roll(gather_rows(table, ids[0, i]), HALO, 0)
        k_high = pltpu.roll(gather_rows(table, ids[1, i]), HALO, 0)
        put(i, jnp.where(low_half, k_high, u[1, i]), jnp.where(low_half, u[0, i], k_low))
    for p in range(cells_x // 2):
        high_one, high_two = flags[1, 2 * p], pltpu.roll(flags[1, 2 * p + 1], HALO, 0)
        low_one, low_two = flags[0, 2 * p], pltpu.roll(flags[0, 2 * p + 1], HALO, 0)
        put(cells_x + p, jnp.where(low_half, high_two, high_one).astype(jnp.float32),
            jnp.where(low_half, low_one, low_two).astype(jnp.float32))


def face_planes(send, start, u, material, goal, table):
    cells_y = u.shape[1]
    for i in range(HALO):
        send[i, 0:cells_y, :] = u[start + i]
        send[HALO + i, 0:cells_y, :] = gather_rows(table, material[start + i])
        send[2 * HALO + i, 0:cells_y, :] = goal[start + i].astype(jnp.float32)


def far_order(odd, cells_x):
    last = cells_x - HALO
    return (
        lambda f: odd * (last + f) + (1 - odd) * (HALO - 1 - f),
        lambda f: odd * (last + f) + (1 - odd) * max(HALO - 2 - f, 0),
    )


def far_kernel(u, material, goal, table, sent, far):
    plane, cell = far_order(lax.axis_index("gx") % 2, u.shape[0])
    kappa = [gather_rows(table[0:1], material[plane(f)]) for f in range(HALO)]
    face = kappa[0] + kappa[1]
    far[3] = face * (u[plane(0)] - u[plane(1)])
    far[7] = face * goal[cell(0)].astype(jnp.float32)
    for f in range(1, HALO):
        far[f - 1] = u[plane(f)]
        far[3 + f] = kappa[f]
        far[7 + f] = goal[cell(f)].astype(jnp.float32)


def from_first(cells_z):
    low_half = lax.broadcasted_iota(jnp.int32, (8, cells_z), 0) < HALO
    even = jnp.broadcast_to(lax.axis_index("gy") % 2 == 0, low_half.shape)
    return low_half == even


def halo_tiles(plane, cells_x, first, second, chosen):
    one, two = first[plane], second[plane]
    return jnp.where(chosen, one, two), pltpu.roll(jnp.where(chosen, two, one), HALO, 0)


def goal_tiles(pair, cells_x, first, second, chosen):
    return halo_tiles(cells_x + pair, cells_x, first, second, chosen)


def near_kernel(u, material, goal, table, first, second, far, near_a, near_b, far_corner):
    cells_x, cells_y, cells_z = u.shape
    chosen = from_first(cells_z)
    odd = lax.axis_index("gx") % 2
    last = cells_x - HALO
    near = Halves(near_a, near_b)
    face_planes(near, (1 - odd) * last, u, material, goal, table[0:1])

    def all_tiles(start):
        us, ks, gs = [], [], []
        for i in range(HALO):
            hu, hk = halo_tiles(start + i, cells_x, first, second, chosen)
            us.append(hu)
            ks.append(hk)
        for i in range(0, HALO, 2):
            gs += goal_tiles(start // 2 + i // 2, cells_x, first, second, chosen)
        return us, ks, gs

    for field, tiles in enumerate(all_tiles((1 - odd) * last)):
        for i in range(HALO):
            near[field * HALO + i, pl.ds(cells_y, 8), :] = tiles[i]

    us, ks, gs = all_tiles(odd * last)
    is_odd = jnp.broadcast_to(odd == 1, chosen.shape)
    us, ks = [[jnp.where(is_odd, t[f], t[HALO - 1 - f]) for f in range(HALO)] for t in (us, ks)]
    gs = [jnp.where(is_odd, gs[f], gs[max(HALO - 2 - f, 0)]) for f in range(HALO)]
    flux = gs[0] * (ks[0] + ks[1])
    sub = lax.broadcasted_iota(jnp.int32, chosen.shape, 0)
    two, four = (sub == 3) | (sub == 4), (sub >= 2) & (sub <= 5)
    far_corner[0] = jnp.where(two, pltpu.roll(us[1], HALO, 0), us[3])
    far_corner[1] = ks[3]
    far_corner[2] = jnp.where(two, pltpu.roll(flux, HALO, 0), gs[3])
    far_corner[3] = ks[2]
    far_corner[4] = gs[2]
    far_corner[5] = jnp.where(four, pltpu.roll(ks[1], HALO, 0), us[2])
    far_corner[6] = gs[1]


class Halves:
    def __init__(self, *parts):
        self.parts, self.size = parts, parts[0].shape[0]

    def at_plane(self, index):
        plane, *rest = index if isinstance(index, tuple) else (index,)
        return self.parts[plane // self.size], (plane % self.size, *rest)

    def __getitem__(self, index):
        ref, inside = self.at_plane(index)
        return ref[inside]

    def __setitem__(self, index, value):
        ref, inside = self.at_plane(index)
        ref[inside] = value


class Steps:
    def __init__(self, cells_x, cells_y, cells_z):
        self.rows = cells_y + 8
        self.cells = (cells_x, cells_y, cells_z)
        self.T = self.rows // 8
        self.right = cells_z - 1
        self.lane = lanes_of((8, cells_z))
        gx, gy = lax.axis_index("gx"), lax.axis_index("gy")
        self.odd = gx % 2
        self.sign = (1 - 2 * self.odd).astype(jnp.float32)
        self.no_far = (gx == 0) | (gx == lax.axis_size("gx") - 1)
        self.no_low, self.no_high = gy == 0, gy == lax.axis_size("gy") - 1

    def rower(self, ref):
        return lambda i, j: ref[i, pl.ds(j, 8, stride=self.T), :]

    def reader(self, load, start):
        seen = {}
        T = self.T

        def read(d, j):
            if (d, j) not in seen:
                if j == -1:
                    seen[d, j] = pltpu.roll(load(start + d, T - 1), 1, 0)
                elif j == T:
                    seen[d, j] = pltpu.roll(load(start + d, 0), 7, 0)
                else:
                    seen[d, j] = load(start + d, j)
            return seen[d, j]

        return read

    def up_lane(self, value):
        return pltpu.roll(value, self.right, 1)

    def down_lane(self, value):
        return pltpu.roll(value, 1, 1)

    def inner_up(self, value):
        return jnp.where(self.lane == self.right, 0.0, self.up_lane(value))

    def inner_down(self, value):
        return jnp.where(self.lane == 0, 0.0, self.down_lane(value))

    def change(self, v, d, j, wx, wxm, wy, wym, wz, s, inflow=None):
        c = v(d, j)
        below = wxm * v(d - 1, j) if inflow is None else inflow
        along = (wx * v(d + 1, j) + below) + (wy * v(d, j + 1) + wym * v(d, j - 1))
        return along + (wz * self.up_lane(c) + self.down_lane(wz * c)) - s * c

    def prelude(self, loads, start, count, finish, outermost=None):
        k, u, g = (self.reader(load, start) for load in loads)
        for j in range(self.T):
            low = -1 if outermost is None else 0
            wx = {d: k(d, j) + k(d + 1, j) for d in range(low, count)}
            flux = {d: (self.sign * g(d, j)) * wx[d] for d in range(low, count)}
            inflow = None
            if outermost is not None:
                inflow, flux[-1] = outermost[0](j), self.sign * outermost[1](j)
            for d in range(count):
                c = k(d, j)
                wy, wym = c + k(d, j + 1), c + k(d, j - 1)
                wzt, wzm = c + self.inner_up(c), c + self.inner_down(c)
                wz = jnp.where(self.lane == self.right, 0.0, wzt)
                wxm = wx.get(d - 1)
                s = ((wx[d] if wxm is None else wx[d] + wxm) + (wy + wym)) + (wzt + wzm)
                e = self.change(u, d, j, wx[d], wxm, wy, wym, wz, s, inflow if d == 0 else None)
                finish(start + d, j, wx[d], wy, wz, s, e, flux[d] - flux[d - 1])

    def clear_rows(self, E, Wy, first, count):
        row = jnp.zeros((count, 1, self.cells[2]), jnp.float32)

        def clear(ref, r):
            at = r // self.T
            ref[first : first + count, r % self.T, at : at + 1, :] = row

        @pl.when(self.no_low)
        def _():
            clear(E, self.rows - 1)
            clear(Wy, self.rows - 1)

        @pl.when(self.no_high)
        def _():
            clear(E, self.cells[1])
            clear(Wy, self.cells[1] - 1)

    def sweep(self, loads, start, count, finish, boxes):
        le, lz, lwx, lwy, lwz, ls = loads
        e, z, wxs, wys = (self.reader(load, start) for load in (le, lz, lwx, lwy))
        for j in range(self.T):
            wanted = {d + o for d in range(count) if boxes[d] for o in (-1, 0, 1)}
            sums = {d: z(d, j) + (z(d, j + 1) + z(d, j - 1)) for d in sorted(wanted)}
            for d in range(count):
                i = start + d
                weights = (wxs(d, j), wxs(d - 1, j), wys(d, j), wys(d, j - 1), lwz(i, j), ls(i, j))
                em = self.change(e, d, j, *weights)
                zm = self.change(z, d, j, *weights)
                q = None
                if boxes[d]:
                    xs = sums[d - 1] + sums[d] + sums[d + 1]
                    xs = xs + (self.inner_up(xs) + self.inner_down(xs))
                    q = xs * (1.0 / 27.0) - z(d, j)
                finish(i, j, e(d, j), em, z(d, j), zm, q)

    def results(self, OI, OS, o, j, total, z):
        OI[o, pl.ds(j, 8, stride=self.T), :] = total * (-1.0 / (step_size * step_size))
        OS[o, pl.ds(j, 8, stride=self.T), :] = z * (1.0 / step_size)

    def leave(self, first, OI, OS, ind, sens, sems, p):
        pair = pl.ds(first, 2)
        return [
            pltpu.make_async_copy(source.at[pair, pl.ds(0, self.cells[1]), :], target.at[pair], sems.at[k, p])
            for k, (source, target) in enumerate(((OI, ind), (OS, sens)))
        ]


KEPT = (("EA", 5, 4), ("ZA", 5, 4), ("EB", 6, 2), ("ZB", 6, 2), ("Wx", 4, 4), ("Wy", 5, 3), ("Wz", 5, 3),
        ("S", 5, 3), ("M0", 6, 2), ("Q3", 6, 2), ("AC", 7, 1))
KEPT_PLANES = sum(count for _, _, count in KEPT)


def turns(count, body, together=9):
    full = count // together

    def turn(p, _):
        for d in range(together):
            body(together * p + d)
        return 0

    lax.fori_loop(0, full, turn, 0)
    for p in range(full * together, count):
        body(p)


def tiler(ref):
    return lambda i, j: ref[i, j]


def inner_kernel(initial, material, goal, table, first, second, near_a, near_b, OI, OS, edge, kept,
                 U, K, G, Wx, Wy, Wz, S, EA, EB, ZA, ZB, M0, Q3, AC):
    cells_x, cells_y, cells_z = initial.shape
    H = HALO
    steps = Steps(cells_x, cells_y, cells_z)
    odd = steps.odd
    planes = cells_x + 2 * H
    chosen = from_first(cells_z)
    near = Halves(near_a, near_b)
    side, step = odd * (planes - 1), 1 - 2 * odd

    def place(natural):
        return side + step * natural

    def own(p):
        ones = goal_tiles(p, cells_x, first, second, chosen)
        for d in range(2):
            i = 2 * p + d
            f = place(H + i)
            U[f, 0:cells_y, :] = initial[i]
            K[f, 0:cells_y, :] = gather_rows(table[0:1], material[i])
            G[f + 1 - odd, 0:cells_y, :] = goal[i].astype(jnp.float32)
            U[f, cells_y:, :], K[f, cells_y:, :] = halo_tiles(i, cells_x, first, second, chosen)
            G[f + 1 - odd, cells_y:, :] = ones[d]

    turns(cells_x // 2, own)
    for i in range(H):
        f = (1 - odd) * (H + cells_x + i) + odd * (planes - 1 - i)
        U[f] = near[i]
        K[f] = near[H + i]
        G[f + 1 - odd] = near[2 * H + i]
    for d in range(2):
        for j in range(steps.T):
            here = pl.ds(j, 8, stride=steps.T)
            edge[d, j] = U[H + d, here, :]
            edge[2 + d, j] = K[H + d, here, :]
            edge[4 + d, j] = G[H + d + 1 - odd, here, :]

    def first_goal(i, j):
        return G[i + 1, pl.ds(j, 8, stride=steps.T), :]

    def begin(i, j, wx, wy, wz, s, e, z):
        Wx[i, j], Wy[i, j], Wz[i, j], S[i, j], EA[i, j], ZA[i, j] = wx, wy, wz, s, e, z

    def prelude(p):
        steps.prelude((steps.rower(K), steps.rower(U), first_goal), H + 1 + 2 * p, 2, begin)

    turns((planes - 2 - H) // 2, prelude)
    for j in range(steps.T):
        k = steps.rower(K)
        Wx[H, j] = k(H, j) + k(H + 1, j)
    steps.clear_rows(EA, Wy, H + 1, planes - 2 - H)

    def store_a(i, j, e, em, z, zm, q):
        EB[i, j] = e + em
        ZB[i, j] = z + zm
        if q is not None:
            M0[i - H, j] = em
            Q3[i - H, j] = q

    def store_b(i, j, e, em, z, zm, q):
        EA[i, j] = e + em
        ZA[i, j] = z + zm
        if q is not None:
            AC[i - H, j] = em * q

    def store_c(i, j, e, em, z, zm, q):
        o = i - H
        total = AC[o, j] + em * Q3[o, j] + M0[o, j] * q
        steps.results(OI, OS, place(i) - H, j, total, z + zm)

    weights = tuple(tiler(ref) for ref in (Wx, Wy, Wz, S))

    def sweep(E, Z, start, finish, boxes):
        steps.sweep((tiler(E), tiler(Z)) + weights, start, len(boxes), finish, boxes)

    def many(E, Z, start, pairs, finish):
        turns(pairs, lambda p: sweep(E, Z, start + 2 * p, finish, (True, True)))

    top = H + cells_x
    many(EA, ZA, H + 2, (cells_x - 2) // 2, store_a)
    sweep(EA, ZA, top, store_a, (False, False))
    many(EB, ZB, H + 3, (cells_x - 4) // 2, store_b)
    sweep(EB, ZB, top - 1, store_b, (True, False))

    turns((cells_x - 4) // 2, lambda p: sweep(EA, ZA, H + 4 + 2 * p, store_c, (True, True)))
    refs = dict(EA=EA, ZA=ZA, EB=EB, ZB=ZB, Wx=Wx, Wy=Wy, Wz=Wz, S=S, M0=M0, Q3=Q3, AC=AC)
    at = 0
    for name, start, count in KEPT:
        shift = H if name in ("M0", "Q3", "AC") else 0
        for d in range(count):
            kept[at + d] = refs[name][start - shift + d]
        at += count


def outer_kernel(far, far_corner, edge, kept, inner_ind, inner_sens, ind, sens,
                 U, K, G, FU, FG, Wx, Wy, Wz, S, EA, EB, EC, ZA, ZB, ZC, M0, Q3, AC, OI, OS, sems):
    cells_x, cells_y, cells_z = ind.shape
    H = HALO
    steps = Steps(cells_x, cells_y, cells_z)
    odd = steps.odd
    done = pl.ds((1 - odd) * H, cells_x - H)
    moves = [
        pltpu.make_async_copy(source.at[done, pl.ds(0, cells_y), :], target.at[done], sems.at[k, 2])
        for k, (source, target) in enumerate(((inner_ind, ind), (inner_sens, sens)))
    ]
    for move in moves:
        move.start()
    FU[0:cells_y, :] = far[3]
    FU[cells_y:, :] = jnp.zeros((8, cells_z), jnp.float32)
    FG[0:cells_y, :] = far[7]
    for f in range(1, H):
        U[f, 0:cells_y, :] = far[f - 1]
        K[f, 0:cells_y, :] = far[3 + f]
        G[f + 1, 0:cells_y, :] = far[7 + f]
    tiles = [far_corner[i] for i in range(7)]
    turned = {i: pltpu.roll(tiles[i], HALO, 0) for i in (0, 2, 5)}
    for ref, values in (
        (U, (turned[0], tiles[5], tiles[0])),
        (K, (turned[5], tiles[3], tiles[1])),
        (G, (tiles[6], tiles[4], tiles[2])),
    ):
        for f in range(1, H):
            ref[f + 1 if ref is G else f, cells_y:, :] = values[f - 1]
    FG[cells_y:, :] = turned[2]

    places, at = {}, 0
    for name, first, count in KEPT:
        places[name] = (first, at)
        at += count

    def mixed(ref, name, own_first, own_last):
        first, offset = places[name]

        def load(i, j):
            if own_first <= i <= own_last:
                return ref[i, j]
            return kept[offset + i - first, j]

        return load

    sub_shape = (8, cells_z)
    is_odd = jnp.broadcast_to(odd == 1, sub_shape)

    def beside(ref, at):
        rows = steps.rower(ref)
        return lambda i, j: rows(i, j) if i < H else edge[at + i - H, j]

    def first_goal(i, j):
        if i < H - 1:
            return G[i + 1, pl.ds(j, 8, stride=steps.T), :]
        other = edge[4, j] if i == H else G[H, pl.ds(j, 8, stride=steps.T), :]
        return jnp.where(is_odd, edge[5 + i - H, j], other)

    sub = lax.broadcasted_iota(jnp.int32, (8, cells_z), 0)
    T = steps.T
    no_far, no_low, no_high = (
        jnp.broadcast_to(flag, sub.shape) for flag in (steps.no_far, steps.no_low, steps.no_high))

    def cleared(value, j, r, flag):
        if r % T != j:
            return value
        return jnp.where((sub == r // T) & flag, 0.0, value)

    def begin(i, j, wx, wy, wz, s, e, z):
        e = cleared(cleared(e, j, steps.rows - 1, no_low), j, cells_y, no_high)
        wy = cleared(cleared(wy, j, steps.rows - 1, no_low), j, cells_y - 1, no_high)
        if i == H - 1:
            wx, e, z = (jnp.where(no_far, 0.0, value) for value in (wx, e, z))
        Wx[i, j], Wy[i, j], Wz[i, j], S[i, j], EA[i, j], ZA[i, j] = wx, wy, wz, s, e, z

    def fluxes(ref):
        return lambda j: ref[pl.ds(j, 8, stride=steps.T), :]

    fields = (beside(K, 2), beside(U, 0), first_goal)
    steps.prelude(fields, 3, 2, begin)
    steps.prelude(fields, 1, 2, begin, (fluxes(FU), fluxes(FG)))
    weights = (mixed(Wx, "Wx", 1, H), mixed(Wy, "Wy", 1, H), mixed(Wz, "Wz", 1, H), mixed(S, "S", 1, H))

    def store_a(i, j, e, em, z, zm, q):
        EB[i, j] = e + em
        ZB[i, j] = z + zm
        if q is not None:
            M0[i, j] = em
            Q3[i, j] = q

    def store_b(i, j, e, em, z, zm, q):
        EC[i, j] = e + em
        ZC[i, j] = z + zm
        if q is not None:
            AC[i, j] = em * q

    top = H + cells_x
    m0, q3, ac = mixed(M0, "M0", H, H + 1), mixed(Q3, "Q3", H, H + 1), mixed(AC, "AC", H, H + 2)

    def store_c(i, j, e, em, z, zm, q):
        total = ac(i, j) + em * q3(i, j) + m0(i, j) * q
        steps.results(OI, OS, (1 - odd) * (i - H) + odd * (top - 1 - i), j, total, z + zm)

    first = (mixed(EA, "EA", 1, H), mixed(ZA, "ZA", 1, H)) + weights
    second = (mixed(EB, "EB", 2, H + 1), mixed(ZB, "ZB", 2, H + 1)) + weights
    third = (mixed(EC, "EA", 3, H + 2), mixed(ZC, "ZA", 3, H + 2)) + weights
    steps.sweep(first, 2, 4, store_a, (False, False, True, True))
    steps.sweep(second, 3, 4, store_b, (False, True, True, True))
    for p in (1, 0):
        f = H + 2 * p
        steps.sweep(third, f, 2, store_c, (True, True))
        moves += steps.leave((1 - odd) * (f - H) + odd * (top - 2 - f), OI, OS, ind, sens, sems, p)
        for move in moves[-2:]:
            move.start()
    for move in moves:
        move.wait()


def whole(memory=None):
    return pl.BlockSpec(memory_space=memory or pltpu.VMEM)


def swap(pairs):
    return [(a, b) for a, b in pairs] + [(b, a) for a, b in pairs]


def per_device(initial, material, goal_faces, conductivity):
    cells_x, cells_y, cells_z = initial.shape
    f32 = jnp.float32
    params = pltpu.CompilerParams(vmem_limit_bytes=LIMIT)
    small = pltpu.CompilerParams(vmem_limit_bytes=LIMIT // 4)
    shape = jax.ShapeDtypeStruct
    hbm, vmem = whole(pltpu.HBM), whole()
    rows = cells_y + 8
    planes = cells_x + 2 * HALO
    send = shape((cells_x + cells_x // 2, 8, cells_z), f32)
    block = shape(initial.shape, f32)
    count = lax.axis_size("gx")
    far_pairs = [(i, i + 1) for i in range(1, count - 1, 2)]
    near_pairs = [(i, i + 1) for i in range(0, count, 2)]

    here = [pltpu.with_memory_space_constraint(x, pltpu.HBM) for x in (initial, material, goal_faces, conductivity)]
    ends = (2, cells_x, 8, cells_z)
    first, second, table = pl.pallas_call(
        edge_kernel,
        out_shape=(send, send, shape((8, cells_z), f32)),
        in_specs=[hbm] * 4,
        out_specs=(vmem, vmem, vmem),
        scratch_shapes=[
            pltpu.VMEM(ends, f32),
            pltpu.VMEM(ends, jnp.int32),
            pltpu.VMEM(ends, jnp.int32),
            pltpu.SMEM(conductivity.shape, f32),
            pltpu.SemaphoreType.DMA((7,)),
        ],
        compiler_params=small,
        name="edges",
    )(*here)
    first_sent = first
    rows_y = lax.axis_size("gy")
    first, second = (
        lax.ppermute(value, "gy", swap([(i, i + 1) for i in range(start, rows_y - 1, 2)]))
        for start, value in enumerate((first, second))
    )
    far = pl.pallas_call(
        far_kernel,
        out_shape=shape((3 * HALO - 1, cells_y, cells_z), f32),
        in_specs=[vmem] * 4 + [whole(pl.ANY)],
        out_specs=vmem,
        compiler_params=small,
        name="far",
    )(initial, material, goal_faces, table, first_sent)
    far_sent = far
    far = lax.ppermute(far, "gx", swap(far_pairs))
    part = shape((3 * HALO // 2, rows, cells_z), f32)
    near_a, near_b, far_corner = pl.pallas_call(
        near_kernel,
        out_shape=(part, part, shape((7, 8, cells_z), f32)),
        in_specs=[vmem] * 6 + [whole(pl.ANY)],
        out_specs=(vmem,) * 3,
        compiler_params=small,
        cost_estimate=pl.CostEstimate(flops=10**9, bytes_accessed=1000, transcendentals=0),
        name="near",
    )(initial, material, goal_faces, table, first, second, far_sent)
    near_a = lax.ppermute(near_a, "gx", swap(near_pairs))
    near_b = lax.ppermute(near_b, "gx", swap(near_pairs))
    far_corner = lax.ppermute(far_corner, "gx", swap(far_pairs))

    def tiles(count):
        return pltpu.VMEM((count, rows // 8, 8, cells_z), f32)

    def natural(count):
        return pltpu.VMEM((count, rows, cells_z), f32)

    wide_block = shape((cells_x, rows, cells_z), f32)
    ind, sens, edge, kept = pl.pallas_call(
        inner_kernel,
        out_shape=(wide_block, wide_block, shape((6, rows // 8, 8, cells_z), f32), shape((KEPT_PLANES, rows // 8, 8, cells_z), f32)),
        in_specs=[vmem] * 8,
        out_specs=(vmem,) * 4,
        scratch_shapes=[natural(planes), natural(planes), natural(planes + 1)]
        + [tiles(planes)] * 8 + [tiles(cells_x)] * 3,
        compiler_params=params,
        cost_estimate=pl.CostEstimate(flops=1000, bytes_accessed=1000, transcendentals=0),
        name="inner",
    )(initial, material, goal_faces, table, first, second, near_a, near_b)
    return pl.pallas_call(
        outer_kernel,
        out_shape=(block, block),
        in_specs=[vmem] * 6,
        out_specs=(hbm, hbm),
        scratch_shapes=[natural(HALO), natural(HALO), natural(HALO + 1)]
        + [pltpu.VMEM((rows, cells_z), f32)] * 2 + [tiles(2 * HALO)] * 13 + [natural(cells_x)] * 2 + [pltpu.SemaphoreType.DMA((2, 3))],
        compiler_params=small,
        name="outer",
    )(far, far_corner, edge, kept, ind, sens)


def solution(mesh):
    placed = (P("gx", "gy", None), P("gx", "gy", None), P("gx", "gy", None), P())
    return jax.shard_map(
        per_device,
        mesh=mesh,
        in_specs=placed,
        out_specs=(P("gx", "gy", None), P("gx", "gy", None)),
        check_vma=False,
    )
```
